32 devices in a mesh: item: 4 (over y, x), seq: 8 (over z, core).
Axes of the slice: x: 2, y: 2, z: 4, core: 2. Of those that a mesh axis runs over, the one named last changes fastest.
Arguments:
- tokens: bfloat16 [8, 1024, 1536], P('item', 'seq'), may hold values from -6 to 6
- timestep: bfloat16 [8, 1536], replicated, may hold values from -6 to 6
- slot_item: int32 [8], replicated, may hold values from 0 to 7, each once
- slot_valid: int32 [8], replicated, may hold values 0 or 1
- cotangent: bfloat16 [8, 1024, 1536], P('item', 'seq'), may hold values from -6 to 6
- in_weight: bfloat16 [1536, 6144], P('seq'), may hold values from -0.15625 to 0.15625
- out_weight: bfloat16 [3072, 1536], P('seq'), may hold values from -0.109375 to 0.109375
- select_weight: bfloat16 [3072, 256], P('seq'), may hold values from -0.109375 to 0.109375
- modulation_weight: bfloat16 [1536, 4608], P('seq'), may hold values from -0.15625 to 0.15625
- delta_weight: bfloat16 [96, 6144], replicated, may hold values from -0.625 to 0.625
- filter_weight: bfloat16 [4, 6144], replicated, may hold values from -3 to 3
- filter_bias: bfloat16 [6144], replicated, may hold values from -3 to 3
- delta_bias: float32 [6144], replicated, may hold values from -4 to -1
- decay_log: float32 [16, 6144], replicated, may hold values from -9 to 1.4
- skip_gain: float32 [6144], replicated, may hold values from -40 to 40
- modulation_bias: bfloat16 [4608], replicated, may hold values from -3 to 3
Outputs:
- output: bfloat16 [8, 1024, 1536], P('item', 'seq')
- grad_tokens: bfloat16 [8, 1024, 1536], P('item', 'seq')
- grad_in_weight: float32 [1536, 6144], P('seq')
- grad_out_weight: float32 [3072, 1536], P('seq')
- grad_select_weight: float32 [3072, 256], P('seq')
- grad_modulation_weight: float32 [1536, 4608], P('seq')
- grad_delta_weight: float32 [96, 6144], replicated
- grad_filter_weight: float32 [4, 6144], replicated
- grad_filter_bias: float32 [6144], replicated
- grad_delta_bias: float32 [6144], replicated
- grad_decay_log: float32 [16, 6144], replicated
- grad_skip_gain: float32 [6144], replicated
- grad_modulation_bias: float32 [4608], replicated
The draws below stay inside these ranges and needn't reach their ends.
Inputs may be any that keep to these rules, and one draw needn't show every extreme that they name: `slot_item`: each item index appears once. `slot_valid`: 1 marks a slot with a real item, 0 a padding slot.
All inputs are finite; a program needn't handle non-finite values.
Results may differ from the reference program's by a relative error of at most 0.015.
Values may be sent and summed in bfloat16 or wider, within the bound.
A program may use at most 320 MiB of HBM per device.

```python
import functools
import math
import jax
import jax.numpy as jnp
from jax import lax

D = 1536
E = 3072
N = 16
R = 96
K = 4
LEN = 1024
SLOTS = 8


def draw_skip_gain(key, part):
    shape = (2 * E,)
    own_key = jax.random.fold_in(key, 7103)
    return jax.random.uniform(own_key, shape, jnp.float32, 0.5, 1.5)


def touch_ends(drawn, rng, smallest, high):
    spot = [jax.random.randint(jax.random.fold_in(rng, axis), (), 0, length) for axis, length in enumerate(drawn.shape)]
    main_axis = drawn.shape.index(max(drawn.shape))
    beside = spot[:main_axis] + [(spot[main_axis] + 1) % drawn.shape[main_axis]] + spot[main_axis + 1:]
    return drawn.at[tuple(spot)].set(smallest).at[tuple(beside)].set(high)


def levels(key, shape, shards, least, top_value):
    gain, own = 1.0, jax.random.fold_in(key, 6)
    for dim, blocks in shards:
        heights = jnp.exp(jax.random.uniform(jax.random.fold_in(own, dim), (blocks,), jnp.float32, least / len(shards), top_value / len(shards)))
        gain = gain * jnp.repeat(heights, shape[dim] // blocks).reshape([-1 if axis == dim else 1 for axis in range(len(shape))])
    return gain


def gaussian(rng, shape, scale, bound, cuts=(), kind=jnp.bfloat16):
    entries = scale * jax.random.normal(rng, shape, jnp.float32)
    if cuts:
        entries = entries * levels(rng, shape, cuts, -0.22, 0.18)
    return jnp.clip(entries, -bound, bound).astype(kind)


def setup_inputs(seed: int = 0) -> dict:
    key_list = jax.random.split(jax.random.key(seed), 17)
    tokens = gaussian(key_list[0], (SLOTS, LEN, D), 1.0, 6.0, ((0, 4), (1, 8)))
    timestep = gaussian(key_list[1], (SLOTS, D), 1.0, 6.0)
    slot_item = jax.random.permutation(key_list[2], SLOTS).astype(jnp.int32)
    slot_valid = touch_ends((jax.random.randint(key_list[3], (SLOTS,), 0, 4) < 3).astype(jnp.int32), jax.random.fold_in(key_list[3], 1), 0, 1)
    cotangent = gaussian(key_list[4], (SLOTS, LEN, D), 1.0, 6.0, ((0, 4), (1, 8)))
    in_weight = gaussian(key_list[5], (D, 2 * E), D ** -0.5, 0.15625, ((0, 8),))
    out_weight = gaussian(key_list[6], (E, D), E ** -0.5, 0.109375, ((0, 8),))
    select_weight = gaussian(key_list[7], (E, 2 * (R + 2 * N)), E ** -0.5, 0.109375, ((0, 8),))
    modulation_weight = gaussian(key_list[8], (D, 3 * D), D ** -0.5, 0.15625, ((0, 8),))
    delta_weight = gaussian(key_list[9], (R, 2 * E), R ** -0.5, 0.625)
    filter_weight = gaussian(key_list[10], (K, 2 * E), K ** -0.5, 3.0)
    filter_bias = gaussian(key_list[11], (2 * E,), 0.5, 3.0)
    delta_bias = jnp.clip(jax.random.uniform(key_list[12], (2 * E,), jnp.float32, -4.0, -1.0), -4.0, -1.0)
    decay_log = jnp.clip(jax.random.uniform(key_list[13], (N, 2 * E), jnp.float32, -9.0, 1.4), -9.0, 1.4)
    skip_gain = draw_skip_gain(jax.random.fold_in(key_list[16], 71), 0)
    modulation_bias = gaussian(key_list[15], (3 * D,), 0.5, 3.0)
    return dict(tokens=tokens, timestep=timestep, slot_item=slot_item, slot_valid=slot_valid, cotangent=cotangent, in_weight=in_weight, out_weight=out_weight, select_weight=select_weight, modulation_weight=modulation_weight, delta_weight=delta_weight, filter_weight=filter_weight, filter_bias=filter_bias, delta_bias=delta_bias, decay_log=decay_log, skip_gain=skip_gain, modulation_bias=modulation_bias)


epsilon = 1e-06
highest = lax.Precision.HIGHEST

@jax.custom_vjp
def low(v):
    return lax.optimization_barrier(v.astype(jnp.bfloat16)).astype(jnp.float32)

@jax.custom_vjp
def low_back(v):
    return v

def low_keep(v):
    return (low(v), None)

def low_pass(kept, grad):
    return (grad,)

def back_keep(v):
    return (v, None)

def back_low(kept, grad):
    return (low(grad),)
low.defvjp(low_keep, low_pass)
low_back.defvjp(back_keep, back_low)

def matmul(left_side, right_side):
    return jnp.dot(left_side, right_side, precision=highest, preferred_element_type=jnp.float32)

def sequence_scan(step_size, activated, state_in, state_out, decay_rate):
    block_size = math.gcd(LEN, 64)

    def token_step(hidden, token_data):
        step_now, input_now, into_now, outof_now = token_data
        hidden = jnp.exp(step_now[None, :] * decay_rate) * hidden + (step_now * input_now)[None, :] * into_now[:, None]
        return (hidden, lax.optimization_barrier(jnp.sum(outof_now[:, None] * hidden, axis=0)))

    @jax.checkpoint
    def block_step(hidden, pieces):
        return lax.scan(token_step, hidden, pieces)
    pieces = tuple((member.reshape(LEN // block_size, block_size, member.shape[-1]) for member in (step_size, activated, state_in, state_out)))
    initial = jnp.zeros(decay_rate.shape, jnp.float32)
    final_state, results = lax.scan(block_step, initial, pieces)
    return results.reshape(LEN, decay_rate.shape[1])

def layer(source, params, embedded, valid_one):
    in_weight, out_weight, select_weight, modulation_weight, delta_weight, filter_weight, filter_bias, delta_bias, decay_log, skip_gain, modulation_bias = params
    condition = low(jax.nn.silu(embedded))
    modulation = matmul(condition[None, :], modulation_weight)[0] + modulation_bias
    shift_mod = modulation[:D]
    scale_mod = modulation[D:2 * D]
    gate_mod = modulation[2 * D:]
    centered = source - lax.optimization_barrier(jnp.mean(source, axis=-1, keepdims=True))
    normed = centered * lax.rsqrt(lax.optimization_barrier(jnp.mean(centered * centered, axis=-1, keepdims=True)) + epsilon)
    mixed_in = low(normed * (1.0 + scale_mod[None, :]) + shift_mod[None, :])
    projected = low_back(matmul(mixed_in, in_weight))
    filter_input = low(projected[:, :E])
    gate_half = projected[:, E:]
    padded = jnp.pad(filter_input, ((K - 1, K - 1), (0, 0)))
    select_width = R + 2 * N
    scanned_sum = jnp.zeros((LEN, E), jnp.float32)
    for direction in range(2):
        columns = slice(direction * E, (direction + 1) * E)
        filtered = jnp.zeros((LEN, E), jnp.float32) + filter_bias[columns][None, :]
        for offset in range(K):
            start_row = 2 * (K - 1) - offset if direction == 1 else offset
            filtered = filtered + filter_weight[offset, columns][None, :] * padded[start_row:start_row + LEN]
        activated = low(jax.nn.silu(filtered))
        selection = low_back(matmul(activated, select_weight[:, direction * select_width:(direction + 1) * select_width]))
        delta_rank = low(selection[:, :R])
        state_in = selection[:, R:R + N]
        state_out = selection[:, R + N:]
        step_size = jax.nn.softplus(low_back(matmul(delta_rank, delta_weight[:, columns])) + delta_bias[columns][None, :])
        decay_rate = -jnp.exp(decay_log[:, columns])
        if direction == 0:
            scanned = sequence_scan(step_size, activated, state_in, state_out, decay_rate)
        else:
            scanned = jnp.flip(sequence_scan(jnp.flip(step_size, 0), jnp.flip(activated, 0), jnp.flip(state_in, 0), jnp.flip(state_out, 0), decay_rate), 0)
        scanned_sum = scanned_sum + scanned + skip_gain[columns][None, :] * activated
    mixed_out = low(scanned_sum * jax.nn.silu(gate_half))
    branch = low_back(matmul(mixed_out, out_weight))
    return source + valid_one * gate_mod[None, :] * branch

def reference(tokens, timestep, slot_item, slot_valid, cotangent, in_weight, out_weight, select_weight, modulation_weight, delta_weight, filter_weight, filter_bias, delta_bias, decay_log, skip_gain, modulation_bias):
    params = tuple((member.astype(jnp.float32) for member in (in_weight, out_weight, select_weight, modulation_weight, delta_weight, filter_weight, filter_bias, delta_bias, decay_log, skip_gain, modulation_bias)))
    chooser = (slot_item[:, None] == jnp.arange(SLOTS, dtype=jnp.int32)[None, :]).astype(jnp.float32)
    embedded = matmul(chooser, timestep.astype(jnp.float32))
    valid_mask = slot_valid.astype(jnp.float32)

    def per_slot(running, inputs):
        source, embedded_row, valid_one, incoming = inputs
        result, pullback = jax.vjp(functools.partial(layer, embedded=embedded_row, valid_one=valid_one), source.astype(jnp.float32), params)
        grad_source, grad_params = pullback(incoming.astype(jnp.float32))
        running = tuple((older + newer for older, newer in zip(running, grad_params)))
        return (running, (result.astype(jnp.bfloat16), grad_source.astype(jnp.bfloat16)))
    zeros_start = tuple((jnp.zeros_like(member) for member in params))
    running, (outputs, grad_tokens) = lax.scan(per_slot, zeros_start, (tokens, embedded, valid_mask, cotangent))
    return (outputs, grad_tokens, running[0], running[1], running[2], running[3], running[4], running[5], running[6], running[7], running[8], running[9], running[10])
```

```python
import functools
import math

import jax
import jax.numpy as jnp
from jax import lax
from jax.experimental import pallas as pl
from jax.experimental.pallas import tpu as pltpu
from jax.sharding import PartitionSpec as P

epsilon = 1e-06
log2e = 1.4426950408889634
ln2 = 0.6931471805599453
chunk = 16
lanes = 128
f32 = jnp.float32
bf16 = jnp.bfloat16


def silu_slope(v):
    s = jax.nn.sigmoid(v)
    return s * (1.0 + v * (1.0 - s))


def dot_rows(a, b):
    return lax.dot_general(a, b, (((0,), (0,)), ((), ())), preferred_element_type=f32)


def dot_cols(a, b):
    return lax.dot_general(a, b, (((1,), (1,)), ((), ())), preferred_element_type=f32)


def fold_sublanes(parts):
    outs = []
    for first in range(0, len(parts), 8):
        cur = parts[first : first + 8]
        row = lax.broadcasted_iota(jnp.int32, cur[0].shape, 0)
        for hop in (4, 2, 1):
            keep = (row // hop) % 2 == 0
            half = len(cur) // 2
            merged = []
            for j in range(half):
                a, b = cur[j], cur[j + half]
                x, y = jnp.where(keep, a, b), jnp.where(keep, b, a)
                if hop == 4:
                    moved = pltpu.roll(y, 4, 0)
                else:
                    moved = jnp.where(keep, pltpu.roll(y, 8 - hop, 0), pltpu.roll(y, hop, 0))
                merged.append(x + moved)
            cur = merged
        outs.append(cur[0])
    return jnp.concatenate(outs, axis=0)


def wide(v, groups):
    return v if groups == 1 else jnp.concatenate([v] * groups, axis=1)


def spread_matrix():
    rows = lax.broadcasted_iota(jnp.int32, (2 * chunk, 2 * lanes), 0) // chunk
    cols = lax.broadcasted_iota(jnp.int32, (2 * chunk, 2 * lanes), 1) // lanes
    return (rows == cols).astype(f32).astype(bf16)


def chunk_sweep(count, body, spread, first, second):
    spread(0, first)
    if count == 1:
        body(0, first)
        return

    def pair(k, carry):
        spread(2 * k + 1, second)
        body(2 * k, first)
        spread(jnp.minimum(2 * k + 2, count - 1), first)
        body(2 * k + 1, second)
        return carry

    lax.fori_loop(0, count // 2, pair, 0)


def states_kernel(count, dt_ref, x_ref, bc_ref, r_ref, y_ref, h_ref, state, even, odd):
    slots, width = dt_ref.shape[1], dt_ref.shape[3]
    groups = width // lanes
    states = r_ref.shape[1]

    @pl.when(pl.program_id(1) == 0)
    def _():
        state[...] = jnp.zeros_like(state)

    def one_direction(reverse):
        mix = spread_matrix()

        def place(i):
            return (count - 1 - i) if reverse else i

        def spread(i, into):
            start = pl.multiple_of(place(i) * chunk, chunk)
            for s in range(slots):
                both = bc_ref[0, s, pl.ds(start, chunk), :]
                span = both.shape[1] // 2
                into[s] = dot_rows(jnp.concatenate([both[:, :span], both[:, span:]], axis=0), mix)

        def body(i, held):
            start = pl.multiple_of(place(i) * chunk, chunk)
            order = range(chunk - 1, -1, -1) if reverse else range(chunk)
            for s in range(slots):
                h = state[s]
                rate = r_ref[0]
                dt = dt_ref[0, s, pl.ds(start, chunk), :]
                u = dt * x_ref[0, s, pl.ds(start, chunk), :].astype(f32)
                kept, sums = [None] * chunk, [None] * chunk
                for t in order:
                    rows = slice(t * states, (t + 1) * states)
                    b = wide(held[s, rows, :lanes], groups)
                    c = wide(held[s, rows, lanes:], groups)
                    h = jnp.exp2(dt[t : t + 1] * rate) * h + u[t : t + 1] * b
                    kept[t] = h.astype(bf16)
                    p = h * c
                    sums[t] = p[:8] + p[8:]
                size = chunk * states
                h_ref[0, s, pl.ds(pl.multiple_of(start * states, size), size), :] = jnp.concatenate(
                    kept, axis=0
                )
                y_ref[0, s, pl.ds(start, chunk), :] = fold_sublanes(sums)
                state[s] = h

        chunk_sweep(count, body, spread, even, odd)

    for d in range(2):

        @pl.when(pl.program_id(0) == d)
        def _():
            one_direction(d == 1)


def adjoint_kernel(
    count,
    dt_ref,
    x_ref,
    bc_ref,
    r_ref,
    g_ref,
    h_ref,
    edge_ref,
    step_ref,
    input_ref,
    coef_ref,
    decay_ref,
    pending,
    even,
    odd,
):
    slots, width = dt_ref.shape[1], dt_ref.shape[3]
    groups = width // lanes
    states = r_ref.shape[1]
    last_block = pl.program_id(1) == pl.num_programs(1) - 1

    @pl.when(pl.program_id(1) == 0)
    def _():
        pending[...] = jnp.zeros_like(pending)
        decay_ref[...] = jnp.zeros_like(decay_ref)

    def one_direction(reverse):
        mix = spread_matrix()
        picks = (
            lax.broadcasted_iota(jnp.int32, (8, 2 * lanes), 0)
            == lax.broadcasted_iota(jnp.int32, (8, 2 * lanes), 1) // lanes
        ).astype(f32).astype(bf16)

        def place(i):
            return i if reverse else (count - 1 - i)

        def spread(i, into):
            start = pl.multiple_of(place(i) * chunk, chunk)
            for s in range(slots):
                both = bc_ref[0, s, pl.ds(start, chunk), :]
                span = both.shape[1] // 2
                into[s] = dot_rows(jnp.concatenate([both[:, :span], both[:, span:]], axis=0), mix)

        def body(i, held):
            here = place(i)
            start = pl.multiple_of(here * chunk, chunk)
            order = range(chunk) if reverse else range(chunk - 1, -1, -1)
            size = chunk * states
            base = pl.multiple_of(start * states, size)
            at_end = here == (count - 1 if reverse else 0)
            outer = jnp.where(last_block, 0.0, 1.0)
            near = pl.multiple_of(
                jnp.clip(start + (chunk if reverse else -1), 0, count * chunk - 1) * states, states
            )
            for s in range(slots):
                pend = pending[s]
                rate = r_ref[0]
                dt = dt_ref[0, s, pl.ds(start, chunk), :]
                x = x_ref[0, s, pl.ds(start, chunk), :].astype(f32)
                g = g_ref[s, pl.ds(start, chunk), :].astype(f32)
                u = dt * x
                before = jnp.where(
                    at_end,
                    edge_ref[0, s].astype(f32) * outer,
                    h_ref[0, s, pl.ds(near, states), :].astype(f32),
                )
                total = decay_ref[0, s]
                rate_sums, into_sums = [None] * chunk, [None] * chunk
                coef = [None] * chunk
                hidden = h_ref[0, s, pl.ds(base, size), :]
                now = hidden[order[0] * states : (order[0] + 1) * states].astype(f32)
                for k, t in enumerate(order):
                    rows = slice(t * states, (t + 1) * states)
                    b = wide(held[s, rows, :lanes], groups)
                    c = wide(held[s, rows, lanes:], groups)
                    if k + 1 < chunk:
                        q = order[k + 1]
                        prev = hidden[q * states : (q + 1) * states].astype(f32)
                    else:
                        prev = before
                    gt = g[t : t + 1]
                    adj = c * gt + pend
                    pend = jnp.exp2(dt[t : t + 1] * rate) * adj
                    through = pend * prev * rate
                    total = total + through * dt[t : t + 1]
                    rate_sums[t] = through[:8] + through[8:]
                    w = adj * b
                    into_sums[t] = w[:8] + w[8:]
                    cb, cc = adj * u[t : t + 1], now * gt
                    sb, sc = cb[:, :lanes], cc[:, :lanes]
                    for j in range(1, groups):
                        sb = sb + cb[:, j * lanes : (j + 1) * lanes]
                        sc = sc + cc[:, j * lanes : (j + 1) * lanes]
                    coef[t] = jnp.concatenate([sb, sc], axis=1).astype(bf16)
                    now = prev
                pending[s] = pend
                decay_ref[0, s] = total
                weighted = fold_sublanes(into_sums)
                step_ref[0, s, pl.ds(start, chunk), :] = (
                    fold_sublanes(rate_sums) * ln2 + weighted * x
                )
                input_ref[0, s, pl.ds(start, chunk), :] = weighted * dt
                coef_ref[0, s, pl.ds(pl.multiple_of(here * 8, 8), 8), :] = dot_cols(
                    picks, jnp.concatenate(coef, axis=0)
                )

        chunk_sweep(count, body, spread, even, odd)

    for d in range(2):

        @pl.when(pl.program_id(0) == d)
        def _():
            one_direction(d == 1)


def block_of(length):
    return math.gcd(length, 128)


def scan_states(dt, x, bc, rate):
    two, slots, length, width = dt.shape
    states = rate.shape[1]
    hidden_size = two * slots * length * states * width
    block = block_of(length)
    blocks = length // block

    def where(d, i):
        return (d, 0, jnp.where(d == 1, blocks - 1 - i, i), 0)

    return pl.pallas_call(
        functools.partial(states_kernel, block // chunk),
        grid=(two, blocks),
        in_specs=[
            pl.BlockSpec((1, slots, block, width), where),
            pl.BlockSpec((1, slots, block, width), where),
            pl.BlockSpec((1, slots, block, 2 * chunk * states), where),
            pl.BlockSpec((1, states, width), lambda d, i: (d, 0, 0)),
        ],
        out_specs=[
            pl.BlockSpec((1, slots, block, width), where),
            pl.BlockSpec((1, slots, block * states, width), where),
        ],
        out_shape=[
            jax.ShapeDtypeStruct((two, slots, length, width), f32),
            jax.ShapeDtypeStruct((two, slots, length * states, width), bf16),
        ],
        scratch_shapes=[
            pltpu.VMEM((slots, states, width), f32),
            pltpu.VMEM((slots, chunk * states, 2 * lanes), f32),
            pltpu.VMEM((slots, chunk * states, 2 * lanes), f32),
        ],
        compiler_params=pltpu.CompilerParams(vmem_limit_bytes=48 * 2**20),
        cost_estimate=pl.CostEstimate(
            flops=64 * 10**9, bytes_accessed=80 * 2**20, transcendentals=hidden_size
        ),
        name="scan_states",
    )(dt, x, bc, rate)


def scan_adjoint(dt, x, bc, rate, g, h):
    two, slots, length, width = dt.shape
    states = rate.shape[1]
    hidden_size = two * slots * length * states * width
    block = block_of(length)
    blocks = length // block

    def at(d, i):
        return jnp.where(d == 1, i, blocks - 1 - i)

    def where(d, i):
        return (d, 0, at(d, i), 0)

    def edge(d, i):
        mine = at(d, i) * block
        return (d, 0, jnp.clip(jnp.where(d == 1, mine + block, mine - 1), 0, length - 1), 0)

    return pl.pallas_call(
        functools.partial(adjoint_kernel, block // chunk),
        grid=(two, blocks),
        in_specs=[
            pl.BlockSpec((1, slots, block, width), where),
            pl.BlockSpec((1, slots, block, width), where),
            pl.BlockSpec((1, slots, block, 2 * chunk * states), where),
            pl.BlockSpec((1, states, width), lambda d, i: (d, 0, 0)),
            pl.BlockSpec((slots, block, width), lambda d, i: (0, at(d, i), 0)),
            pl.BlockSpec((1, slots, block * states, width), where),
            pl.BlockSpec((1, slots, states, width), edge),
        ],
        out_specs=[
            pl.BlockSpec((1, slots, block, width), where),
            pl.BlockSpec((1, slots, block, width), where),
            pl.BlockSpec((1, slots, block // chunk * 8, chunk * states), where),
            pl.BlockSpec((1, slots, states, width), lambda d, i: (d, 0, 0, 0)),
        ],
        out_shape=[
            jax.ShapeDtypeStruct((two, slots, length, width), f32),
            jax.ShapeDtypeStruct((two, slots, length, width), f32),
            jax.ShapeDtypeStruct((two, slots, length // chunk * 8, chunk * states), f32),
            jax.ShapeDtypeStruct((two, slots, states, width), f32),
        ],
        scratch_shapes=[
            pltpu.VMEM((slots, states, width), f32),
            pltpu.VMEM((slots, chunk * states, 2 * lanes), f32),
            pltpu.VMEM((slots, chunk * states, 2 * lanes), f32),
        ],
        compiler_params=pltpu.CompilerParams(vmem_limit_bytes=48 * 2**20),
        cost_estimate=pl.CostEstimate(
            flops=100 * 10**9, bytes_accessed=100 * 2**20, transcendentals=hidden_size
        ),
        name="scan_adjoint",
    )(dt, x, bc, rate, g, h, h)


def coefficient_rows(selection, rank, states):
    rows, width = selection.shape[1:]
    span = chunk * states
    col = jnp.arange(2 * span)
    origin = rank + (col // span) * states + col % states
    copies = (jnp.arange(width)[:, None] == origin[None, :]).astype(bf16)
    own = (jnp.arange(rows) % chunk)[:, None] == ((col % span) // states)[None, :]
    placed = jnp.einsum("drk,kc->drc", selection, copies, preferred_element_type=f32)
    return jnp.where(own, placed, 0.0).astype(bf16)


def widen(v, width):
    short = width - v.shape[-1]
    return v if short == 0 else jnp.pad(v, ((0, 0),) * (v.ndim - 1) + ((0, short),))


def remote(src, dst, sends, recvs, slot, axis, to):
    return pltpu.make_async_remote_copy(
        src_ref=src,
        dst_ref=dst,
        send_sem=sends.at[slot],
        recv_sem=recvs.at[slot],
        device_id={axis: to},
        device_id_type=pl.DeviceIdType.MESH,
    )


def each(first, last, body):
    def run(k, carry):
        body(k)
        return carry

    lax.fori_loop(first, last, run, 0)


def greet(peers):
    barrier = pltpu.get_barrier_semaphore()
    total = 0
    for axis, me, count in peers:

        def hello(k):
            pl.semaphore_signal(
                barrier,
                inc=1,
                device_id={axis: lax.rem(me + k, count)},
                device_id_type=pl.DeviceIdType.MESH,
            )

        each(1, count, hello)
        total += count - 1
    pl.semaphore_wait(barrier, total)


def total_kernel(line, v_ref, o_ref, pairbox, stage, inbox, *sems):
    pair_send, pair_recv, sum_send, sum_recv, out_send, out_recv, fwd_send, fwd_recv = sems
    me = lax.axis_index("seq")
    pos, core = me // 2, lax.rem(me, 2)
    partner = me + 1 - 2 * core
    barrier = pltpu.get_barrier_semaphore()

    def hello(to):
        pl.semaphore_signal(
            barrier, inc=1, device_id={"seq": to}, device_id_type=pl.DeviceIdType.MESH
        )

    hello(partner)
    each(1, line, lambda k: hello(lax.rem(pos + k, line) * 2 + core))
    pl.semaphore_wait(barrier, line)

    pair = remote(v_ref.at[:, :, 1 - core], pairbox, pair_send, pair_recv, 0, "seq", partner)
    pair.start()
    pair.wait_recv()

    def own(q):
        return v_ref[:, q, core].astype(f32) + pairbox[:, q].astype(f32)

    def summand(k):
        q = lax.rem(pos + k, line)
        return remote(
            stage.at[q], inbox.at[pos], sum_send, sum_recv, k - 1, "seq", q * 2 + core
        )

    def send(k):
        q = lax.rem(pos + k, line)
        stage[q] = own(q).astype(bf16)
        summand(k).start()

    each(1, line, send)

    def source(k):
        return lax.rem(pos - k + line, line)

    def arrived(k, total):
        q = source(k)
        remote(stage.at[q], inbox.at[q], sum_send, sum_recv, k - 1, "seq", partner).wait_recv()
        return total + inbox[q].astype(f32)

    total = lax.fori_loop(1, line, arrived, own(pos))
    o_ref[:, pos, core] = total.astype(bf16)

    def result(k):
        mine = o_ref.at[:, pos, core]
        return remote(
            mine, mine, out_send, out_recv, k - 1, "seq", lax.rem(pos + k, line) * 2 + core
        )

    def forward(k):
        block = o_ref.at[:, source(k), core]
        return remote(block, block, fwd_send, fwd_recv, k, "seq", partner)

    each(1, line, lambda k: result(k).start())
    forward(0).start()

    def pass_on(k):
        block = o_ref.at[:, source(k), core]
        remote(block, block, out_send, out_recv, k - 1, "seq", partner).wait_recv()
        forward(k).start()

    each(1, line, pass_on)

    def finish(k):
        block = o_ref.at[:, source(k), 1 - core]
        remote(block, block, fwd_send, fwd_recv, k, "seq", partner).wait_recv()
        forward(k).wait_send()

    each(0, line, finish)
    pair.wait_send()

    def drain(k):
        summand(k).wait_send()
        result(k).wait_send()

    each(1, line, drain)


def summed_everywhere(v, call):
    batch, length, width = v.shape
    shares = lax.axis_size("seq")
    line, rows = shares // 2, length // shares
    vmem = pl.BlockSpec(memory_space=pltpu.VMEM)
    dma = pltpu.SemaphoreType.DMA
    blocks = v.reshape(batch, line, 2, rows, width)
    out = pl.pallas_call(
        functools.partial(total_kernel, line),
        in_specs=[vmem],
        out_specs=vmem,
        out_shape=jax.ShapeDtypeStruct(blocks.shape, bf16),
        scratch_shapes=[
            pltpu.VMEM((batch, line, rows, width), bf16),
            pltpu.VMEM((line, batch, rows, width), bf16),
            pltpu.VMEM((line, batch, rows, width), bf16),
            dma((1,)),
            dma((1,)),
            dma((line,)),
            dma((line,)),
            dma((line,)),
            dma((line,)),
            dma((line,)),
            dma((line,)),
        ],
        compiler_params=pltpu.CompilerParams(
            collective_id=call, has_side_effects=True, vmem_limit_bytes=40 * 2**20
        ),
        cost_estimate=pl.CostEstimate(flops=25 * 10**9, bytes_accessed=2**20, transcendentals=0),
        name="sum_" + str(call),
    )(blocks)
    return out.reshape(v.shape)


def head_kernel(w_ref, mod_ref, box_ref, out_ref, parts, *sems):
    keep, w_send, w_recv, f_send, f_recv, m_send, m_recv = sems
    shares, peers = box_ref.shape[0], box_ref.shape[1]
    me, item = lax.axis_index("seq"), lax.axis_index("item")
    greet((("seq", me, shares), ("item", item, peers)))

    def modulation(k):
        return remote(
            mod_ref, parts.at[k - 1], m_send, m_recv, k - 1, "seq", lax.rem(me + k, shares)
        )

    def weight(k):
        to = lax.rem(me + k, shares)
        return remote(w_ref.at[to], box_ref.at[me, item], w_send, w_recv, k, "seq", to)

    each(1, shares, lambda k: weight(k).start())
    each(1, shares, lambda k: modulation(k).start())
    own = pltpu.make_async_copy(w_ref.at[me], box_ref.at[me, item], keep)
    own.start()

    def forward(k, t):
        block = box_ref.at[lax.rem(me - k + shares, shares), item]
        return remote(
            block, block, f_send, f_recv, k * (peers - 1) + t - 1, "item", lax.rem(item + t, peers)
        )

    own.wait()
    each(1, peers, lambda t: forward(0, t).start())

    def pass_on(k):
        source = lax.rem(me - k + shares, shares)
        block = box_ref.at[source, item]
        remote(block, block, w_send, w_recv, k, "seq", source).wait_recv()
        each(1, peers, lambda t: forward(k, t).start())

    each(1, shares, pass_on)

    def add(k, total):
        modulation(k).wait_recv()
        return total + parts[k - 1]

    out_ref[...] = lax.fori_loop(1, shares, add, mod_ref[...])

    def finish(k):
        def one(t):
            source = lax.rem(item - t + peers, peers)
            block = box_ref.at[lax.rem(me - k + shares, shares), source]
            remote(
                block, block, f_send, f_recv, k * (peers - 1) + t - 1, "item", source
            ).wait_recv()
            forward(k, t).wait_send()

        each(1, peers, one)

    each(0, shares, finish)

    def drain(k):
        weight(k).wait_send()
        modulation(k).wait_send()

    each(1, shares, drain)


def input_columns(blocks, modulation):
    shares, peers = lax.axis_size("seq"), lax.axis_size("item")
    vmem, anywhere = pl.BlockSpec(memory_space=pltpu.VMEM), pl.BlockSpec(memory_space=pl.ANY)
    dma = pltpu.SemaphoreType.DMA
    return pl.pallas_call(
        head_kernel,
        in_specs=[anywhere, vmem],
        out_specs=[anywhere, vmem],
        out_shape=[
            jax.ShapeDtypeStruct((shares, peers) + blocks.shape[1:], bf16),
            jax.ShapeDtypeStruct(modulation.shape, f32),
        ],
        scratch_shapes=[
            pltpu.VMEM((shares - 1,) + modulation.shape, f32),
            dma,
            dma((shares,)),
            dma((shares,)),
            dma((shares * (peers - 1),)),
            dma((shares * (peers - 1),)),
            dma((shares,)),
            dma((shares,)),
        ],
        compiler_params=pltpu.CompilerParams(collective_id=1, has_side_effects=True),
        cost_estimate=pl.CostEstimate(flops=40 * 10**9, bytes_accessed=2**20, transcendentals=0),
        name="input_columns",
    )(blocks, modulation)


def tail_kernel(
    g_ref, small_ref, select_ref, g_out, small_out, select_out, g_box, small_box, select_box, g_stage, *sems
):
    (a_send, a_recv, s_send, s_recv, c_send, c_recv, z_send, z_recv, y_send, y_recv) = sems[:10]
    f_send, f_recv, h_send, h_recv, e_send, e_recv = sems[10:]
    shares, peers = g_ref.shape[0], g_ref.shape[1]
    me, item = lax.axis_index("seq"), lax.axis_index("item")
    greet((("seq", me, shares), ("item", item, peers)))

    def other(t):
        return lax.rem(item + t, peers)

    def origin(t):
        return lax.rem(item - t + peers, peers)

    def ahead(k):
        return lax.rem(me + k, shares)

    def behind(k):
        return lax.rem(me - k + shares, shares)

    def flat(k, t):
        return k * (peers - 1) + t - 1

    def share_small(t):
        return remote(
            small_ref.at[other(t)], small_box.at[t - 1], s_send, s_recv, t - 1, "item", other(t)
        )

    def share_select(t):
        return remote(
            select_ref.at[other(t)], select_box.at[t - 1], c_send, c_recv, t - 1, "item", other(t)
        )

    def share_in(k, t):
        p = ahead(k)
        return remote(
            g_ref.at[p, other(t)], g_box.at[t - 1, p], a_send, a_recv, flat(k, t), "item", other(t)
        )

    each(1, peers, lambda t: share_small(t).start())
    each(1, shares, lambda k: each(1, peers, lambda t: share_in(k, t).start()))
    each(1, peers, lambda t: share_in(0, t).start())
    each(1, peers, lambda t: share_select(t).start())

    def add_small(t, total):
        share_small(t).wait_recv()
        return total + small_box[t - 1].astype(f32)

    small_out[item, me] = lax.fori_loop(
        1, peers, add_small, small_ref[item].astype(f32)
    ).astype(bf16)

    def spread_small(k):
        block = small_out.at[item, me]
        return remote(block, block, y_send, y_recv, k, "seq", ahead(k))

    each(1, shares, lambda k: spread_small(k).start())

    def sum_in(k):
        p = ahead(k)

        def add(t, total):
            share_in(k, t).wait_recv()
            return total + g_box[t - 1, p].astype(f32)

        return lax.fori_loop(1, peers, add, g_ref[p, item].astype(f32)).astype(bf16)

    def place_in(k):
        return remote(
            g_stage.at[k], g_out.at[item, me], z_send, z_recv, k, "seq", ahead(k)
        )

    def turn(k):
        g_stage[k] = sum_in(k)
        place_in(k).start()

    each(1, shares, turn)
    g_out[item, me] = sum_in(0)

    def forward_in(k, t):
        block = g_out.at[item, behind(k)]
        return remote(block, block, f_send, f_recv, flat(k, t), "item", other(t))

    def forward_small(k, t):
        block = small_out.at[item, behind(k)]
        return remote(block, block, h_send, h_recv, flat(k, t), "item", other(t))

    each(1, peers, lambda t: forward_in(0, t).start())
    each(1, peers, lambda t: forward_small(0, t).start())

    def add_select(t, total):
        share_select(t).wait_recv()
        return total + select_box[t - 1].astype(f32)

    select_out[item] = lax.fori_loop(
        1, peers, add_select, select_ref[item].astype(f32)
    ).astype(bf16)

    def forward_select(t):
        block = select_out.at[item]
        return remote(block, block, e_send, e_recv, t - 1, "item", other(t))

    each(1, peers, lambda t: forward_select(t).start())

    def pass_on(k):
        block = g_out.at[item, behind(k)]
        remote(block, block, z_send, z_recv, k, "seq", behind(k)).wait_recv()
        each(1, peers, lambda t: forward_in(k, t).start())
        little = small_out.at[item, behind(k)]
        remote(little, little, y_send, y_recv, k, "seq", behind(k)).wait_recv()
        each(1, peers, lambda t: forward_small(k, t).start())

    each(1, shares, pass_on)

    def finish(k):
        def one(t):
            block = g_out.at[origin(t), behind(k)]
            remote(block, block, f_send, f_recv, flat(k, t), "item", other(t)).wait_recv()
            little = small_out.at[origin(t), behind(k)]
            remote(little, little, h_send, h_recv, flat(k, t), "item", other(t)).wait_recv()
            forward_in(k, t).wait_send()
            forward_small(k, t).wait_send()
            share_in(k, t).wait_send()

        each(1, peers, one)

    each(0, shares, finish)

    def finish_item(t):
        block = select_out.at[origin(t)]
        remote(block, block, e_send, e_recv, t - 1, "item", other(t)).wait_recv()
        forward_select(t).wait_send()
        share_small(t).wait_send()
        share_select(t).wait_send()

    each(1, peers, finish_item)

    def finish_seq(k):
        spread_small(k).wait_send()
        place_in(k).wait_send()

    each(1, shares, finish_seq)


def weight_sums(g, small, select):
    shares, peers = g.shape[:2]
    vmem = pl.BlockSpec(memory_space=pltpu.VMEM)
    dma = pltpu.SemaphoreType.DMA
    some = peers - 1
    sizes = [shares * some] * 2 + [some] * 4 + [shares] * 4 + [shares * some] * 4 + [some] * 2
    return pl.pallas_call(
        tail_kernel,
        in_specs=[vmem] * 3,
        out_specs=[vmem] * 3,
        out_shape=[
            jax.ShapeDtypeStruct((peers, shares) + g.shape[2:], bf16),
            jax.ShapeDtypeStruct((peers, shares) + small.shape[1:], bf16),
            jax.ShapeDtypeStruct(select.shape, bf16),
        ],
        scratch_shapes=[
            pltpu.VMEM((some, shares) + g.shape[2:], bf16),
            pltpu.VMEM((some,) + small.shape[1:], bf16),
            pltpu.VMEM((some,) + select.shape[1:], bf16),
            pltpu.VMEM((shares,) + g.shape[2:], bf16),
        ]
        + [dma((size,)) for size in sizes],
        compiler_params=pltpu.CompilerParams(
            collective_id=2, has_side_effects=True, vmem_limit_bytes=40 * 2**20
        ),
        cost_estimate=pl.CostEstimate(flops=60 * 10**9, bytes_accessed=2**20, transcendentals=0),
        name="weight_sums",
    )(g, small, select)


def modulation_kernel(v_ref, out_ref, parts, m_send, m_recv, f_send, f_recv):
    shares = parts.shape[0] + 1
    peers = out_ref.shape[0]
    me, item = lax.axis_index("seq"), lax.axis_index("item")
    greet((("seq", me, shares), ("item", item, peers)))

    def part(k):
        return remote(v_ref, parts.at[k - 1], m_send, m_recv, k - 1, "seq", lax.rem(me + k, shares))

    each(1, shares, lambda k: part(k).start())

    def add(k, total):
        part(k).wait_recv()
        return total + parts[k - 1]

    out_ref[item] = lax.fori_loop(1, shares, add, v_ref[...])

    def forward(t):
        block = out_ref.at[item]
        return remote(block, block, f_send, f_recv, t - 1, "item", lax.rem(item + t, peers))

    each(1, peers, lambda t: forward(t).start())

    def finish(t):
        source = lax.rem(item - t + peers, peers)
        block = out_ref.at[source]
        remote(block, block, f_send, f_recv, t - 1, "item", source).wait_recv()
        forward(t).wait_send()

    each(1, peers, finish)
    each(1, shares, lambda k: part(k).wait_send())


def modulation_sums(v):
    shares, peers = lax.axis_size("seq"), lax.axis_size("item")
    vmem = pl.BlockSpec(memory_space=pltpu.VMEM)
    dma = pltpu.SemaphoreType.DMA
    return pl.pallas_call(
        modulation_kernel,
        in_specs=[vmem],
        out_specs=vmem,
        out_shape=jax.ShapeDtypeStruct((peers,) + v.shape, f32),
        scratch_shapes=[
            pltpu.VMEM((shares - 1,) + v.shape, f32),
            dma((shares,)),
            dma((shares,)),
            dma((peers,)),
            dma((peers,)),
        ],
        compiler_params=pltpu.CompilerParams(collective_id=3, has_side_effects=True),
        cost_estimate=pl.CostEstimate(flops=10 * 10**9, bytes_accessed=2**20, transcendentals=0),
        name="modulation_sums",
    )(v)


def filter_windows(x, taps, reverse):
    rim = taps - 1
    length = x.shape[1]
    padded = jnp.pad(x, ((0, 0), (rim, rim), (0, 0)))
    starts = [2 * rim - j if reverse else j for j in range(taps)]
    return [padded[:, s : s + length] for s in starts]


def per_device(
    tokens,
    timestep,
    slot_item,
    slot_valid,
    cotangent,
    in_weight,
    out_weight,
    select_weight,
    modulation_weight,
    delta_weight,
    filter_weight,
    filter_bias,
    delta_bias,
    decay_log,
    skip_gain,
    modulation_bias,
):
    slots, local, model = tokens.shape
    shares = lax.axis_size("seq")
    place = lax.axis_index("seq")
    rank, inner = delta_weight.shape[0], delta_weight.shape[1] // 2
    states = decay_log.shape[0]
    select = select_weight.shape[1] // 2
    taps = filter_weight.shape[0]
    rim = taps - 1
    length = local * shares
    rows = slots * length
    mine = inner // shares
    padded_width = -(-mine // lanes) * lanes
    shard_rows = modulation_weight.shape[0]
    items = timestep.shape[0]

    def own_columns(v):
        split = v.reshape(v.shape[:-1] + (2, shares, mine))
        return lax.dynamic_index_in_dim(split, place, split.ndim - 2, False)

    first_slot = lax.axis_index("item") * slots
    valid = lax.dynamic_slice_in_dim(slot_valid, first_slot, slots).astype(f32)[:, None, None]
    chooser = (slot_item[:, None] == jnp.arange(items, dtype=jnp.int32)[None, :]).astype(bf16)
    embedded = jnp.dot(chooser, timestep, preferred_element_type=f32)
    condition = jax.nn.silu(embedded).astype(bf16)
    own_features = lax.dynamic_slice_in_dim(condition, place * shard_rows, shard_rows, 1)
    own_condition = lax.dynamic_slice_in_dim(own_features, first_slot, slots, 0)
    modulation_part = jnp.dot(own_condition, modulation_weight, preferred_element_type=f32)
    peers = lax.axis_size("item")
    share_rows = in_weight.shape[0] // peers
    own_rows = lax.dynamic_slice_in_dim(
        in_weight, lax.axis_index("item") * share_rows, share_rows, 0
    )
    own_rows = jnp.moveaxis(own_rows.reshape(share_rows, 2, shares, mine), 2, 0)
    own_in, modulation = input_columns(
        own_rows.reshape(shares, share_rows, 2 * mine), modulation_part
    )
    own_in = own_in.reshape(model, 2 * mine)
    modulation = modulation + modulation_bias.astype(f32)[None, :]
    shift = modulation[:, None, :model]
    scale = modulation[:, None, model : 2 * model]
    gate = modulation[:, None, 2 * model :]

    all_tokens = lax.all_gather(tokens, "seq", axis=1, tiled=True)
    source = all_tokens.astype(f32)
    centered = source - jnp.mean(source, axis=-1, keepdims=True)
    spread = lax.rsqrt(jnp.mean(centered * centered, axis=-1, keepdims=True) + epsilon)
    mixed_in = (centered * spread * (1.0 + scale) + shift).astype(bf16).reshape(rows, model)
    projected = jnp.dot(mixed_in, own_in, preferred_element_type=f32).reshape(
        slots, length, 2 * mine
    )
    x_half = projected[..., :mine].astype(bf16)
    gate_half = projected[..., mine:]

    tap_weight = own_columns(filter_weight).astype(f32)
    tap_bias = own_columns(filter_bias).astype(f32)
    step_weight = own_columns(delta_weight)
    step_bias = own_columns(delta_bias)
    rate = -jnp.exp(own_columns(decay_log))
    skip = own_columns(skip_gain)

    filtered, activated, partial = [], [], []
    for d in range(2):
        f = tap_bias[d]
        for j, window in enumerate(filter_windows(x_half, taps, d == 1)):
            f = f + tap_weight[j, d] * window.astype(f32)
        a = jax.nn.silu(f).astype(bf16)
        filtered.append(f)
        activated.append(a)
        partial.append(
            jnp.dot(
                a.reshape(rows, mine),
                select_weight[:, d * select : (d + 1) * select],
                preferred_element_type=f32,
            )
        )
    selection = summed_everywhere(
        jnp.stack(partial).astype(bf16).reshape(2 * slots, length, select), 4
    ).reshape(2, rows, select)
    selection, late_cotangent = lax.optimization_barrier((selection, cotangent))
    all_cotangent = lax.all_gather(late_cotangent, "seq", axis=1, tiled=True)
    delta_rank = selection[:, :, :rank]
    bc = coefficient_rows(selection, rank, states).reshape(2, slots, length, -1)
    step_pre = [
        jnp.dot(delta_rank[d], step_weight[:, d], preferred_element_type=f32) + step_bias[d]
        for d in range(2)
    ]
    step = jnp.stack([jax.nn.softplus(p) for p in step_pre]).reshape(2, slots, length, mine)
    active = jnp.stack(activated)
    wide_step = widen(step, padded_width)
    wide_active = widen(active, padded_width)
    wide_rate = widen(jnp.swapaxes(rate, 0, 1) * log2e, padded_width)
    scanned, hidden = scan_states(wide_step, wide_active, bc, wide_rate)
    scanned = scanned[..., :mine]
    scanned_sum = scanned[0] + scanned[1]
    for d in range(2):
        scanned_sum = scanned_sum + skip[d] * activated[d].astype(f32)
    silu_gate = jax.nn.silu(gate_half)
    mixed_out = (scanned_sum * silu_gate).astype(bf16).reshape(rows, mine)
    own_cotangent = cotangent.astype(f32)

    grad_branch = (
        (valid * gate * all_cotangent.astype(f32)).astype(bf16).reshape(rows, model)
    )
    grad_mixed = dot_cols(grad_branch, out_weight).reshape(slots, length, mine)
    grad_scanned = grad_mixed * silu_gate
    grad_gate_half = grad_mixed * scanned_sum * silu_slope(gate_half)
    grad_out = dot_rows(mixed_out, grad_branch).astype(bf16)
    branch_part = (
        jnp.dot(mixed_out, out_weight, preferred_element_type=f32)
        .astype(bf16)
        .reshape(slots, length, model)
    )
    branch_part, grad_out, scan_grad = lax.optimization_barrier(
        (branch_part, grad_out, grad_scanned)
    )
    branch_part = lax.psum_scatter(branch_part, "seq", scatter_dimension=1, tiled=True)
    grad_out, branch_part = lax.optimization_barrier((grad_out, branch_part))
    grad_out = lax.psum(grad_out, "item")
    grad_step, grad_input, grad_coef, grad_rate = scan_adjoint(
        wide_step, wide_active, bc, wide_rate, widen(scan_grad, padded_width), hidden
    )
    grad_decay = jnp.sum(grad_rate, axis=1)[..., :mine] * ln2
    grad_coef = grad_coef.reshape(2, slots, length // chunk, 8, chunk, states)[:, :, :, :2]
    grad_coef = jnp.moveaxis(grad_coef, 3, 4).reshape(2, rows, 2 * states)
    parts = []
    grad_skip, grad_step_bias, grad_delta = [], [], []
    for d in range(2):
        grad_skip.append(jnp.sum(grad_scanned * activated[d].astype(f32), axis=(0, 1)))
        grad_pre = grad_step[d, ..., :mine].reshape(rows, mine) * jax.nn.sigmoid(step_pre[d])
        low = grad_pre.astype(bf16)
        grad_step_bias.append(jnp.sum(grad_pre, axis=0))
        grad_delta.append(dot_rows(delta_rank[d], low))
        parts.append(jnp.concatenate([dot_cols(low, step_weight[:, d]), grad_coef[d]], axis=1))
    parts[1], grad_out, branch_part = lax.optimization_barrier((parts[1], grad_out, branch_part))
    grad_selection = summed_everywhere(
        jnp.stack(parts).astype(bf16).reshape(2 * slots, length, select), 5
    ).reshape(2, rows, select)
    grad_x = jnp.zeros((slots, length, mine), f32)
    grad_select, grad_taps, grad_tap_bias = [], [], []
    for d in range(2):
        block = select_weight[:, d * select : (d + 1) * select]
        grad_select.append(dot_rows(activated[d].reshape(rows, mine), grad_selection[d]))
        grad_active = (
            grad_input[d, ..., :mine]
            + skip[d] * grad_scanned
            + dot_cols(grad_selection[d], block).reshape(slots, length, mine)
        )
        grad_filtered = grad_active * silu_slope(filtered[d])
        grad_tap_bias.append(jnp.sum(grad_filtered, axis=(0, 1)))
        windows = filter_windows(x_half, taps, d == 1)
        grad_taps.append(
            jnp.stack([jnp.sum(grad_filtered * w.astype(f32), axis=(0, 1)) for w in windows])
        )
        for j, window in enumerate(filter_windows(grad_filtered, taps, d == 0)):
            grad_x = grad_x + tap_weight[j, d] * window
    grad_projected = (
        jnp.concatenate([grad_x, grad_gate_half], axis=2).astype(bf16).reshape(rows, 2 * mine)
    )
    grad_mixed_in = lax.psum_scatter(
        dot_cols(grad_projected, own_in).astype(bf16).reshape(slots, length, model),
        "seq",
        scatter_dimension=1,
        tiled=True,
    ).astype(f32)
    grad_in = dot_rows(mixed_in, grad_projected).astype(bf16)
    own_source = tokens.astype(f32)
    own_centered = own_source - jnp.mean(own_source, axis=-1, keepdims=True)
    own_spread = lax.rsqrt(
        jnp.mean(own_centered * own_centered, axis=-1, keepdims=True) + epsilon
    )
    normed = own_centered * own_spread
    grad_normed = grad_mixed_in * (1.0 + scale)
    grad_source = own_spread * (
        grad_normed
        - jnp.mean(grad_normed, axis=-1, keepdims=True)
        - normed * jnp.mean(grad_normed * normed, axis=-1, keepdims=True)
    )
    grad_tokens = (own_cotangent + grad_source).astype(bf16)
    branch = branch_part.astype(f32)
    output = (tokens.astype(f32) + valid * gate * branch).astype(bf16)
    grad_gate = jnp.sum(valid * own_cotangent * branch, axis=1)
    grad_modulation = jnp.concatenate(
        [jnp.sum(grad_mixed_in, axis=1), jnp.sum(grad_mixed_in * normed, axis=1), grad_gate], axis=1
    )
    grad_modulation = modulation_sums(grad_modulation).reshape(-1, 3 * model)
    grad_modulation_weight = lax.dot_general(
        own_features.astype(f32),
        grad_modulation,
        (((0,), (0,)), ((), ())),
        precision=lax.Precision.HIGHEST,
        preferred_element_type=f32,
    )
    small = jnp.concatenate(
        [
            jnp.stack(grad_delta, 1),
            jnp.stack(grad_taps, 1),
            jnp.stack(grad_tap_bias)[None],
            jnp.stack(grad_step_bias)[None],
            jnp.swapaxes(grad_decay, 0, 1),
            jnp.stack(grad_skip)[None],
        ],
        axis=0,
    )
    small_rows = small.shape[0]
    share = -(-small_rows // (16 * peers)) * 16
    small = jnp.pad(
        small.astype(bf16).reshape(small_rows, 2 * mine), ((0, peers * share - small_rows), (0, 0))
    )
    grad_select = jnp.concatenate(grad_select, axis=1).astype(bf16)
    grad_in, small, grad_select = weight_sums(
        grad_in.reshape(shares, peers, share_rows, 2 * mine),
        small.reshape(peers, share, 2 * mine),
        grad_select.reshape(peers, mine // peers, 2 * select),
    )
    grad_in = grad_in.reshape(peers, shares, share_rows, 2, mine)
    grad_in = jnp.transpose(grad_in, (0, 2, 3, 1, 4)).reshape(peers * share_rows, 2 * inner)
    grad_select = grad_select.reshape(mine, 2 * select)
    small = small.reshape(peers, shares, share, 2, mine)
    small = jnp.transpose(small, (0, 2, 3, 1, 4)).reshape(peers * share, 2 * inner).astype(f32)
    cuts = [rank, rank + taps, rank + taps + 1, rank + taps + 2, rank + taps + 2 + states]
    return (
        output,
        grad_tokens,
        grad_in.astype(f32),
        grad_out.astype(f32),
        grad_select.astype(f32),
        grad_modulation_weight,
        small[: cuts[0]],
        small[cuts[0] : cuts[1]],
        small[cuts[1]],
        small[cuts[2]],
        small[cuts[3] : cuts[4]],
        small[cuts[4]],
        jnp.sum(grad_modulation, axis=0),
    )


def solution(mesh):
    tokens, rows, same = P("item", "seq", None), P("seq", None), P()
    return jax.shard_map(
        per_device,
        mesh=mesh,
        in_specs=(tokens, same, same, same, tokens, rows, rows, rows, rows) + (same,) * 7,
        out_specs=(tokens, tokens, rows, rows, rows, rows) + (same,) * 7,
        check_vma=False,
    )
```

```python
import functools
import math

import jax
import jax.numpy as jnp
from jax import lax
from jax.experimental import pallas as pl
from jax.experimental.pallas import tpu as pltpu
from jax.sharding import PartitionSpec as P

epsilon = 1e-06
log2e = 1.4426950408889634
ln2 = 0.6931471805599453
chunk = 16
lanes = 128
f32 = jnp.float32
bf16 = jnp.bfloat16


def silu_slope(v):
    s = jax.nn.sigmoid(v)
    return s * (1.0 + v * (1.0 - s))


def dot_rows(a, b):
    return lax.dot_general(a, b, (((0,), (0,)), ((), ())), preferred_element_type=f32)


def dot_cols(a, b):
    return lax.dot_general(a, b, (((1,), (1,)), ((), ())), preferred_element_type=f32)


def fold_sublanes(parts):
    outs = []
    for first in range(0, len(parts), 8):
        cur = parts[first : first + 8]
        row = lax.broadcasted_iota(jnp.int32, cur[0].shape, 0)
        for hop in (4, 2, 1):
            keep = (row // hop) % 2 == 0
            half = len(cur) // 2
            merged = []
            for j in range(half):
                a, b = cur[j], cur[j + half]
                x, y = jnp.where(keep, a, b), jnp.where(keep, b, a)
                if hop == 4:
                    moved = pltpu.roll(y, 4, 0)
                else:
                    moved = jnp.where(keep, pltpu.roll(y, 8 - hop, 0), pltpu.roll(y, hop, 0))
                merged.append(x + moved)
            cur = merged
        outs.append(cur[0])
    return jnp.concatenate(outs, axis=0)


def wide(v, groups):
    return v if groups == 1 else jnp.concatenate([v] * groups, axis=1)


def spread_matrix():
    rows = lax.broadcasted_iota(jnp.int32, (2 * chunk, 2 * lanes), 0) // chunk
    cols = lax.broadcasted_iota(jnp.int32, (2 * chunk, 2 * lanes), 1) // lanes
    return (rows == cols).astype(f32).astype(bf16)


def chunk_sweep(count, body, spread, first, second):
    spread(0, first)
    if count == 1:
        body(0, first)
        return

    def pair(k, carry):
        spread(2 * k + 1, second)
        body(2 * k, first)
        spread(jnp.minimum(2 * k + 2, count - 1), first)
        body(2 * k + 1, second)
        return carry

    lax.fori_loop(0, count // 2, pair, 0)


def place_coefficients(selection, copies):
    placed = jnp.dot(selection, copies, preferred_element_type=f32)
    row = lax.rem(lax.broadcasted_iota(jnp.int32, placed.shape, 0), chunk)
    span = placed.shape[1] // 2
    col = lax.rem(lax.broadcasted_iota(jnp.int32, placed.shape, 1), span) // (span // chunk)
    return jnp.where(row == col, placed, 0.0).astype(bf16)


def softplus(v):
    return jnp.maximum(v, 0.0) + jnp.log1p(jnp.exp(-jnp.abs(v)))


def states_kernel(
    count,
    sel_ref,
    x_ref,
    w_ref,
    bias_ref,
    r_ref,
    copies_ref,
    y_ref,
    h_ref,
    dt_ref,
    state,
    bc,
    even,
    odd,
):
    slots, width = dt_ref.shape[1], dt_ref.shape[3]
    groups = width // lanes
    states = r_ref.shape[1]

    @pl.when(pl.program_id(1) == 0)
    def _():
        state[...] = jnp.zeros_like(state)

    for s in range(slots):
        selection = sel_ref[0, s]
        dt_ref[0, s] = softplus(
            jnp.dot(selection, w_ref[0], preferred_element_type=f32) + bias_ref[0]
        )
        bc[s] = place_coefficients(selection, copies_ref[...])

    def one_direction(reverse):
        mix = spread_matrix()

        def place(i):
            return (count - 1 - i) if reverse else i

        def spread(i, into):
            start = pl.multiple_of(place(i) * chunk, chunk)
            for s in range(slots):
                both = bc[s, pl.ds(start, chunk), :]
                span = both.shape[1] // 2
                into[s] = dot_rows(jnp.concatenate([both[:, :span], both[:, span:]], axis=0), mix)

        def body(i, held):
            start = pl.multiple_of(place(i) * chunk, chunk)
            order = range(chunk - 1, -1, -1) if reverse else range(chunk)
            for s in range(slots):
                h = state[s]
                rate = r_ref[0]
                dt = dt_ref[0, s, pl.ds(start, chunk), :]
                u = dt * x_ref[0, s, pl.ds(start, chunk), :].astype(f32)
                kept, sums = [None] * chunk, [None] * chunk
                for t in order:
                    rows = slice(t * states, (t + 1) * states)
                    b = wide(held[s, rows, :lanes], groups)
                    c = wide(held[s, rows, lanes:], groups)
                    h = jnp.exp2(dt[t : t + 1] * rate) * h + u[t : t + 1] * b
                    kept[t] = h.astype(bf16)
                    p = h * c
                    sums[t] = p[:8] + p[8:]
                size = chunk * states
                h_ref[0, s, pl.ds(pl.multiple_of(start * states, size), size), :] = jnp.concatenate(
                    kept, axis=0
                )
                y_ref[0, s, pl.ds(start, chunk), :] = fold_sublanes(sums)
                state[s] = h

        chunk_sweep(count, body, spread, even, odd)

    for d in range(2):

        @pl.when(pl.program_id(0) == d)
        def _():
            one_direction(d == 1)


def adjoint_kernel(
    count,
    sel_ref,
    x_ref,
    w_ref,
    r_ref,
    copies_ref,
    skip_ref,
    dt_ref,
    g_ref,
    h_ref,
    edge_ref,
    low_ref,
    input_ref,
    gsel_ref,
    decay_ref,
    sums_ref,
    pending,
    bc,
    coefs,
    even,
    odd,
):
    slots, width = dt_ref.shape[1], dt_ref.shape[3]
    groups = width // lanes
    states = r_ref.shape[1]
    last_block = pl.program_id(1) == pl.num_programs(1) - 1

    @pl.when(pl.program_id(1) == 0)
    def _():
        pending[...] = jnp.zeros_like(pending)
        decay_ref[...] = jnp.zeros_like(decay_ref)
        sums_ref[...] = jnp.zeros_like(sums_ref)

    for s in range(slots):
        bc[s] = place_coefficients(sel_ref[0, s], copies_ref[...])

    def one_direction(reverse):
        mix = spread_matrix()
        picks = (
            lax.broadcasted_iota(jnp.int32, (8, 2 * lanes), 0)
            == lax.broadcasted_iota(jnp.int32, (8, 2 * lanes), 1) // lanes
        ).astype(f32).astype(bf16)

        def place(i):
            return i if reverse else (count - 1 - i)

        def spread(i, into):
            start = pl.multiple_of(place(i) * chunk, chunk)
            for s in range(slots):
                both = bc[s, pl.ds(start, chunk), :]
                span = both.shape[1] // 2
                into[s] = dot_rows(jnp.concatenate([both[:, :span], both[:, span:]], axis=0), mix)

        def body(i, held):
            here = place(i)
            start = pl.multiple_of(here * chunk, chunk)
            order = range(chunk) if reverse else range(chunk - 1, -1, -1)
            size = chunk * states
            base = pl.multiple_of(start * states, size)
            at_end = here == (count - 1 if reverse else 0)
            outer = jnp.where(last_block, 0.0, 1.0)
            near = pl.multiple_of(
                jnp.clip(start + (chunk if reverse else -1), 0, count * chunk - 1) * states, states
            )
            for s in range(slots):
                pend = pending[s]
                rate = r_ref[0]
                dt = dt_ref[0, s, pl.ds(start, chunk), :]
                x = x_ref[0, s, pl.ds(start, chunk), :].astype(f32)
                g = g_ref[s, pl.ds(start, chunk), :].astype(f32)
                u = dt * x
                before = jnp.where(
                    at_end,
                    edge_ref[0, s].astype(f32) * outer,
                    h_ref[0, s, pl.ds(near, states), :].astype(f32),
                )
                total = decay_ref[0, s]
                rate_sums, into_sums = [None] * chunk, [None] * chunk
                coef = [None] * chunk
                hidden = h_ref[0, s, pl.ds(base, size), :]
                now = hidden[order[0] * states : (order[0] + 1) * states].astype(f32)
                for k, t in enumerate(order):
                    rows = slice(t * states, (t + 1) * states)
                    b = wide(held[s, rows, :lanes], groups)
                    c = wide(held[s, rows, lanes:], groups)
                    if k + 1 < chunk:
                        q = order[k + 1]
                        prev = hidden[q * states : (q + 1) * states].astype(f32)
                    else:
                        prev = before
                    gt = g[t : t + 1]
                    adj = c * gt + pend
                    pend = jnp.exp2(dt[t : t + 1] * rate) * adj
                    through = pend * prev * rate
                    total = total + through * dt[t : t + 1]
                    rate_sums[t] = through[:8] + through[8:]
                    w = adj * b
                    into_sums[t] = w[:8] + w[8:]
                    cb, cc = adj * u[t : t + 1], now * gt
                    sb, sc = cb[:, :lanes], cc[:, :lanes]
                    for j in range(1, groups):
                        sb = sb + cb[:, j * lanes : (j + 1) * lanes]
                        sc = sc + cc[:, j * lanes : (j + 1) * lanes]
                    coef[t] = jnp.concatenate([sb, sc], axis=1).astype(bf16)
                    now = prev
                pending[s] = pend
                decay_ref[0, s] = total
                weighted = fold_sublanes(into_sums)
                few = dt * (1.0 - dt * (0.5 - dt * (1.0 / 6.0 - dt * (1.0 / 24.0))))
                slope = jnp.where(dt < 0.03, few, 1.0 - jnp.exp(-dt))
                grad_pre = (fold_sublanes(rate_sums) * ln2 + weighted * x) * slope
                low_ref[0, s, pl.ds(start, chunk), :] = grad_pre.astype(bf16)
                input_ref[0, s, pl.ds(start, chunk), :] = weighted * dt + skip_ref[0] * g
                gx = g * x
                sums_ref[0] += jnp.concatenate(
                    [grad_pre[:8] + grad_pre[8:], gx[:8] + gx[8:]], axis=0
                )
                coefs[s, pl.ds(pl.multiple_of(here * 8, 8), 8), :] = dot_cols(
                    picks, jnp.concatenate(coef, axis=0)
                )

        chunk_sweep(count, body, spread, even, odd)

    for d in range(2):

        @pl.when(pl.program_id(0) == d)
        def _():
            one_direction(d == 1)


    own = lax.broadcasted_iota(jnp.int32, (chunk, chunk * states), 0) == (
        lax.broadcasted_iota(jnp.int32, (chunk, chunk * states), 1) // states
    )
    for s in range(slots):
        placed = []
        for c in range(count):
            placed.append(
                jnp.concatenate(
                    [
                        jnp.where(own, coefs[s, c * 8 + k : c * 8 + k + 1, :], 0.0)
                        for k in range(2)
                    ],
                    axis=1,
                )
            )
        placed = jnp.concatenate(placed, axis=0).astype(bf16)
        gsel_ref[0, s] = (
            dot_cols(low_ref[0, s], w_ref[0]) + dot_cols(placed, copies_ref[...])
        ).astype(bf16)


def block_of(length):
    return math.gcd(length, 128)


def scan_states(selection, x, weight, bias, rate, copies):
    two, slots, length, width = x.shape
    select = selection.shape[3]
    states = rate.shape[1]
    hidden_size = two * slots * length * states * width
    block = block_of(length)
    blocks = length // block
    spread = copies.shape[1]

    def where(d, i):
        return (d, 0, jnp.where(d == 1, blocks - 1 - i, i), 0)

    def by_direction(d, i):
        return (d, 0, 0)

    return pl.pallas_call(
        functools.partial(states_kernel, block // chunk),
        grid=(two, blocks),
        in_specs=[
            pl.BlockSpec((1, slots, block, select), where),
            pl.BlockSpec((1, slots, block, width), where),
            pl.BlockSpec((1, select, width), by_direction),
            pl.BlockSpec((1, 1, width), by_direction),
            pl.BlockSpec((1, states, width), by_direction),
            pl.BlockSpec((select, spread), lambda d, i: (0, 0)),
        ],
        out_specs=[
            pl.BlockSpec((1, slots, block, width), where),
            pl.BlockSpec((1, slots, block * states, width), where),
            pl.BlockSpec((1, slots, block, width), where),
        ],
        out_shape=[
            jax.ShapeDtypeStruct((two, slots, length, width), f32),
            jax.ShapeDtypeStruct((two, slots, length * states, width), bf16),
            jax.ShapeDtypeStruct((two, slots, length, width), f32),
        ],
        scratch_shapes=[
            pltpu.VMEM((slots, states, width), f32),
            pltpu.VMEM((slots, block, spread), bf16),
            pltpu.VMEM((slots, chunk * states, 2 * lanes), f32),
            pltpu.VMEM((slots, chunk * states, 2 * lanes), f32),
        ],
        compiler_params=pltpu.CompilerParams(vmem_limit_bytes=48 * 2**20),
        cost_estimate=pl.CostEstimate(
            flops=64 * 10**9, bytes_accessed=80 * 2**20, transcendentals=hidden_size
        ),
        name="scan_states",
    )(selection, x, weight, bias, rate, copies)


def scan_adjoint(selection, x, weight, rate, copies, skip, dt, g, h):
    two, slots, length, width = dt.shape
    select = selection.shape[3]
    states = rate.shape[1]
    hidden_size = two * slots * length * states * width
    block = block_of(length)
    blocks = length // block
    spread = copies.shape[1]

    def at(d, i):
        return jnp.where(d == 1, i, blocks - 1 - i)

    def where(d, i):
        return (d, 0, at(d, i), 0)

    def edge(d, i):
        mine = at(d, i) * block
        return (d, 0, jnp.clip(jnp.where(d == 1, mine + block, mine - 1), 0, length - 1), 0)

    def by_direction(d, i):
        return (d, 0, 0)

    return pl.pallas_call(
        functools.partial(adjoint_kernel, block // chunk),
        grid=(two, blocks),
        in_specs=[
            pl.BlockSpec((1, slots, block, select), where),
            pl.BlockSpec((1, slots, block, width), where),
            pl.BlockSpec((1, select, width), by_direction),
            pl.BlockSpec((1, states, width), by_direction),
            pl.BlockSpec((select, spread), lambda d, i: (0, 0)),
            pl.BlockSpec((1, 1, width), by_direction),
            pl.BlockSpec((1, slots, block, width), where),
            pl.BlockSpec((slots, block, width), lambda d, i: (0, at(d, i), 0)),
            pl.BlockSpec((1, slots, block * states, width), where),
            pl.BlockSpec((1, slots, states, width), edge),
        ],
        out_specs=[
            pl.BlockSpec((1, slots, block, width), where),
            pl.BlockSpec((1, slots, block, width), where),
            pl.BlockSpec((1, slots, block, select), where),
            pl.BlockSpec((1, slots, states, width), lambda d, i: (d, 0, 0, 0)),
            pl.BlockSpec((1, 16, width), by_direction),
        ],
        out_shape=[
            jax.ShapeDtypeStruct((two, slots, length, width), bf16),
            jax.ShapeDtypeStruct((two, slots, length, width), f32),
            jax.ShapeDtypeStruct((two, slots, length, select), bf16),
            jax.ShapeDtypeStruct((two, slots, states, width), f32),
            jax.ShapeDtypeStruct((two, 16, width), f32),
        ],
        scratch_shapes=[
            pltpu.VMEM((slots, states, width), f32),
            pltpu.VMEM((slots, block, spread), bf16),
            pltpu.VMEM((slots, block // chunk * 8, chunk * states), f32),
            pltpu.VMEM((slots, chunk * states, 2 * lanes), f32),
            pltpu.VMEM((slots, chunk * states, 2 * lanes), f32),
        ],
        compiler_params=pltpu.CompilerParams(vmem_limit_bytes=48 * 2**20),
        cost_estimate=pl.CostEstimate(
            flops=100 * 10**9, bytes_accessed=100 * 2**20, transcendentals=hidden_size
        ),
        name="scan_adjoint",
    )(selection, x, weight, rate, copies, skip, dt, g, h, h)


def coefficient_copies(width, rank, states):
    span = chunk * states
    col = jnp.arange(2 * span)
    origin = rank + (col // span) * states + col % states
    return (jnp.arange(width)[:, None] == origin[None, :]).astype(bf16)


def widen(v, width):
    short = width - v.shape[-1]
    return v if short == 0 else jnp.pad(v, ((0, 0),) * (v.ndim - 1) + ((0, short),))


def remote(src, dst, sends, recvs, slot, axis, to):
    return pltpu.make_async_remote_copy(
        src_ref=src,
        dst_ref=dst,
        send_sem=sends.at[slot],
        recv_sem=recvs.at[slot],
        device_id={axis: to},
        device_id_type=pl.DeviceIdType.MESH,
    )


def each(first, last, body):
    def run(k, carry):
        body(k)
        return carry

    lax.fori_loop(first, last, run, 0)


def greet(peers):
    barrier = pltpu.get_barrier_semaphore()
    total = 0
    for axis, me, count in peers:

        def hello(k):
            pl.semaphore_signal(
                barrier,
                inc=1,
                device_id={axis: lax.rem(me + k, count)},
                device_id_type=pl.DeviceIdType.MESH,
            )

        each(1, count, hello)
        total += count - 1
    pl.semaphore_wait(barrier, total)


def total_kernel(line, v_ref, o_ref, pairbox, stage, inbox, *sems):
    pair_send, pair_recv, sum_send, sum_recv, out_send, out_recv, fwd_send, fwd_recv = sems
    me = lax.axis_index("seq")
    pos, core = me // 2, lax.rem(me, 2)
    partner = me + 1 - 2 * core
    barrier = pltpu.get_barrier_semaphore()

    def hello(to):
        pl.semaphore_signal(
            barrier, inc=1, device_id={"seq": to}, device_id_type=pl.DeviceIdType.MESH
        )

    hello(partner)
    each(1, line, lambda k: hello(lax.rem(pos + k, line) * 2 + core))
    pl.semaphore_wait(barrier, line)

    pair = remote(v_ref.at[:, :, 1 - core], pairbox, pair_send, pair_recv, 0, "seq", partner)
    pair.start()
    pair.wait_recv()

    def own(q):
        return v_ref[:, q, core].astype(f32) + pairbox[:, q].astype(f32)

    def summand(k):
        q = lax.rem(pos + k, line)
        return remote(
            stage.at[q], inbox.at[pos], sum_send, sum_recv, k - 1, "seq", q * 2 + core
        )

    def send(k):
        q = lax.rem(pos + k, line)
        stage[q] = own(q).astype(bf16)
        summand(k).start()

    each(1, line, send)

    def source(k):
        return lax.rem(pos - k + line, line)

    def arrived(k, total):
        q = source(k)
        remote(stage.at[q], inbox.at[q], sum_send, sum_recv, k - 1, "seq", partner).wait_recv()
        return total + inbox[q].astype(f32)

    total = lax.fori_loop(1, line, arrived, own(pos))
    o_ref[:, pos, core] = total.astype(bf16)

    def result(k):
        mine = o_ref.at[:, pos, core]
        return remote(
            mine, mine, out_send, out_recv, k - 1, "seq", lax.rem(pos + k, line) * 2 + core
        )

    def forward(k):
        block = o_ref.at[:, source(k), core]
        return remote(block, block, fwd_send, fwd_recv, k, "seq", partner)

    each(1, line, lambda k: result(k).start())
    forward(0).start()

    def pass_on(k):
        block = o_ref.at[:, source(k), core]
        remote(block, block, out_send, out_recv, k - 1, "seq", partner).wait_recv()
        forward(k).start()

    each(1, line, pass_on)

    def finish(k):
        block = o_ref.at[:, source(k), 1 - core]
        remote(block, block, fwd_send, fwd_recv, k, "seq", partner).wait_recv()
        forward(k).wait_send()

    each(0, line, finish)
    pair.wait_send()

    def drain(k):
        summand(k).wait_send()
        result(k).wait_send()

    each(1, line, drain)


def summed_everywhere(v, call):
    batch, length, width = v.shape
    shares = lax.axis_size("seq")
    line, rows = shares // 2, length // shares
    vmem = pl.BlockSpec(memory_space=pltpu.VMEM)
    dma = pltpu.SemaphoreType.DMA
    blocks = v.reshape(batch, line, 2, rows, width)
    out = pl.pallas_call(
        functools.partial(total_kernel, line),
        in_specs=[vmem],
        out_specs=vmem,
        out_shape=jax.ShapeDtypeStruct(blocks.shape, bf16),
        scratch_shapes=[
            pltpu.VMEM((batch, line, rows, width), bf16),
            pltpu.VMEM((line, batch, rows, width), bf16),
            pltpu.VMEM((line, batch, rows, width), bf16),
            dma((1,)),
            dma((1,)),
            dma((line,)),
            dma((line,)),
            dma((line,)),
            dma((line,)),
            dma((line,)),
            dma((line,)),
        ],
        compiler_params=pltpu.CompilerParams(
            collective_id=call, has_side_effects=True, vmem_limit_bytes=40 * 2**20
        ),
        cost_estimate=pl.CostEstimate(flops=25 * 10**9, bytes_accessed=2**20, transcendentals=0),
        name="sum_" + str(call),
    )(blocks)
    return out.reshape(v.shape)


def head_kernel(w_ref, mod_ref, box_ref, out_ref, parts, *sems):
    keep, w_send, w_recv, f_send, f_recv, m_send, m_recv = sems
    shares, peers = box_ref.shape[0], box_ref.shape[1]
    me, item = lax.axis_index("seq"), lax.axis_index("item")
    greet((("seq", me, shares), ("item", item, peers)))

    def modulation(k):
        return remote(
            mod_ref, parts.at[k - 1], m_send, m_recv, k - 1, "seq", lax.rem(me + k, shares)
        )

    def weight(k):
        to = lax.rem(me + k, shares)
        return remote(w_ref.at[to], box_ref.at[me, item], w_send, w_recv, k, "seq", to)

    each(1, shares, lambda k: weight(k).start())
    each(1, shares, lambda k: modulation(k).start())
    own = pltpu.make_async_copy(w_ref.at[me], box_ref.at[me, item], keep)
    own.start()

    def forward(k, t):
        block = box_ref.at[lax.rem(me - k + shares, shares), item]
        return remote(
            block, block, f_send, f_recv, k * (peers - 1) + t - 1, "item", lax.rem(item + t, peers)
        )

    own.wait()
    each(1, peers, lambda t: forward(0, t).start())

    def pass_on(k):
        source = lax.rem(me - k + shares, shares)
        block = box_ref.at[source, item]
        remote(block, block, w_send, w_recv, k, "seq", source).wait_recv()
        each(1, peers, lambda t: forward(k, t).start())

    each(1, shares, pass_on)

    def add(k, total):
        modulation(k).wait_recv()
        return total + parts[k - 1]

    out_ref[...] = lax.fori_loop(1, shares, add, mod_ref[...])

    def finish(k):
        def one(t):
            source = lax.rem(item - t + peers, peers)
            block = box_ref.at[lax.rem(me - k + shares, shares), source]
            remote(
                block, block, f_send, f_recv, k * (peers - 1) + t - 1, "item", source
            ).wait_recv()
            forward(k, t).wait_send()

        each(1, peers, one)

    each(0, shares, finish)

    def drain(k):
        weight(k).wait_send()
        modulation(k).wait_send()

    each(1, shares, drain)


def input_columns(blocks, modulation):
    shares, peers = lax.axis_size("seq"), lax.axis_size("item")
    vmem, anywhere = pl.BlockSpec(memory_space=pltpu.VMEM), pl.BlockSpec(memory_space=pl.ANY)
    dma = pltpu.SemaphoreType.DMA
    return pl.pallas_call(
        head_kernel,
        in_specs=[anywhere, vmem],
        out_specs=[anywhere, vmem],
        out_shape=[
            jax.ShapeDtypeStruct((shares, peers) + blocks.shape[1:], bf16),
            jax.ShapeDtypeStruct(modulation.shape, f32),
        ],
        scratch_shapes=[
            pltpu.VMEM((shares - 1,) + modulation.shape, f32),
            dma,
            dma((shares,)),
            dma((shares,)),
            dma((shares * (peers - 1),)),
            dma((shares * (peers - 1),)),
            dma((shares,)),
            dma((shares,)),
        ],
        compiler_params=pltpu.CompilerParams(collective_id=1, has_side_effects=True),
        cost_estimate=pl.CostEstimate(flops=40 * 10**9, bytes_accessed=2**20, transcendentals=0),
        name="input_columns",
    )(blocks, modulation)


def tail_kernel(cuts, g_ref, small_ref, select_ref, *refs):
    if cuts is None:
        g_out, small_out, select_out, *refs = refs
    else:
        in_final, select_final, *refs = refs
        finals, refs = refs[: len(cuts)], refs[len(cuts) :]
        g_out, small_out, select_out, *refs = refs
    g_box, small_box, select_box, g_stage, *sems = refs
    (a_send, a_recv, s_send, s_recv, c_send, c_recv, z_send, z_recv, y_send, y_recv) = sems[:10]
    f_send, f_recv, h_send, h_recv, e_send, e_recv = sems[10:]
    shares, peers = g_ref.shape[0], g_ref.shape[1]
    me, item = lax.axis_index("seq"), lax.axis_index("item")
    greet((("seq", me, shares), ("item", item, peers)))

    def other(t):
        return lax.rem(item + t, peers)

    def origin(t):
        return lax.rem(item - t + peers, peers)

    def ahead(k):
        return lax.rem(me + k, shares)

    def behind(k):
        return lax.rem(me - k + shares, shares)

    def flat(k, t):
        return k * (peers - 1) + t - 1

    def share_small(t):
        return remote(
            small_ref.at[other(t)], small_box.at[t - 1], s_send, s_recv, t - 1, "item", other(t)
        )

    def share_select(t):
        return remote(
            select_ref.at[other(t)], select_box.at[t - 1], c_send, c_recv, t - 1, "item", other(t)
        )

    def share_in(k, t):
        p = ahead(k)
        return remote(
            g_ref.at[p, other(t)], g_box.at[t - 1, p], a_send, a_recv, flat(k, t), "item", other(t)
        )

    each(1, peers, lambda t: share_small(t).start())
    each(1, shares, lambda k: each(1, peers, lambda t: share_in(k, t).start()))
    each(1, peers, lambda t: share_in(0, t).start())
    each(1, peers, lambda t: share_select(t).start())

    def add_small(t, total):
        share_small(t).wait_recv()
        return total + small_box[t - 1].astype(f32)

    small_out[item, me] = lax.fori_loop(
        1, peers, add_small, small_ref[item].astype(f32)
    ).astype(bf16)

    def spread_small(k):
        block = small_out.at[item, me]
        return remote(block, block, y_send, y_recv, k, "seq", ahead(k))

    each(1, shares, lambda k: spread_small(k).start())

    def sum_in(k):
        p = ahead(k)

        def add(t, total):
            share_in(k, t).wait_recv()
            return total + g_box[t - 1, p].astype(f32)

        return lax.fori_loop(1, peers, add, g_ref[p, item].astype(f32)).astype(bf16)

    def place_in(k):
        return remote(
            g_stage.at[k], g_out.at[item, me], z_send, z_recv, k, "seq", ahead(k)
        )

    def turn(k):
        g_stage[k] = sum_in(k)
        place_in(k).start()

    each(1, shares, turn)
    g_out[item, me] = sum_in(0)

    def forward_in(k, t):
        block = g_out.at[item, behind(k)]
        return remote(block, block, f_send, f_recv, flat(k, t), "item", other(t))

    def forward_small(k, t):
        block = small_out.at[item, behind(k)]
        return remote(block, block, h_send, h_recv, flat(k, t), "item", other(t))

    each(1, peers, lambda t: forward_in(0, t).start())
    each(1, peers, lambda t: forward_small(0, t).start())

    def add_select(t, total):
        share_select(t).wait_recv()
        return total + select_box[t - 1].astype(f32)

    select_out[item] = lax.fori_loop(
        1, peers, add_select, select_ref[item].astype(f32)
    ).astype(bf16)

    def forward_select(t):
        block = select_out.at[item]
        return remote(block, block, e_send, e_recv, t - 1, "item", other(t))

    each(1, peers, lambda t: forward_select(t).start())

    def pass_on(k):
        block = g_out.at[item, behind(k)]
        remote(block, block, z_send, z_recv, k, "seq", behind(k)).wait_recv()
        each(1, peers, lambda t: forward_in(k, t).start())
        little = small_out.at[item, behind(k)]
        remote(little, little, y_send, y_recv, k, "seq", behind(k)).wait_recv()
        each(1, peers, lambda t: forward_small(k, t).start())

    each(1, shares, pass_on)

    def widen_in(j, s):
        if cuts is None:
            return
        rows, mine = g_ref.shape[2], g_ref.shape[3] // 2
        inner = in_final.shape[1] // 2
        block = g_out[j, s].astype(f32)
        place = pl.ds(pl.multiple_of(j * rows, rows), rows)
        for half in range(2):
            first = pl.multiple_of(s * mine + half * inner, lanes)
            in_final[place, pl.ds(first, mine)] = block[:, half * mine : (half + 1) * mine]

    each(0, shares, lambda k: widen_in(item, behind(k)))

    def finish(k):
        def one(t):
            block = g_out.at[origin(t), behind(k)]
            remote(block, block, f_send, f_recv, flat(k, t), "item", other(t)).wait_recv()
            little = small_out.at[origin(t), behind(k)]
            remote(little, little, h_send, h_recv, flat(k, t), "item", other(t)).wait_recv()
            widen_in(origin(t), behind(k))
            forward_in(k, t).wait_send()
            forward_small(k, t).wait_send()
            share_in(k, t).wait_send()

        each(1, peers, one)

    each(0, shares, finish)

    def finish_item(t):
        block = select_out.at[origin(t)]
        remote(block, block, e_send, e_recv, t - 1, "item", other(t)).wait_recv()
        forward_select(t).wait_send()
        share_small(t).wait_send()
        share_select(t).wait_send()

    each(1, peers, finish_item)

    def finish_seq(k):
        spread_small(k).wait_send()
        place_in(k).wait_send()

    each(1, shares, finish_seq)
    if cuts is None:
        return
    for j in range(peers):
        rows = select_ref.shape[1]
        select_final[j * rows : (j + 1) * rows] = select_out[j].astype(f32)
    inner = in_final.shape[1] // 2
    mine, share = small_ref.shape[2] // 2, small_ref.shape[1]
    for s in range(shares):
        whole = jnp.concatenate([small_out[j, s].astype(f32) for j in range(peers)], axis=0)
        for half in range(2):
            columns = slice(half * inner + s * mine, half * inner + (s + 1) * mine)
            first = 0
            for cut, final in zip(cuts, finals):
                final[:, columns] = whole[first : first + cut, half * mine : (half + 1) * mine]
                first += cut


def weight_sums(g, small, select, cuts):
    shares, peers = g.shape[:2]
    vmem = pl.BlockSpec(memory_space=pltpu.VMEM)
    dma = pltpu.SemaphoreType.DMA
    some = peers - 1
    sizes = [shares * some] * 2 + [some] * 4 + [shares] * 4 + [shares * some] * 4 + [some] * 2
    kept = [
        ((peers, shares) + g.shape[2:], bf16),
        ((peers, shares) + small.shape[1:], bf16),
        (select.shape, bf16),
    ]
    inner2 = shares * g.shape[3]
    direct = (g.shape[3] // 2) % lanes == 0
    outs = kept
    if direct:
        outs = [((peers * g.shape[2], inner2), f32), ((peers * select.shape[1], select.shape[2]), f32)]
        outs += [((cut, inner2), f32) for cut in cuts]
    return pl.pallas_call(
        functools.partial(tail_kernel, cuts if direct else None),
        in_specs=[vmem] * 3,
        out_specs=[vmem] * len(outs),
        out_shape=[jax.ShapeDtypeStruct(shape, kind) for shape, kind in outs],
        scratch_shapes=[pltpu.VMEM(shape, kind) for shape, kind in kept if direct]
        + [
            pltpu.VMEM((some, shares) + g.shape[2:], bf16),
            pltpu.VMEM((some,) + small.shape[1:], bf16),
            pltpu.VMEM((some,) + select.shape[1:], bf16),
            pltpu.VMEM((shares,) + g.shape[2:], bf16),
        ]
        + [dma((size,)) for size in sizes],
        compiler_params=pltpu.CompilerParams(
            collective_id=2, has_side_effects=True, vmem_limit_bytes=40 * 2**20
        ),
        cost_estimate=pl.CostEstimate(flops=60 * 10**9, bytes_accessed=2**20, transcendentals=0),
        name="weight_sums",
    )(g, small, select)


def modulation_kernel(v_ref, out_ref, parts, m_send, m_recv, f_send, f_recv):
    shares = parts.shape[0] + 1
    peers = out_ref.shape[0]
    me, item = lax.axis_index("seq"), lax.axis_index("item")
    greet((("seq", me, shares), ("item", item, peers)))

    def part(k):
        return remote(v_ref, parts.at[k - 1], m_send, m_recv, k - 1, "seq", lax.rem(me + k, shares))

    each(1, shares, lambda k: part(k).start())

    def add(k, total):
        part(k).wait_recv()
        return total + parts[k - 1]

    out_ref[item] = lax.fori_loop(1, shares, add, v_ref[...])

    def forward(t):
        block = out_ref.at[item]
        return remote(block, block, f_send, f_recv, t - 1, "item", lax.rem(item + t, peers))

    each(1, peers, lambda t: forward(t).start())

    def finish(t):
        source = lax.rem(item - t + peers, peers)
        block = out_ref.at[source]
        remote(block, block, f_send, f_recv, t - 1, "item", source).wait_recv()
        forward(t).wait_send()

    each(1, peers, finish)
    each(1, shares, lambda k: part(k).wait_send())


def modulation_sums(v):
    shares, peers = lax.axis_size("seq"), lax.axis_size("item")
    vmem = pl.BlockSpec(memory_space=pltpu.VMEM)
    dma = pltpu.SemaphoreType.DMA
    return pl.pallas_call(
        modulation_kernel,
        in_specs=[vmem],
        out_specs=vmem,
        out_shape=jax.ShapeDtypeStruct((peers,) + v.shape, f32),
        scratch_shapes=[
            pltpu.VMEM((shares - 1,) + v.shape, f32),
            dma((shares,)),
            dma((shares,)),
            dma((peers,)),
            dma((peers,)),
        ],
        compiler_params=pltpu.CompilerParams(collective_id=3, has_side_effects=True),
        cost_estimate=pl.CostEstimate(flops=10 * 10**9, bytes_accessed=2**20, transcendentals=0),
        name="modulation_sums",
    )(v)


def filter_windows(x, taps, reverse):
    rim = taps - 1
    length = x.shape[1]
    padded = jnp.pad(x, ((0, 0), (rim, rim), (0, 0)))
    starts = [2 * rim - j if reverse else j for j in range(taps)]
    return [padded[:, s : s + length] for s in starts]


def per_device(
    tokens,
    timestep,
    slot_item,
    slot_valid,
    cotangent,
    in_weight,
    out_weight,
    select_weight,
    modulation_weight,
    delta_weight,
    filter_weight,
    filter_bias,
    delta_bias,
    decay_log,
    skip_gain,
    modulation_bias,
):
    slots, local, model = tokens.shape
    shares = lax.axis_size("seq")
    place = lax.axis_index("seq")
    rank, inner = delta_weight.shape[0], delta_weight.shape[1] // 2
    states = decay_log.shape[0]
    select = select_weight.shape[1] // 2
    taps = filter_weight.shape[0]
    rim = taps - 1
    length = local * shares
    rows = slots * length
    mine = inner // shares
    padded_width = -(-mine // lanes) * lanes
    shard_rows = modulation_weight.shape[0]
    items = timestep.shape[0]

    def own_columns(v):
        split = v.reshape(v.shape[:-1] + (2, shares, mine))
        return lax.dynamic_index_in_dim(split, place, split.ndim - 2, False)

    first_slot = lax.axis_index("item") * slots
    valid = lax.dynamic_slice_in_dim(slot_valid, first_slot, slots).astype(f32)[:, None, None]
    chooser = (slot_item[:, None] == jnp.arange(items, dtype=jnp.int32)[None, :]).astype(bf16)
    embedded = jnp.dot(chooser, timestep, preferred_element_type=f32)
    condition = jax.nn.silu(embedded).astype(bf16)
    own_features = lax.dynamic_slice_in_dim(condition, place * shard_rows, shard_rows, 1)
    own_condition = lax.dynamic_slice_in_dim(own_features, first_slot, slots, 0)
    modulation_part = jnp.dot(own_condition, modulation_weight, preferred_element_type=f32)
    peers = lax.axis_size("item")
    share_rows = in_weight.shape[0] // peers
    own_rows = lax.dynamic_slice_in_dim(
        in_weight, lax.axis_index("item") * share_rows, share_rows, 0
    )
    own_rows = jnp.moveaxis(own_rows.reshape(share_rows, 2, shares, mine), 2, 0)
    own_in, modulation = input_columns(
        own_rows.reshape(shares, share_rows, 2 * mine), modulation_part
    )
    own_in = own_in.reshape(model, 2 * mine)
    modulation = modulation + modulation_bias.astype(f32)[None, :]
    shift = modulation[:, None, :model]
    scale = modulation[:, None, model : 2 * model]
    gate = modulation[:, None, 2 * model :]

    all_tokens = lax.all_gather(tokens, "seq", axis=1, tiled=True)
    source = all_tokens.astype(f32)
    centered = source - jnp.mean(source, axis=-1, keepdims=True)
    spread = lax.rsqrt(jnp.mean(centered * centered, axis=-1, keepdims=True) + epsilon)
    mixed_in = (centered * spread * (1.0 + scale) + shift).astype(bf16).reshape(rows, model)
    projected = jnp.dot(mixed_in, own_in, preferred_element_type=f32).reshape(
        slots, length, 2 * mine
    )
    x_half = projected[..., :mine].astype(bf16)
    gate_half = projected[..., mine:]

    tap_weight = own_columns(filter_weight).astype(f32)
    tap_bias = own_columns(filter_bias).astype(f32)
    step_weight = own_columns(delta_weight)
    step_bias = own_columns(delta_bias)
    rate = -jnp.exp(own_columns(decay_log))
    skip = own_columns(skip_gain)

    filtered, activated, partial = [], [], []
    for d in range(2):
        f = tap_bias[d]
        for j, window in enumerate(filter_windows(x_half, taps, d == 1)):
            f = f + tap_weight[j, d] * window.astype(f32)
        a = jax.nn.silu(f).astype(bf16)
        filtered.append(f)
        activated.append(a)
        partial.append(
            jnp.dot(
                a.reshape(rows, mine),
                select_weight[:, d * select : (d + 1) * select],
                preferred_element_type=f32,
            )
        )
    selection = summed_everywhere(
        jnp.stack(partial).astype(bf16).reshape(2 * slots, length, select), 4
    ).reshape(2, rows, select)
    selection, late_cotangent = lax.optimization_barrier((selection, cotangent))
    all_cotangent = lax.all_gather(late_cotangent, "seq", axis=1, tiled=True)
    delta_rank = selection[:, :, :rank]
    selection = selection.reshape(2, slots, length, select)
    copies = coefficient_copies(select, rank, states)
    wide_active = widen(jnp.stack(activated), padded_width)
    wide_rate = widen(jnp.swapaxes(rate, 0, 1) * log2e, padded_width)
    wide_weight = widen(
        jnp.pad(jnp.swapaxes(step_weight, 0, 1), ((0, 0), (0, select - rank), (0, 0))),
        padded_width,
    )
    wide_bias = widen(step_bias[:, None, :], padded_width)
    wide_skip = widen(skip[:, None, :], padded_width)
    scanned, hidden, step = scan_states(
        selection, wide_active, wide_weight, wide_bias, wide_rate, copies
    )
    scanned = scanned[..., :mine]
    scanned_sum = scanned[0] + scanned[1]
    for d in range(2):
        scanned_sum = scanned_sum + skip[d] * activated[d].astype(f32)
    silu_gate = jax.nn.silu(gate_half)
    mixed_out = (scanned_sum * silu_gate).astype(bf16).reshape(rows, mine)
    own_cotangent = cotangent.astype(f32)

    grad_branch = (
        (valid * gate * all_cotangent.astype(f32)).astype(bf16).reshape(rows, model)
    )
    grad_mixed = dot_cols(grad_branch, out_weight).reshape(slots, length, mine)
    grad_scanned = grad_mixed * silu_gate
    grad_gate_half = grad_mixed * scanned_sum * silu_slope(gate_half)
    grad_out = dot_rows(mixed_out, grad_branch).astype(bf16)
    branch_part = (
        jnp.dot(mixed_out, out_weight, preferred_element_type=f32)
        .astype(bf16)
        .reshape(slots, length, model)
    )
    branch_part, grad_out, scan_grad = lax.optimization_barrier(
        (branch_part, grad_out, grad_scanned)
    )
    branch_part = lax.psum_scatter(branch_part, "seq", scatter_dimension=1, tiled=True)
    grad_low, grad_input, grad_parts, grad_rate, grad_sums = scan_adjoint(
        selection,
        wide_active,
        wide_weight,
        wide_rate,
        copies,
        wide_skip,
        step,
        widen(scan_grad, padded_width),
        hidden,
    )
    grad_decay = jnp.sum(grad_rate, axis=1)[..., :mine] * ln2
    grad_step_bias = jnp.sum(grad_sums[:, :8, :mine], axis=1)
    grad_skip = jnp.sum(grad_sums[:, 8:, :mine], axis=1)
    grad_parts, grad_out, branch_part = lax.optimization_barrier(
        (grad_parts, grad_out, branch_part)
    )
    grad_out = lax.psum_scatter(grad_out, "item", scatter_dimension=0, tiled=True)
    grad_out = lax.all_gather(grad_out, "item", axis=0, tiled=True)
    grad_selection = summed_everywhere(
        grad_parts.reshape(2 * slots, length, select), 5
    ).reshape(2, rows, select)
    grad_delta = [
        dot_rows(delta_rank[d], grad_low[d, ..., :mine].reshape(rows, mine)) for d in range(2)
    ]
    grad_x = jnp.zeros((slots, length, mine), f32)
    grad_select, grad_taps, grad_tap_bias = [], [], []
    for d in range(2):
        block = select_weight[:, d * select : (d + 1) * select]
        grad_select.append(dot_rows(activated[d].reshape(rows, mine), grad_selection[d]))
        grad_active = (
            grad_input[d, ..., :mine]
            + dot_cols(grad_selection[d], block).reshape(slots, length, mine)
        )
        grad_filtered = grad_active * silu_slope(filtered[d])
        grad_tap_bias.append(jnp.sum(grad_filtered, axis=(0, 1)))
        windows = filter_windows(x_half, taps, d == 1)
        grad_taps.append(
            jnp.stack([jnp.sum(grad_filtered * w.astype(f32), axis=(0, 1)) for w in windows])
        )
        for j, window in enumerate(filter_windows(grad_filtered, taps, d == 0)):
            grad_x = grad_x + tap_weight[j, d] * window
    grad_projected = (
        jnp.concatenate([grad_x, grad_gate_half], axis=2).astype(bf16).reshape(rows, 2 * mine)
    )
    grad_mixed_in = lax.psum_scatter(
        dot_cols(grad_projected, own_in).astype(bf16).reshape(slots, length, model),
        "seq",
        scatter_dimension=1,
        tiled=True,
    ).astype(f32)
    grad_in = dot_rows(mixed_in, grad_projected).astype(bf16)
    own_source = tokens.astype(f32)
    own_centered = own_source - jnp.mean(own_source, axis=-1, keepdims=True)
    own_spread = lax.rsqrt(
        jnp.mean(own_centered * own_centered, axis=-1, keepdims=True) + epsilon
    )
    normed = own_centered * own_spread
    grad_normed = grad_mixed_in * (1.0 + scale)
    grad_source = own_spread * (
        grad_normed
        - jnp.mean(grad_normed, axis=-1, keepdims=True)
        - normed * jnp.mean(grad_normed * normed, axis=-1, keepdims=True)
    )
    grad_tokens = (own_cotangent + grad_source).astype(bf16)
    branch = branch_part.astype(f32)
    output = (tokens.astype(f32) + valid * gate * branch).astype(bf16)
    grad_gate = jnp.sum(valid * own_cotangent * branch, axis=1)
    grad_modulation = jnp.concatenate(
        [jnp.sum(grad_mixed_in, axis=1), jnp.sum(grad_mixed_in * normed, axis=1), grad_gate], axis=1
    )
    grad_modulation = modulation_sums(grad_modulation).reshape(-1, 3 * model)
    grad_modulation_weight = lax.dot_general(
        own_features.astype(f32),
        grad_modulation,
        (((0,), (0,)), ((), ())),
        precision=lax.Precision.HIGHEST,
        preferred_element_type=f32,
    )
    small = jnp.concatenate(
        [
            jnp.stack(grad_delta, 1),
            jnp.swapaxes(grad_decay, 0, 1),
            jnp.stack(grad_taps, 1),
            jnp.stack(grad_tap_bias)[None],
            grad_step_bias[None],
            grad_skip[None],
        ],
        axis=0,
    )
    small_rows = small.shape[0]
    share = -(-small_rows // (16 * peers)) * 16
    small = jnp.pad(
        small.astype(bf16).reshape(small_rows, 2 * mine), ((0, peers * share - small_rows), (0, 0))
    )
    grad_select = jnp.concatenate(grad_select, axis=1).astype(bf16)
    cuts = [rank, states, taps, 1, 1, 1]
    results = weight_sums(
        grad_in.reshape(shares, peers, share_rows, 2 * mine),
        small.reshape(peers, share, 2 * mine),
        grad_select.reshape(peers, mine // peers, 2 * select),
        cuts,
    )
    if mine % lanes == 0:
        grad_in, grad_select, *small = results
    else:
        grad_in, small, grad_select = results
        grad_in = grad_in.reshape(peers, shares, share_rows, 2, mine)
        grad_in = jnp.transpose(grad_in, (0, 2, 3, 1, 4)).reshape(peers * share_rows, 2 * inner)
        grad_in = grad_in.astype(f32)
        small = small.reshape(peers, shares, share, 2, mine)
        small = jnp.transpose(small, (0, 2, 3, 1, 4)).reshape(peers * share, 2 * inner).astype(f32)
        ends = [sum(cuts[: i + 1]) for i in range(len(cuts))]
        small = [small[end - cut : end] for cut, end in zip(cuts, ends)]
        grad_select = grad_select.reshape(mine, 2 * select).astype(f32)
    return (
        output,
        grad_tokens,
        grad_in,
        grad_out.astype(f32),
        grad_select,
        grad_modulation_weight,
        small[0],
        small[2],
        small[3].reshape(-1),
        small[4].reshape(-1),
        small[1],
        small[5].reshape(-1),
        jnp.sum(grad_modulation, axis=0),
    )


def solution(mesh):
    tokens, rows, same = P("item", "seq", None), P("seq", None), P()
    return jax.shard_map(
        per_device,
        mesh=mesh,
        in_specs=(tokens, same, same, same, tokens, rows, rows, rows, rows) + (same,) * 7,
        out_specs=(tokens, tokens, rows, rows, rows, rows) + (same,) * 7,
        check_vma=False,
    )
```

```python
import functools
import math

import jax
import jax.numpy as jnp
from jax import lax
from jax.experimental import pallas as pl
from jax.experimental.pallas import tpu as pltpu
from jax.sharding import PartitionSpec as P

epsilon = 1e-06
log2e = 1.4426950408889634
ln2 = 0.6931471805599453
chunk = 16
lanes = 128
f32 = jnp.float32
bf16 = jnp.bfloat16


def silu_slope(v):
    s = jax.nn.sigmoid(v)
    return s * (1.0 + v * (1.0 - s))


def dot_rows(a, b):
    return lax.dot_general(a, b, (((0,), (0,)), ((), ())), preferred_element_type=f32)


def dot_cols(a, b):
    return lax.dot_general(a, b, (((1,), (1,)), ((), ())), preferred_element_type=f32)


def fold_sublanes(parts):
    outs = []
    for first in range(0, len(parts), 8):
        cur = parts[first : first + 8]
        row = lax.broadcasted_iota(jnp.int32, cur[0].shape, 0)
        for hop in (4, 2, 1):
            keep = (row // hop) % 2 == 0
            half = len(cur) // 2
            merged = []
            for j in range(half):
                a, b = cur[j], cur[j + half]
                x, y = jnp.where(keep, a, b), jnp.where(keep, b, a)
                if hop == 4:
                    moved = pltpu.roll(y, 4, 0)
                else:
                    moved = jnp.where(keep, pltpu.roll(y, 8 - hop, 0), pltpu.roll(y, hop, 0))
                merged.append(x + moved)
            cur = merged
        outs.append(cur[0])
    return jnp.concatenate(outs, axis=0)


def wide(v, groups):
    return v if groups == 1 else jnp.concatenate([v] * groups, axis=1)


def spread_matrix():
    rows = lax.broadcasted_iota(jnp.int32, (2 * chunk, 2 * lanes), 0) // chunk
    cols = lax.broadcasted_iota(jnp.int32, (2 * chunk, 2 * lanes), 1) // lanes
    return (rows == cols).astype(f32).astype(bf16)


def chunk_sweep(count, body, spread, first, second):
    spread(0, first)
    if count == 1:
        body(0, first)
        return

    def pair(k, carry):
        spread(2 * k + 1, second)
        body(2 * k, first)
        spread(jnp.minimum(2 * k + 2, count - 1), first)
        body(2 * k + 1, second)
        return carry

    lax.fori_loop(0, count // 2, pair, 0)


def place_coefficients(selection, copies):
    placed = jnp.dot(selection, copies, preferred_element_type=f32)
    row = lax.rem(lax.broadcasted_iota(jnp.int32, placed.shape, 0), chunk)
    span = placed.shape[1] // 2
    col = lax.rem(lax.broadcasted_iota(jnp.int32, placed.shape, 1), span) // (span // chunk)
    return jnp.where(row == col, placed, 0.0).astype(bf16)


def softplus(v):
    return jnp.maximum(v, 0.0) + jnp.log1p(jnp.exp(-jnp.abs(v)))


def states_kernel(
    count,
    sel_ref,
    x_ref,
    w_ref,
    bias_ref,
    r_ref,
    copies_ref,
    y_ref,
    h_ref,
    dt_ref,
    state,
    bc,
    even,
    odd,
):
    slots, width = dt_ref.shape[1], dt_ref.shape[3]
    groups = width // lanes
    states = r_ref.shape[1]

    @pl.when(pl.program_id(1) == 0)
    def _():
        state[...] = jnp.zeros_like(state)

    for s in range(slots):
        selection = sel_ref[0, s]
        dt_ref[0, s] = softplus(
            jnp.dot(selection, w_ref[0], preferred_element_type=f32) + bias_ref[0]
        )
        bc[s] = place_coefficients(selection, copies_ref[...])

    def one_direction(reverse):
        mix = spread_matrix()

        def place(i):
            return (count - 1 - i) if reverse else i

        def spread(i, into):
            start = pl.multiple_of(place(i) * chunk, chunk)
            for s in range(slots):
                both = bc[s, pl.ds(start, chunk), :]
                span = both.shape[1] // 2
                into[s] = dot_rows(jnp.concatenate([both[:, :span], both[:, span:]], axis=0), mix)

        def body(i, held):
            start = pl.multiple_of(place(i) * chunk, chunk)
            order = range(chunk - 1, -1, -1) if reverse else range(chunk)
            for s in range(slots):
                h = state[s]
                rate = r_ref[0]
                dt = dt_ref[0, s, pl.ds(start, chunk), :]
                u = dt * x_ref[0, s, pl.ds(start, chunk), :].astype(f32)
                kept, sums = [None] * chunk, [None] * chunk
                for t in order:
                    rows = slice(t * states, (t + 1) * states)
                    b = wide(held[s, rows, :lanes], groups)
                    c = wide(held[s, rows, lanes:], groups)
                    h = jnp.exp2(dt[t : t + 1] * rate) * h + u[t : t + 1] * b
                    kept[t] = h.astype(bf16)
                    p = h * c
                    sums[t] = p[:8] + p[8:]
                size = chunk * states
                h_ref[0, s, pl.ds(pl.multiple_of(start * states, size), size), :] = jnp.concatenate(
                    kept, axis=0
                )
                y_ref[0, s, pl.ds(start, chunk), :] = fold_sublanes(sums)
                state[s] = h

        chunk_sweep(count, body, spread, even, odd)

    for d in range(2):

        @pl.when(pl.program_id(0) == d)
        def _():
            one_direction(d == 1)


def side_exchange(b_ref, q_ref, b_out, q_out, b_box, q_box, q_stage, *sems):
    b_keep, q_keep, o_keep, p_keep = sems[:4]
    (i_send, i_recv, j_send, j_recv, a_send, a_recv, z_send, z_recv, f_send, f_recv) = sems[4:]
    shares, peers = q_ref.shape[0], q_ref.shape[1]
    me, item = lax.axis_index("seq"), lax.axis_index("item")
    step = pl.program_id(0) * pl.num_programs(1) + pl.program_id(1)
    quarter = pl.num_programs(0) * pl.num_programs(1) // 4

    def other(t):
        return lax.rem(item + t, peers)

    def origin(t):
        return lax.rem(item - t + peers, peers)

    def ahead(k):
        return lax.rem(me + k, shares)

    def behind(k):
        return lax.rem(me - k + shares, shares)

    def own_b():
        return pltpu.make_async_copy(b_ref.at[item], b_box.at[0], b_keep)

    def own_q():
        return pltpu.make_async_copy(q_ref.at[:, item], q_box.at[0], q_keep)

    def share_b(t):
        return remote(b_ref.at[other(t)], b_box.at[t], i_send, i_recv, t - 1, "item", other(t))

    def share_q(t):
        return remote(q_ref.at[:, other(t)], q_box.at[t], a_send, a_recv, t - 1, "item", other(t))

    def keep_b():
        return pltpu.make_async_copy(b_box.at[0], b_out.at[item], o_keep)

    def keep_q():
        return pltpu.make_async_copy(q_stage.at[me], q_out.at[item, me], p_keep)

    def give_b(t):
        return remote(b_box.at[0], b_out.at[item], j_send, j_recv, t - 1, "item", other(t))

    def place_q(k):
        return remote(
            q_stage.at[ahead(k)], q_out.at[item, me], z_send, z_recv, k, "seq", ahead(k)
        )

    def forward_q(k, t):
        source = q_stage.at[me] if isinstance(k, int) else q_out.at[item, behind(k)]
        return remote(
            source,
            q_out.at[item, behind(k)],
            f_send,
            f_recv,
            k * (peers - 1) + t - 1,
            "item",
            other(t),
        )

    @pl.when(step == 0)
    def _():
        greet((("seq", me, shares), ("item", item, peers)))
        each(1, peers, lambda t: share_q(t).start())
        each(1, peers, lambda t: share_b(t).start())
        own_b().start()
        own_q().start()

    @pl.when(step == quarter)
    def _():
        own_q().wait()
        own_b().wait()

        def arrived(t):
            share_q(t).wait_recv()
            share_b(t).wait_recv()

        each(1, peers, arrived)

        def sum_q(p):
            def add(t, total):
                return total + q_box[t, p].astype(f32)

            q_stage[p] = lax.fori_loop(1, peers, add, q_box[0, p].astype(f32)).astype(bf16)

        each(0, shares, sum_q)
        rows = 16 if b_box.shape[1] % 16 == 0 else b_box.shape[1]

        def sum_b(r):
            place = pl.ds(pl.multiple_of(r * rows, rows), rows)

            def add(t, total):
                return total + b_box[t, place, :].astype(f32)

            total = lax.fori_loop(1, peers, add, b_box[0, place, :].astype(f32))
            b_box[0, place, :] = total.astype(bf16)

        each(0, b_box.shape[1] // rows, sum_b)
        each(1, shares, lambda k: place_q(k).start())
        each(1, peers, lambda t: forward_q(0, t).start())
        each(1, peers, lambda t: give_b(t).start())
        keep_b().start()
        keep_q().start()

    @pl.when(step == 2 * quarter)
    def _():
        def pass_on(k):
            block = q_out.at[item, behind(k)]
            remote(block, block, z_send, z_recv, k, "seq", behind(k)).wait_recv()
            each(1, peers, lambda t: forward_q(k, t).start())

        each(1, shares, pass_on)

    @pl.when(step == 3 * quarter)
    def _():
        keep_b().wait()
        keep_q().wait()

        def finish(t):
            block = b_out.at[origin(t)]
            remote(block, block, j_send, j_recv, t - 1, "item", other(t)).wait_recv()
            give_b(t).wait_send()
            share_b(t).wait_send()
            share_q(t).wait_send()

        each(1, peers, finish)

        def finish_q(k):
            def one(t):
                block = q_out.at[origin(t), behind(k)]
                remote(
                    block, block, f_send, f_recv, k * (peers - 1) + t - 1, "item", other(t)
                ).wait_recv()
                forward_q(k, t).wait_send()

            each(1, peers, one)

        each(0, shares, finish_q)
        each(1, shares, lambda k: place_q(k).wait_send())


def adjoint_kernel(
    count,
    sel_ref,
    x_ref,
    w_ref,
    r_ref,
    copies_ref,
    skip_ref,
    dt_ref,
    g_ref,
    h_ref,
    edge_ref,
    b_ref,
    q_ref,
    low_ref,
    input_ref,
    gsel_ref,
    decay_ref,
    sums_ref,
    b_out,
    q_out,
    pending,
    bc,
    coefs,
    even,
    odd,
    *side,
):
    slots, width = dt_ref.shape[1], dt_ref.shape[3]
    groups = width // lanes
    states = r_ref.shape[1]
    last_block = pl.program_id(1) == pl.num_programs(1) - 1

    side_exchange(b_ref, q_ref, b_out, q_out, *side)

    @pl.when(pl.program_id(1) == 0)
    def _():
        pending[...] = jnp.zeros_like(pending)
        decay_ref[...] = jnp.zeros_like(decay_ref)
        sums_ref[...] = jnp.zeros_like(sums_ref)

    for s in range(slots):
        bc[s] = place_coefficients(sel_ref[0, s], copies_ref[...])

    def one_direction(reverse):
        mix = spread_matrix()
        picks = (
            lax.broadcasted_iota(jnp.int32, (8, 2 * lanes), 0)
            == lax.broadcasted_iota(jnp.int32, (8, 2 * lanes), 1) // lanes
        ).astype(f32).astype(bf16)

        def place(i):
            return i if reverse else (count - 1 - i)

        def spread(i, into):
            start = pl.multiple_of(place(i) * chunk, chunk)
            for s in range(slots):
                both = bc[s, pl.ds(start, chunk), :]
                span = both.shape[1] // 2
                into[s] = dot_rows(jnp.concatenate([both[:, :span], both[:, span:]], axis=0), mix)

        def body(i, held):
            here = place(i)
            start = pl.multiple_of(here * chunk, chunk)
            order = range(chunk) if reverse else range(chunk - 1, -1, -1)
            size = chunk * states
            base = pl.multiple_of(start * states, size)
            at_end = here == (count - 1 if reverse else 0)
            outer = jnp.where(last_block, 0.0, 1.0)
            near = pl.multiple_of(
                jnp.clip(start + (chunk if reverse else -1), 0, count * chunk - 1) * states, states
            )
            for s in range(slots):
                pend = pending[s]
                rate = r_ref[0]
                dt = dt_ref[0, s, pl.ds(start, chunk), :]
                x = x_ref[0, s, pl.ds(start, chunk), :].astype(f32)
                g = g_ref[s, pl.ds(start, chunk), :].astype(f32)
                u = dt * x
                before = jnp.where(
                    at_end,
                    edge_ref[0, s].astype(f32) * outer,
                    h_ref[0, s, pl.ds(near, states), :].astype(f32),
                )
                total = decay_ref[0, s]
                rate_sums, into_sums = [None] * chunk, [None] * chunk
                coef = [None] * chunk
                hidden = h_ref[0, s, pl.ds(base, size), :]
                now = hidden[order[0] * states : (order[0] + 1) * states].astype(f32)
                for k, t in enumerate(order):
                    rows = slice(t * states, (t + 1) * states)
                    b = wide(held[s, rows, :lanes], groups)
                    c = wide(held[s, rows, lanes:], groups)
                    if k + 1 < chunk:
                        q = order[k + 1]
                        prev = hidden[q * states : (q + 1) * states].astype(f32)
                    else:
                        prev = before
                    gt = g[t : t + 1]
                    adj = c * gt + pend
                    pend = jnp.exp2(dt[t : t + 1] * rate) * adj
                    through = pend * prev * rate
                    total = total + through * dt[t : t + 1]
                    rate_sums[t] = through[:8] + through[8:]
                    w = adj * b
                    into_sums[t] = w[:8] + w[8:]
                    cb, cc = adj * u[t : t + 1], now * gt
                    sb, sc = cb[:, :lanes], cc[:, :lanes]
                    for j in range(1, groups):
                        sb = sb + cb[:, j * lanes : (j + 1) * lanes]
                        sc = sc + cc[:, j * lanes : (j + 1) * lanes]
                    coef[t] = jnp.concatenate([sb, sc], axis=1).astype(bf16)
                    now = prev
                pending[s] = pend
                decay_ref[0, s] = total
                weighted = fold_sublanes(into_sums)
                few = dt * (1.0 - dt * (0.5 - dt * (1.0 / 6.0 - dt * (1.0 / 24.0))))
                slope = jnp.where(dt < 0.03, few, 1.0 - jnp.exp(-dt))
                grad_pre = (fold_sublanes(rate_sums) * ln2 + weighted * x) * slope
                low_ref[0, s, pl.ds(start, chunk), :] = grad_pre.astype(bf16)
                input_ref[0, s, pl.ds(start, chunk), :] = weighted * dt + skip_ref[0] * g
                gx = g * x
                sums_ref[0] += jnp.concatenate(
                    [grad_pre[:8] + grad_pre[8:], gx[:8] + gx[8:]], axis=0
                )
                coefs[s, pl.ds(pl.multiple_of(here * 8, 8), 8), :] = dot_cols(
                    picks, jnp.concatenate(coef, axis=0)
                )

        chunk_sweep(count, body, spread, even, odd)

    for d in range(2):

        @pl.when(pl.program_id(0) == d)
        def _():
            one_direction(d == 1)


    own = lax.broadcasted_iota(jnp.int32, (chunk, chunk * states), 0) == (
        lax.broadcasted_iota(jnp.int32, (chunk, chunk * states), 1) // states
    )
    for s in range(slots):
        placed = []
        for c in range(count):
            placed.append(
                jnp.concatenate(
                    [
                        jnp.where(own, coefs[s, c * 8 + k : c * 8 + k + 1, :], 0.0)
                        for k in range(2)
                    ],
                    axis=1,
                )
            )
        placed = jnp.concatenate(placed, axis=0).astype(bf16)
        gsel_ref[0, s] = (
            dot_cols(low_ref[0, s], w_ref[0]) + dot_cols(placed, copies_ref[...])
        ).astype(bf16)


def block_of(length):
    return math.gcd(length, 128)


def scan_states(selection, x, weight, bias, rate, copies):
    two, slots, length, width = x.shape
    select = selection.shape[3]
    states = rate.shape[1]
    hidden_size = two * slots * length * states * width
    block = block_of(length)
    blocks = length // block
    spread = copies.shape[1]

    def where(d, i):
        return (d, 0, jnp.where(d == 1, blocks - 1 - i, i), 0)

    def by_direction(d, i):
        return (d, 0, 0)

    return pl.pallas_call(
        functools.partial(states_kernel, block // chunk),
        grid=(two, blocks),
        in_specs=[
            pl.BlockSpec((1, slots, block, select), where),
            pl.BlockSpec((1, slots, block, width), where),
            pl.BlockSpec((1, select, width), by_direction),
            pl.BlockSpec((1, 1, width), by_direction),
            pl.BlockSpec((1, states, width), by_direction),
            pl.BlockSpec((select, spread), lambda d, i: (0, 0)),
        ],
        out_specs=[
            pl.BlockSpec((1, slots, block, width), where),
            pl.BlockSpec((1, slots, block * states, width), where),
            pl.BlockSpec((1, slots, block, width), where),
        ],
        out_shape=[
            jax.ShapeDtypeStruct((two, slots, length, width), f32),
            jax.ShapeDtypeStruct((two, slots, length * states, width), bf16),
            jax.ShapeDtypeStruct((two, slots, length, width), f32),
        ],
        scratch_shapes=[
            pltpu.VMEM((slots, states, width), f32),
            pltpu.VMEM((slots, block, spread), bf16),
            pltpu.VMEM((slots, chunk * states, 2 * lanes), f32),
            pltpu.VMEM((slots, chunk * states, 2 * lanes), f32),
        ],
        compiler_params=pltpu.CompilerParams(vmem_limit_bytes=48 * 2**20),
        cost_estimate=pl.CostEstimate(
            flops=64 * 10**9, bytes_accessed=80 * 2**20, transcendentals=hidden_size
        ),
        name="scan_states",
    )(selection, x, weight, bias, rate, copies)


def scan_adjoint(selection, x, weight, rate, copies, skip, dt, g, h, b, q):
    two, slots, length, width = dt.shape
    select = selection.shape[3]
    states = rate.shape[1]
    hidden_size = two * slots * length * states * width
    block = block_of(length)
    blocks = length // block
    spread = copies.shape[1]
    shares, peers = q.shape[:2]
    anywhere, dma = pl.BlockSpec(memory_space=pl.ANY), pltpu.SemaphoreType.DMA

    def at(d, i):
        return jnp.where(d == 1, i, blocks - 1 - i)

    def where(d, i):
        return (d, 0, at(d, i), 0)

    def edge(d, i):
        mine = at(d, i) * block
        return (d, 0, jnp.clip(jnp.where(d == 1, mine + block, mine - 1), 0, length - 1), 0)

    def by_direction(d, i):
        return (d, 0, 0)

    return pl.pallas_call(
        functools.partial(adjoint_kernel, block // chunk),
        grid=(two, blocks),
        in_specs=[
            pl.BlockSpec((1, slots, block, select), where),
            pl.BlockSpec((1, slots, block, width), where),
            pl.BlockSpec((1, select, width), by_direction),
            pl.BlockSpec((1, states, width), by_direction),
            pl.BlockSpec((select, spread), lambda d, i: (0, 0)),
            pl.BlockSpec((1, 1, width), by_direction),
            pl.BlockSpec((1, slots, block, width), where),
            pl.BlockSpec((slots, block, width), lambda d, i: (0, at(d, i), 0)),
            pl.BlockSpec((1, slots, block * states, width), where),
            pl.BlockSpec((1, slots, states, width), edge),
            anywhere,
            anywhere,
        ],
        out_specs=[
            pl.BlockSpec((1, slots, block, width), where),
            pl.BlockSpec((1, slots, block, width), where),
            pl.BlockSpec((1, slots, block, select), where),
            pl.BlockSpec((1, slots, states, width), lambda d, i: (d, 0, 0, 0)),
            pl.BlockSpec((1, 16, width), by_direction),
            anywhere,
            anywhere,
        ],
        out_shape=[
            jax.ShapeDtypeStruct((two, slots, length, width), bf16),
            jax.ShapeDtypeStruct((two, slots, length, width), f32),
            jax.ShapeDtypeStruct((two, slots, length, select), bf16),
            jax.ShapeDtypeStruct((two, slots, states, width), f32),
            jax.ShapeDtypeStruct((two, 16, width), f32),
            jax.ShapeDtypeStruct(b.shape, bf16),
            jax.ShapeDtypeStruct((peers, shares) + q.shape[2:], bf16),
        ],
        scratch_shapes=[
            pltpu.VMEM((slots, states, width), f32),
            pltpu.VMEM((slots, block, spread), bf16),
            pltpu.VMEM((slots, block // chunk * 8, chunk * states), f32),
            pltpu.VMEM((slots, chunk * states, 2 * lanes), f32),
            pltpu.VMEM((slots, chunk * states, 2 * lanes), f32),
            pltpu.VMEM(b.shape, bf16),
            pltpu.VMEM((peers, shares) + q.shape[2:], bf16),
            pltpu.VMEM((shares,) + q.shape[2:], bf16),
        ]
        + [dma] * 4
        + [dma((peers - 1,))] * 6
        + [dma((shares,))] * 2
        + [dma((shares * (peers - 1),))] * 2,
        compiler_params=pltpu.CompilerParams(
            collective_id=6, has_side_effects=True, vmem_limit_bytes=48 * 2**20
        ),
        cost_estimate=pl.CostEstimate(
            flops=100 * 10**9, bytes_accessed=100 * 2**20, transcendentals=hidden_size
        ),
        name="scan_adjoint",
    )(selection, x, weight, rate, copies, skip, dt, g, h, h, b, q)


def coefficient_copies(width, rank, states):
    span = chunk * states
    col = jnp.arange(2 * span)
    origin = rank + (col // span) * states + col % states
    return (jnp.arange(width)[:, None] == origin[None, :]).astype(bf16)


def widen(v, width):
    short = width - v.shape[-1]
    return v if short == 0 else jnp.pad(v, ((0, 0),) * (v.ndim - 1) + ((0, short),))


def remote(src, dst, sends, recvs, slot, axis, to):
    return pltpu.make_async_remote_copy(
        src_ref=src,
        dst_ref=dst,
        send_sem=sends.at[slot],
        recv_sem=recvs.at[slot],
        device_id={axis: to},
        device_id_type=pl.DeviceIdType.MESH,
    )


def each(first, last, body):
    def run(k, carry):
        body(k)
        return carry

    lax.fori_loop(first, last, run, 0)


def greet(peers):
    barrier = pltpu.get_barrier_semaphore()
    total = 0
    for axis, me, count in peers:

        def hello(k):
            pl.semaphore_signal(
                barrier,
                inc=1,
                device_id={axis: lax.rem(me + k, count)},
                device_id_type=pl.DeviceIdType.MESH,
            )

        each(1, count, hello)
        total += count - 1
    pl.semaphore_wait(barrier, total)


def total_kernel(line, v_ref, o_ref, pairbox, stage, inbox, *sems):
    pair_send, pair_recv, sum_send, sum_recv, out_send, out_recv, fwd_send, fwd_recv = sems
    me = lax.axis_index("seq")
    pos, core = me // 2, lax.rem(me, 2)
    partner = me + 1 - 2 * core
    barrier = pltpu.get_barrier_semaphore()

    def hello(to):
        pl.semaphore_signal(
            barrier, inc=1, device_id={"seq": to}, device_id_type=pl.DeviceIdType.MESH
        )

    hello(partner)
    each(1, line, lambda k: hello(lax.rem(pos + k, line) * 2 + core))
    pl.semaphore_wait(barrier, line)

    pair = remote(v_ref.at[:, :, 1 - core], pairbox, pair_send, pair_recv, 0, "seq", partner)
    pair.start()
    pair.wait_recv()

    def own(q):
        return v_ref[:, q, core].astype(f32) + pairbox[:, q].astype(f32)

    def summand(k):
        q = lax.rem(pos + k, line)
        return remote(
            stage.at[q], inbox.at[pos], sum_send, sum_recv, k - 1, "seq", q * 2 + core
        )

    def send(k):
        q = lax.rem(pos + k, line)
        stage[q] = own(q).astype(bf16)
        summand(k).start()

    each(1, line, send)

    def source(k):
        return lax.rem(pos - k + line, line)

    def arrived(k, total):
        q = source(k)
        remote(stage.at[q], inbox.at[q], sum_send, sum_recv, k - 1, "seq", partner).wait_recv()
        return total + inbox[q].astype(f32)

    total = lax.fori_loop(1, line, arrived, own(pos))
    o_ref[:, pos, core] = total.astype(bf16)

    def result(k):
        mine = o_ref.at[:, pos, core]
        return remote(
            mine, mine, out_send, out_recv, k - 1, "seq", lax.rem(pos + k, line) * 2 + core
        )

    def forward(k):
        block = o_ref.at[:, source(k), core]
        return remote(block, block, fwd_send, fwd_recv, k, "seq", partner)

    each(1, line, lambda k: result(k).start())
    forward(0).start()

    def pass_on(k):
        block = o_ref.at[:, source(k), core]
        remote(block, block, out_send, out_recv, k - 1, "seq", partner).wait_recv()
        forward(k).start()

    each(1, line, pass_on)

    def finish(k):
        block = o_ref.at[:, source(k), 1 - core]
        remote(block, block, fwd_send, fwd_recv, k, "seq", partner).wait_recv()
        forward(k).wait_send()

    each(0, line, finish)
    pair.wait_send()

    def drain(k):
        summand(k).wait_send()
        result(k).wait_send()

    each(1, line, drain)


def summed_everywhere(v, call):
    batch, length, width = v.shape
    shares = lax.axis_size("seq")
    line, rows = shares // 2, length // shares
    vmem = pl.BlockSpec(memory_space=pltpu.VMEM)
    dma = pltpu.SemaphoreType.DMA
    blocks = v.reshape(batch, line, 2, rows, width)
    out = pl.pallas_call(
        functools.partial(total_kernel, line),
        in_specs=[vmem],
        out_specs=vmem,
        out_shape=jax.ShapeDtypeStruct(blocks.shape, bf16),
        scratch_shapes=[
            pltpu.VMEM((batch, line, rows, width), bf16),
            pltpu.VMEM((line, batch, rows, width), bf16),
            pltpu.VMEM((line, batch, rows, width), bf16),
            dma((1,)),
            dma((1,)),
            dma((line,)),
            dma((line,)),
            dma((line,)),
            dma((line,)),
            dma((line,)),
            dma((line,)),
        ],
        compiler_params=pltpu.CompilerParams(
            collective_id=call, has_side_effects=True, vmem_limit_bytes=40 * 2**20
        ),
        cost_estimate=pl.CostEstimate(flops=25 * 10**9, bytes_accessed=2**20, transcendentals=0),
        name="sum_" + str(call),
    )(blocks)
    return out.reshape(v.shape)


def head_kernel(line, t_ref, w_ref, mod_ref, all_ref, box_ref, out_ref, parts, *sems):
    keep, t_keep, u_send, u_recv, d_send, d_recv, p_send, p_recv = sems[:8]
    w_send, w_recv, f_send, f_recv, m_send, m_recv = sems[8:]
    shares, peers = box_ref.shape[0], box_ref.shape[1]
    slots, local = t_ref.shape[0], t_ref.shape[1]
    me, item = lax.axis_index("seq"), lax.axis_index("item")
    pos, core = me // 2, lax.rem(me, 2)
    partner = me + 1 - 2 * core
    greet((("seq", me, shares), ("item", item, peers)))

    def region(q, c, s):
        first = pl.multiple_of((q * 2 + c) * local, local)
        return all_ref.at[s, pl.ds(first, local), :]

    def hop(q, s, source, sends, recvs, k, to):
        return remote(source, region(q, core, s), sends, recvs, k * slots + s, "seq", to)

    def up(k, s):
        source = t_ref.at[s] if isinstance(k, int) else region(pos - k, core, s)
        return hop(pos - k, s, source, u_send, u_recv, k, me + 2)

    def down(k, s):
        source = t_ref.at[s] if isinstance(k, int) else region(pos + k, core, s)
        return hop(pos + k, s, source, d_send, d_recv, k, me - 2)

    def across(q, s):
        return remote(
            region(q, core, s), region(q, core, s), p_send, p_recv, q * slots + s, "seq", partner
        )

    def own_across(s):
        return remote(
            t_ref.at[s], region(pos, core, s), p_send, p_recv, pos * slots + s, "seq", partner
        )

    not_last, not_first = pos < line - 1, pos > 0
    for s in range(slots):

        @pl.when(not_last)
        def _():
            up(0, s).start()

        @pl.when(not_first)
        def _():
            down(0, s).start()

    def modulation(k):
        return remote(
            mod_ref, parts.at[k - 1], m_send, m_recv, k - 1, "seq", lax.rem(me + k, shares)
        )

    def weight(k):
        to = lax.rem(me + k, shares)
        return remote(w_ref.at[to], box_ref.at[me, item], w_send, w_recv, k, "seq", to)

    each(1, shares, lambda k: modulation(k).start())
    each(1, shares, lambda k: weight(k).start())
    own = pltpu.make_async_copy(w_ref.at[me], box_ref.at[me, item], keep)
    own.start()
    kept = []
    for s in range(slots):
        own_across(s).start()
        kept.append(pltpu.make_async_copy(t_ref.at[s], region(pos, core, s), t_keep.at[s]))
        kept[-1].start()

    def forward(k, t):
        block = box_ref.at[lax.rem(me - k + shares, shares), item]
        return remote(
            block, block, f_send, f_recv, k * (peers - 1) + t - 1, "item", lax.rem(item + t, peers)
        )

    def pass_on(k):
        source = lax.rem(me - k + shares, shares)
        block = box_ref.at[source, item]
        remote(block, block, w_send, w_recv, k, "seq", source).wait_recv()
        each(1, peers, lambda t: forward(k, t).start())

    def relay(k):
        for s in range(slots):

            @pl.when(k < pos)
            def _():
                q = pos - 1 - k
                hop(q, s, region(q, core, s), u_send, u_recv, k, partner).wait_recv()

                @pl.when(not_last)
                def _():
                    up(k + 1, s).start()

                across(q, s).start()

            @pl.when(k < line - 1 - pos)
            def _():
                q = pos + 1 + k
                hop(q, s, region(q, core, s), d_send, d_recv, k, partner).wait_recv()

                @pl.when(not_first)
                def _():
                    down(k + 1, s).start()

                across(q, s).start()

    own.wait()
    each(1, peers, lambda t: forward(0, t).start())
    half = shares // 2
    each(1, half, pass_on)
    each(0, 1, relay)
    each(half, shares, pass_on)

    def add(k, total):
        modulation(k).wait_recv()
        return total + parts[k - 1]

    out_ref[...] = lax.fori_loop(1, shares, add, mod_ref[...])
    each(1, line - 1, relay)

    def finish(k):
        def one(t):
            source = lax.rem(item - t + peers, peers)
            block = box_ref.at[lax.rem(me - k + shares, shares), source]
            remote(
                block, block, f_send, f_recv, k * (peers - 1) + t - 1, "item", source
            ).wait_recv()
            forward(k, t).wait_send()

        each(1, peers, one)

    each(0, shares, finish)

    def drain(k):
        weight(k).wait_send()
        modulation(k).wait_send()

    each(1, shares, drain)

    def drain_tokens(q):
        for s in range(slots):
            remote(
                region(q, core, s),
                region(q, 1 - core, s),
                p_send,
                p_recv,
                q * slots + s,
                "seq",
                partner,
            ).wait_recv()
            across(q, s).wait_send()

    each(0, line, drain_tokens)

    def drain_line(k):
        for s in range(slots):

            @pl.when(not_last & (k <= pos))
            def _():
                up(k, s).wait_send()

            @pl.when(not_first & (k <= line - 1 - pos))
            def _():
                down(k, s).wait_send()

    each(0, line, drain_line)
    for copy in kept:
        copy.wait()


def gather_inputs(tokens, blocks, modulation):
    shares, peers = lax.axis_size("seq"), lax.axis_size("item")
    slots, local, model = tokens.shape
    line = shares // 2
    vmem, anywhere = pl.BlockSpec(memory_space=pltpu.VMEM), pl.BlockSpec(memory_space=pl.ANY)
    dma = pltpu.SemaphoreType.DMA
    return pl.pallas_call(
        functools.partial(head_kernel, line),
        in_specs=[anywhere, anywhere, vmem],
        out_specs=[anywhere, anywhere, vmem],
        out_shape=[
            jax.ShapeDtypeStruct((slots, local * shares, model), bf16),
            jax.ShapeDtypeStruct((shares, peers) + blocks.shape[1:], bf16),
            jax.ShapeDtypeStruct(modulation.shape, f32),
        ],
        scratch_shapes=[pltpu.VMEM((shares - 1,) + modulation.shape, f32), dma, dma((slots,))]
        + [dma((line * slots,))] * 6
        + [dma((shares,))] * 2
        + [dma((shares * (peers - 1),))] * 2
        + [dma((shares,))] * 2,
        compiler_params=pltpu.CompilerParams(collective_id=1, has_side_effects=True),
        cost_estimate=pl.CostEstimate(flops=60 * 10**9, bytes_accessed=2**20, transcendentals=0),
        name="gather_inputs",
    )(tokens, blocks, modulation)


def tail_kernel(cuts, m_ref, g_ref, gate_ref, small_ref, select_ref, m_out, *refs):
    if cuts is None:
        g_out, small_out, select_out, *refs = refs
    else:
        in_final, select_final, *refs = refs
        finals, refs = refs[: len(cuts)], refs[len(cuts) :]
        g_out, small_out, select_out, *refs = refs
    m_parts, g_box, small_box, select_box, g_stage, *sems = refs
    (a_send, a_recv, s_send, s_recv, c_send, c_recv, z_send, z_recv, y_send, y_recv) = sems[:10]
    f_send, f_recv, h_send, h_recv, e_send, e_recv = sems[10:16]
    m_send, m_recv, n_send, n_recv = sems[16:]
    shares, peers = g_ref.shape[0], g_ref.shape[1]
    me, item = lax.axis_index("seq"), lax.axis_index("item")
    greet((("seq", me, shares), ("item", item, peers)))

    def other(t):
        return lax.rem(item + t, peers)

    def origin(t):
        return lax.rem(item - t + peers, peers)

    def ahead(k):
        return lax.rem(me + k, shares)

    def behind(k):
        return lax.rem(me - k + shares, shares)

    def flat(k, t):
        return k * (peers - 1) + t - 1

    def share_small(t):
        return remote(
            small_ref.at[other(t)], small_box.at[t - 1], s_send, s_recv, t - 1, "item", other(t)
        )

    def share_select(t):
        return remote(
            select_ref.at[other(t)], select_box.at[t - 1], c_send, c_recv, t - 1, "item", other(t)
        )

    def share_in(k, t):
        p = ahead(k)
        return remote(
            g_ref.at[p, other(t)], g_box.at[t - 1, p], a_send, a_recv, flat(k, t), "item", other(t)
        )

    def part(k):
        return remote(m_ref, m_parts.at[k - 1], m_send, m_recv, k - 1, "seq", ahead(k))

    def forward_modulation(t):
        block = m_out.at[item]
        return remote(block, block, n_send, n_recv, t - 1, "item", other(t))

    each(1, shares, lambda k: part(k).start())
    each(1, peers, lambda t: share_small(t).start())
    each(1, shares, lambda k: each(1, peers, lambda t: share_in(k, t).start()))
    each(1, peers, lambda t: share_in(0, t).start())
    each(1, peers, lambda t: share_select(t).start())

    def add_small(t, total):
        share_small(t).wait_recv()
        return total + small_box[t - 1].astype(f32)

    small_out[item, me] = lax.fori_loop(
        1, peers, add_small, small_ref[item].astype(f32)
    ).astype(bf16)

    def spread_small(k):
        block = small_out.at[item, me]
        return remote(block, block, y_send, y_recv, k, "seq", ahead(k))

    each(1, shares, lambda k: spread_small(k).start())

    def sum_in(k):
        p = ahead(k)

        def add(t, total):
            share_in(k, t).wait_recv()
            return total + g_box[t - 1, p].astype(f32)

        return lax.fori_loop(1, peers, add, g_ref[p, item].astype(f32)).astype(bf16)

    def place_in(k):
        return remote(
            g_stage.at[k], g_out.at[item, me], z_send, z_recv, k, "seq", ahead(k)
        )

    def turn(k):
        g_stage[k] = sum_in(k)
        place_in(k).start()

    each(1, shares, turn)
    g_out[item, me] = sum_in(0)

    def forward_in(k, t):
        block = g_out.at[item, behind(k)]
        return remote(block, block, f_send, f_recv, flat(k, t), "item", other(t))

    def forward_small(k, t):
        block = small_out.at[item, behind(k)]
        return remote(block, block, h_send, h_recv, flat(k, t), "item", other(t))

    each(1, peers, lambda t: forward_in(0, t).start())
    each(1, peers, lambda t: forward_small(0, t).start())

    def add_part(k, total):
        part(k).wait_recv()
        return total + m_parts[k - 1]

    m_out[item] = lax.fori_loop(1, shares, add_part, m_ref[...])
    each(1, peers, lambda t: forward_modulation(t).start())

    def add_select(t, total):
        share_select(t).wait_recv()
        return total + select_box[t - 1].astype(f32)

    select_out[item] = lax.fori_loop(
        1, peers, add_select, select_ref[item].astype(f32)
    ).astype(bf16)

    def forward_select(t):
        block = select_out.at[item]
        return remote(block, block, e_send, e_recv, t - 1, "item", other(t))

    each(1, peers, lambda t: forward_select(t).start())

    def pass_on(k):
        block = g_out.at[item, behind(k)]
        remote(block, block, z_send, z_recv, k, "seq", behind(k)).wait_recv()
        each(1, peers, lambda t: forward_in(k, t).start())
        little = small_out.at[item, behind(k)]
        remote(little, little, y_send, y_recv, k, "seq", behind(k)).wait_recv()
        each(1, peers, lambda t: forward_small(k, t).start())

    each(1, shares, pass_on)

    def widen_half(block, half, j, s):
        rows, mine = block.shape
        inner = in_final.shape[1] // 2
        place = pl.ds(pl.multiple_of(j * rows, rows), rows)
        first = pl.multiple_of(s * mine + half * inner, lanes)
        in_final[place, pl.ds(first, mine)] = block.astype(f32)

    def widen_in(j, s):
        if cuts is not None:
            widen_half(g_out[j, s], 0, j, s)

    if cuts is not None:
        each(
            0,
            peers,
            lambda j: each(0, shares, lambda s: widen_half(gate_ref[j, s], 1, j, s)),
        )
    each(0, shares, lambda k: widen_in(item, behind(k)))

    def finish(k):
        def one(t):
            block = g_out.at[origin(t), behind(k)]
            remote(block, block, f_send, f_recv, flat(k, t), "item", other(t)).wait_recv()
            little = small_out.at[origin(t), behind(k)]
            remote(little, little, h_send, h_recv, flat(k, t), "item", other(t)).wait_recv()
            widen_in(origin(t), behind(k))
            forward_in(k, t).wait_send()
            forward_small(k, t).wait_send()
            share_in(k, t).wait_send()

        each(1, peers, one)

    each(0, shares, finish)

    def finish_item(t):
        block = select_out.at[origin(t)]
        remote(block, block, e_send, e_recv, t - 1, "item", other(t)).wait_recv()
        forward_select(t).wait_send()
        block = m_out.at[origin(t)]
        remote(block, block, n_send, n_recv, t - 1, "item", other(t)).wait_recv()
        forward_modulation(t).wait_send()
        share_small(t).wait_send()
        share_select(t).wait_send()

    each(1, peers, finish_item)

    def finish_seq(k):
        spread_small(k).wait_send()
        place_in(k).wait_send()
        part(k).wait_send()

    each(1, shares, finish_seq)
    if cuts is None:
        return
    for j in range(peers):
        rows = select_ref.shape[1]
        select_final[j * rows : (j + 1) * rows] = select_out[j].astype(f32)
    inner = in_final.shape[1] // 2
    mine, share = small_ref.shape[2] // 2, small_ref.shape[1]
    for s in range(shares):
        whole = jnp.concatenate([small_out[j, s].astype(f32) for j in range(peers)], axis=0)
        for half in range(2):
            columns = slice(half * inner + s * mine, half * inner + (s + 1) * mine)
            first = 0
            for cut, final in zip(cuts, finals):
                final[:, columns] = whole[first : first + cut, half * mine : (half + 1) * mine]
                first += cut


def weight_sums(modulation, g, gate, small, select, cuts):
    shares, peers = g.shape[:2]
    vmem = pl.BlockSpec(memory_space=pltpu.VMEM)
    dma = pltpu.SemaphoreType.DMA
    some = peers - 1
    sizes = [shares * some] * 2 + [some] * 4 + [shares] * 4 + [shares * some] * 4 + [some] * 2
    sizes += [shares] * 2 + [some] * 2
    kept = [
        ((peers, shares) + g.shape[2:], bf16),
        ((peers, shares) + small.shape[1:], bf16),
        (select.shape, bf16),
    ]
    inner2 = 2 * shares * g.shape[3]
    direct = g.shape[3] % lanes == 0
    outs = kept
    if direct:
        outs = [((peers * g.shape[2], inner2), f32), ((peers * select.shape[1], select.shape[2]), f32)]
        outs += [((cut, inner2), f32) for cut in cuts]
    outs = [((peers,) + modulation.shape, f32)] + outs
    return pl.pallas_call(
        functools.partial(tail_kernel, cuts if direct else None),
        in_specs=[vmem] * 5,
        out_specs=[vmem] * len(outs),
        out_shape=[jax.ShapeDtypeStruct(shape, kind) for shape, kind in outs],
        scratch_shapes=[pltpu.VMEM(shape, kind) for shape, kind in kept if direct]
        + [
            pltpu.VMEM((shares - 1,) + modulation.shape, f32),
            pltpu.VMEM((some, shares) + g.shape[2:], bf16),
            pltpu.VMEM((some,) + small.shape[1:], bf16),
            pltpu.VMEM((some,) + select.shape[1:], bf16),
            pltpu.VMEM((shares,) + g.shape[2:], bf16),
        ]
        + [dma((size,)) for size in sizes],
        compiler_params=pltpu.CompilerParams(
            collective_id=2, has_side_effects=True, vmem_limit_bytes=40 * 2**20
        ),
        cost_estimate=pl.CostEstimate(flops=60 * 10**9, bytes_accessed=2**20, transcendentals=0),
        name="weight_sums",
    )(modulation, g, gate, small, select)


def filter_windows(x, taps, reverse):
    rim = taps - 1
    length = x.shape[1]
    padded = jnp.pad(x, ((0, 0), (rim, rim), (0, 0)))
    starts = [2 * rim - j if reverse else j for j in range(taps)]
    return [padded[:, s : s + length] for s in starts]


def per_device(
    tokens,
    timestep,
    slot_item,
    slot_valid,
    cotangent,
    in_weight,
    out_weight,
    select_weight,
    modulation_weight,
    delta_weight,
    filter_weight,
    filter_bias,
    delta_bias,
    decay_log,
    skip_gain,
    modulation_bias,
):
    slots, local, model = tokens.shape
    shares = lax.axis_size("seq")
    place = lax.axis_index("seq")
    rank, inner = delta_weight.shape[0], delta_weight.shape[1] // 2
    states = decay_log.shape[0]
    select = select_weight.shape[1] // 2
    taps = filter_weight.shape[0]
    rim = taps - 1
    length = local * shares
    rows = slots * length
    mine = inner // shares
    padded_width = -(-mine // lanes) * lanes
    shard_rows = modulation_weight.shape[0]
    items = timestep.shape[0]

    def own_columns(v):
        split = v.reshape(v.shape[:-1] + (2, shares, mine))
        return lax.dynamic_index_in_dim(split, place, split.ndim - 2, False)

    first_slot = lax.axis_index("item") * slots
    valid = lax.dynamic_slice_in_dim(slot_valid, first_slot, slots).astype(f32)[:, None, None]
    chooser = (slot_item[:, None] == jnp.arange(items, dtype=jnp.int32)[None, :]).astype(bf16)
    embedded = jnp.dot(chooser, timestep, preferred_element_type=f32)
    condition = jax.nn.silu(embedded).astype(bf16)
    own_features = lax.dynamic_slice_in_dim(condition, place * shard_rows, shard_rows, 1)
    own_condition = lax.dynamic_slice_in_dim(own_features, first_slot, slots, 0)
    modulation_part = jnp.dot(own_condition, modulation_weight, preferred_element_type=f32)
    peers = lax.axis_size("item")
    share_rows = in_weight.shape[0] // peers
    own_rows = lax.dynamic_slice_in_dim(
        in_weight, lax.axis_index("item") * share_rows, share_rows, 0
    )
    own_rows = jnp.moveaxis(own_rows.reshape(share_rows, 2, shares, mine), 2, 0)
    all_tokens, own_in, modulation = gather_inputs(
        tokens, own_rows.reshape(shares, share_rows, 2 * mine), modulation_part
    )
    own_in = own_in.reshape(model, 2 * mine)
    modulation = modulation + modulation_bias.astype(f32)[None, :]
    shift = modulation[:, None, :model]
    scale = modulation[:, None, model : 2 * model]
    gate = modulation[:, None, 2 * model :]

    source = all_tokens.astype(f32)
    centered = source - jnp.mean(source, axis=-1, keepdims=True)
    spread = lax.rsqrt(jnp.mean(centered * centered, axis=-1, keepdims=True) + epsilon)
    mixed_in = (centered * spread * (1.0 + scale) + shift).astype(bf16).reshape(rows, model)
    projected = jnp.dot(mixed_in, own_in, preferred_element_type=f32).reshape(
        slots, length, 2 * mine
    )
    x_half = projected[..., :mine].astype(bf16)
    gate_half = projected[..., mine:]

    tap_weight = own_columns(filter_weight).astype(f32)
    tap_bias = own_columns(filter_bias).astype(f32)
    step_weight = own_columns(delta_weight)
    step_bias = own_columns(delta_bias)
    rate = -jnp.exp(own_columns(decay_log))
    skip = own_columns(skip_gain)

    filtered, activated, partial = [], [], []
    for d in range(2):
        f = tap_bias[d]
        for j, window in enumerate(filter_windows(x_half, taps, d == 1)):
            f = f + tap_weight[j, d] * window.astype(f32)
        a = jax.nn.silu(f).astype(bf16)
        filtered.append(f)
        activated.append(a)
        partial.append(
            jnp.dot(
                a.reshape(rows, mine),
                select_weight[:, d * select : (d + 1) * select],
                preferred_element_type=f32,
            )
        )
    selection = summed_everywhere(
        jnp.stack(partial).astype(bf16).reshape(2 * slots, length, select), 4
    ).reshape(2, rows, select)
    own_cotangent = cotangent.astype(f32)
    own_grad_branch = (valid * gate * own_cotangent).astype(bf16)
    selection, own_grad_branch = lax.optimization_barrier((selection, own_grad_branch))
    grad_branch = lax.all_gather(own_grad_branch, "seq", axis=1, tiled=True).reshape(rows, model)
    delta_rank = selection[:, :, :rank]
    selection = selection.reshape(2, slots, length, select)
    copies = coefficient_copies(select, rank, states)
    wide_active = widen(jnp.stack(activated), padded_width)
    wide_rate = widen(jnp.swapaxes(rate, 0, 1) * log2e, padded_width)
    wide_weight = widen(
        jnp.pad(jnp.swapaxes(step_weight, 0, 1), ((0, 0), (0, select - rank), (0, 0))),
        padded_width,
    )
    wide_bias = widen(step_bias[:, None, :], padded_width)
    wide_skip = widen(skip[:, None, :], padded_width)
    scanned, hidden, step = scan_states(
        selection, wide_active, wide_weight, wide_bias, wide_rate, copies
    )
    scanned = scanned[..., :mine]
    scanned_sum = scanned[0] + scanned[1]
    for d in range(2):
        scanned_sum = scanned_sum + skip[d] * activated[d].astype(f32)
    silu_gate = jax.nn.silu(gate_half)
    mixed_out = (scanned_sum * silu_gate).astype(bf16).reshape(rows, mine)
    grad_mixed = dot_cols(grad_branch, out_weight).reshape(slots, length, mine)
    grad_scanned = grad_mixed * silu_gate
    grad_gate_half = grad_mixed * scanned_sum * silu_slope(gate_half)
    grad_out = dot_rows(mixed_out, grad_branch).astype(bf16)
    branch_part = (
        jnp.dot(mixed_out, out_weight, preferred_element_type=f32)
        .astype(bf16)
        .reshape(slots, length, model)
    )
    grad_gate_half = grad_gate_half.astype(bf16)
    grad_in_gate = dot_rows(mixed_in, grad_gate_half.reshape(rows, mine)).astype(bf16)
    branch_part, grad_out, grad_in_gate, scan_grad = lax.optimization_barrier(
        (branch_part, grad_out, grad_in_gate, grad_scanned)
    )
    branch_part = lax.psum_scatter(branch_part, "seq", scatter_dimension=1, tiled=True)
    grad_low, grad_input, grad_parts, grad_rate, grad_sums, grad_out, gate_in = scan_adjoint(
        selection,
        wide_active,
        wide_weight,
        wide_rate,
        copies,
        wide_skip,
        step,
        widen(scan_grad, padded_width),
        hidden,
        grad_out.reshape(peers, mine // peers, model),
        grad_in_gate.reshape(shares, peers, share_rows, mine),
    )
    grad_out = grad_out.reshape(mine, model).astype(f32)
    grad_decay = jnp.sum(grad_rate, axis=1)[..., :mine] * ln2
    grad_step_bias = jnp.sum(grad_sums[:, :8, :mine], axis=1)
    grad_skip = jnp.sum(grad_sums[:, 8:, :mine], axis=1)
    grad_parts, branch_part = lax.optimization_barrier((grad_parts, branch_part))
    grad_selection = summed_everywhere(
        grad_parts.reshape(2 * slots, length, select), 5
    ).reshape(2, rows, select)
    grad_delta = [
        dot_rows(delta_rank[d], grad_low[d, ..., :mine].reshape(rows, mine)) for d in range(2)
    ]
    grad_x = jnp.zeros((slots, length, mine), f32)
    grad_select, grad_taps, grad_tap_bias = [], [], []
    for d in range(2):
        block = select_weight[:, d * select : (d + 1) * select]
        grad_select.append(dot_rows(activated[d].reshape(rows, mine), grad_selection[d]))
        grad_active = (
            grad_input[d, ..., :mine]
            + dot_cols(grad_selection[d], block).reshape(slots, length, mine)
        )
        grad_filtered = grad_active * silu_slope(filtered[d])
        grad_tap_bias.append(jnp.sum(grad_filtered, axis=(0, 1)))
        windows = filter_windows(x_half, taps, d == 1)
        grad_taps.append(
            jnp.stack([jnp.sum(grad_filtered * w.astype(f32), axis=(0, 1)) for w in windows])
        )
        for j, window in enumerate(filter_windows(grad_filtered, taps, d == 0)):
            grad_x = grad_x + tap_weight[j, d] * window
    grad_x = grad_x.astype(bf16)
    grad_projected = (
        jnp.concatenate([grad_x, grad_gate_half], axis=2).reshape(rows, 2 * mine)
    )
    mixed_part = dot_cols(grad_projected, own_in).astype(bf16).reshape(slots, length, model)
    grad_mixed_in = lax.psum_scatter(mixed_part, "seq", scatter_dimension=1, tiled=True)
    wide_part = mixed_part.astype(f32)
    grad_modulation_part = jnp.concatenate(
        [
            jnp.sum(wide_part, axis=1),
            jnp.sum(wide_part * (centered * spread), axis=1),
            jnp.sum(valid * own_cotangent * branch_part.astype(f32), axis=1),
        ],
        axis=1,
    )
    grad_in = dot_rows(mixed_in, grad_x.reshape(rows, mine)).astype(bf16)
    branch = branch_part.astype(f32)
    output = (tokens.astype(f32) + valid * gate * branch).astype(bf16)
    small = jnp.concatenate(
        [
            jnp.stack(grad_delta, 1),
            jnp.swapaxes(grad_decay, 0, 1),
            jnp.stack(grad_taps, 1),
            jnp.stack(grad_tap_bias)[None],
            grad_step_bias[None],
            grad_skip[None],
        ],
        axis=0,
    )
    small_rows = small.shape[0]
    share = -(-small_rows // (16 * peers)) * 16
    small = jnp.pad(
        small.astype(bf16).reshape(small_rows, 2 * mine), ((0, peers * share - small_rows), (0, 0))
    )
    grad_select = jnp.concatenate(grad_select, axis=1).astype(bf16)
    cuts = [rank, states, taps, 1, 1, 1]
    grad_modulation, *results = weight_sums(
        grad_modulation_part,
        grad_in.reshape(shares, peers, share_rows, mine),
        gate_in,
        small.reshape(peers, share, 2 * mine),
        grad_select.reshape(peers, mine // peers, 2 * select),
        cuts,
    )
    grad_modulation, grad_mixed_in = lax.optimization_barrier((grad_modulation, grad_mixed_in))
    grad_mixed_in = grad_mixed_in.astype(f32)
    grad_modulation = grad_modulation.reshape(-1, 3 * model)
    own_source = tokens.astype(f32)
    own_centered = own_source - jnp.mean(own_source, axis=-1, keepdims=True)
    own_spread = lax.rsqrt(
        jnp.mean(own_centered * own_centered, axis=-1, keepdims=True) + epsilon
    )
    normed = own_centered * own_spread
    grad_normed = grad_mixed_in * (1.0 + scale)
    grad_source = own_spread * (
        grad_normed
        - jnp.mean(grad_normed, axis=-1, keepdims=True)
        - normed * jnp.mean(grad_normed * normed, axis=-1, keepdims=True)
    )
    grad_tokens = (own_cotangent + grad_source).astype(bf16)
    grad_modulation_weight = lax.dot_general(
        own_features.astype(f32),
        grad_modulation,
        (((0,), (0,)), ((), ())),
        precision=lax.Precision.HIGHEST,
        preferred_element_type=f32,
    )
    if mine % lanes == 0:
        grad_in, grad_select, *small = results
    else:
        grad_in, small, grad_select = results
        grad_in = jnp.stack([grad_in, gate_in]).reshape(2, peers, shares, share_rows, mine)
        grad_in = jnp.transpose(grad_in, (1, 3, 0, 2, 4)).reshape(peers * share_rows, 2 * inner)
        grad_in = grad_in.astype(f32)
        small = small.reshape(peers, shares, share, 2, mine)
        small = jnp.transpose(small, (0, 2, 3, 1, 4)).reshape(peers * share, 2 * inner).astype(f32)
        ends = [sum(cuts[: i + 1]) for i in range(len(cuts))]
        small = [small[end - cut : end] for cut, end in zip(cuts, ends)]
        grad_select = grad_select.reshape(mine, 2 * select).astype(f32)
    return (
        output,
        grad_tokens,
        grad_in,
        grad_out,
        grad_select,
        grad_modulation_weight,
        small[0],
        small[2],
        small[3].reshape(-1),
        small[4].reshape(-1),
        small[1],
        small[5].reshape(-1),
        jnp.sum(grad_modulation, axis=0),
    )


def solution(mesh):
    tokens, rows, same = P("item", "seq", None), P("seq", None), P()
    return jax.shard_map(
        per_device,
        mesh=mesh,
        in_specs=(tokens, same, same, same, tokens, rows, rows, rows, rows) + (same,) * 7,
        out_specs=(tokens, tokens, rows, rows, rows, rows) + (same,) * 7,
        check_vma=False,
    )
```

```python
import functools
import math

import jax
import jax.numpy as jnp
from jax import lax
from jax.experimental import pallas as pl
from jax.experimental.pallas import tpu as pltpu
from jax.sharding import PartitionSpec as P

epsilon = 1e-06
log2e = 1.4426950408889634
ln2 = 0.6931471805599453
chunk = 16
lanes = 128
f32 = jnp.float32
bf16 = jnp.bfloat16


def silu_slope(v):
    s = jax.nn.sigmoid(v)
    return s * (1.0 + v * (1.0 - s))


def dot_rows(a, b):
    return lax.dot_general(a, b, (((0,), (0,)), ((), ())), preferred_element_type=f32)


def dot_cols(a, b):
    return lax.dot_general(a, b, (((1,), (1,)), ((), ())), preferred_element_type=f32)


def fold_sublanes(parts):
    outs = []
    for first in range(0, len(parts), 8):
        cur = parts[first : first + 8]
        row = lax.broadcasted_iota(jnp.int32, cur[0].shape, 0)
        for hop in (4, 2, 1):
            keep = (row // hop) % 2 == 0
            half = len(cur) // 2
            merged = []
            for j in range(half):
                a, b = cur[j], cur[j + half]
                x, y = jnp.where(keep, a, b), jnp.where(keep, b, a)
                if hop == 4:
                    moved = pltpu.roll(y, 4, 0)
                else:
                    moved = jnp.where(keep, pltpu.roll(y, 8 - hop, 0), pltpu.roll(y, hop, 0))
                merged.append(x + moved)
            cur = merged
        outs.append(cur[0])
    return jnp.concatenate(outs, axis=0)


def wide(v, groups):
    return v if groups == 1 else jnp.concatenate([v] * groups, axis=1)


def spread_matrix():
    rows = lax.broadcasted_iota(jnp.int32, (2 * chunk, 2 * lanes), 0) // chunk
    cols = lax.broadcasted_iota(jnp.int32, (2 * chunk, 2 * lanes), 1) // lanes
    return (rows == cols).astype(f32).astype(bf16)


def chunk_sweep(count, body, spread, first, second):
    spread(0, first)
    if count == 1:
        body(0, first)
        return

    def pair(k, carry):
        spread(2 * k + 1, second)
        body(2 * k, first)
        spread(jnp.minimum(2 * k + 2, count - 1), first)
        body(2 * k + 1, second)
        return carry

    lax.fori_loop(0, count // 2, pair, 0)


def place_coefficients(selection, copies):
    placed = jnp.dot(selection, copies, preferred_element_type=f32)
    row = lax.rem(lax.broadcasted_iota(jnp.int32, placed.shape, 0), chunk)
    span = placed.shape[1] // 2
    col = lax.rem(lax.broadcasted_iota(jnp.int32, placed.shape, 1), span) // (span // chunk)
    return jnp.where(row == col, placed, 0.0).astype(bf16)


def softplus(v):
    return jnp.maximum(v, 0.0) + jnp.log1p(jnp.exp(-jnp.abs(v)))


def states_kernel(
    count,
    sel_ref,
    x_ref,
    w_ref,
    bias_ref,
    r_ref,
    copies_ref,
    skip_ref,
    y_ref,
    h_ref,
    dt_ref,
    bc_ref,
    state,
    even,
    odd,
):
    slots, width = dt_ref.shape[1], dt_ref.shape[3]
    groups = width // lanes
    states = r_ref.shape[1]

    @pl.when(pl.program_id(1) == 0)
    def _():
        state[...] = jnp.zeros_like(state)

    for s in range(slots):
        selection = sel_ref[0, s]
        dt_ref[0, s] = softplus(
            jnp.dot(selection, w_ref[0], preferred_element_type=f32) + bias_ref[0]
        )
        bc_ref[0, s] = place_coefficients(selection, copies_ref[...])

    def one_direction(reverse):
        mix = spread_matrix()

        def place(i):
            return (count - 1 - i) if reverse else i

        def spread(i, into):
            start = pl.multiple_of(place(i) * chunk, chunk)
            for s in range(slots):
                both = bc_ref[0, s, pl.ds(start, chunk), :]
                span = both.shape[1] // 2
                into[s] = dot_rows(jnp.concatenate([both[:, :span], both[:, span:]], axis=0), mix)

        def body(i, held):
            start = pl.multiple_of(place(i) * chunk, chunk)
            order = range(chunk - 1, -1, -1) if reverse else range(chunk)
            for s in range(slots):
                h = state[s]
                rate = r_ref[0]
                dt = dt_ref[0, s, pl.ds(start, chunk), :]
                x = x_ref[0, s, pl.ds(start, chunk), :].astype(f32)
                u = dt * x
                kept, sums = [None] * chunk, [None] * chunk
                for t in order:
                    rows = slice(t * states, (t + 1) * states)
                    b = wide(held[s, rows, :lanes], groups)
                    c = wide(held[s, rows, lanes:], groups)
                    h = jnp.exp2(dt[t : t + 1] * rate) * h + u[t : t + 1] * b
                    kept[t] = h.astype(bf16)
                    p = h * c
                    sums[t] = p[:8] + p[8:]
                size = chunk * states
                h_ref[0, s, pl.ds(pl.multiple_of(start * states, size), size), :] = jnp.concatenate(
                    kept, axis=0
                )
                y = fold_sublanes(sums) + skip_ref[0] * x
                y_ref[0, s, pl.ds(start, chunk), :] = y.astype(bf16)
                state[s] = h

        chunk_sweep(count, body, spread, even, odd)

    for d in range(2):

        @pl.when(pl.program_id(0) == d)
        def _():
            one_direction(d == 1)


def side_exchange(b_ref, q_ref, b_out, q_out, b_box, q_box, q_stage, *sems):
    b_keep, q_keep, o_keep, p_keep = sems[:4]
    (i_send, i_recv, j_send, j_recv, a_send, a_recv, z_send, z_recv, f_send, f_recv) = sems[4:]
    shares, peers = q_ref.shape[0], q_ref.shape[1]
    me, item = lax.axis_index("seq"), lax.axis_index("item")
    step = pl.program_id(0) * pl.num_programs(1) + pl.program_id(1)
    quarter = pl.num_programs(0) * pl.num_programs(1) // 4

    def other(t):
        return lax.rem(item + t, peers)

    def origin(t):
        return lax.rem(item - t + peers, peers)

    def ahead(k):
        return lax.rem(me + k, shares)

    def behind(k):
        return lax.rem(me - k + shares, shares)

    def own_b():
        return pltpu.make_async_copy(b_ref.at[item], b_box.at[0], b_keep)

    def own_q():
        return pltpu.make_async_copy(q_ref.at[:, item], q_box.at[0], q_keep)

    def share_b(t):
        return remote(b_ref.at[other(t)], b_box.at[t], i_send, i_recv, t - 1, "item", other(t))

    def share_q(t):
        return remote(q_ref.at[:, other(t)], q_box.at[t], a_send, a_recv, t - 1, "item", other(t))

    def keep_b():
        return pltpu.make_async_copy(b_box.at[0], b_out.at[item], o_keep)

    def keep_q():
        return pltpu.make_async_copy(q_stage.at[me], q_out.at[item, me], p_keep)

    def give_b(t):
        return remote(b_box.at[0], b_out.at[item], j_send, j_recv, t - 1, "item", other(t))

    def place_q(k):
        return remote(
            q_stage.at[ahead(k)], q_out.at[item, me], z_send, z_recv, k, "seq", ahead(k)
        )

    def forward_q(k, t):
        source = q_stage.at[me] if isinstance(k, int) else q_out.at[item, behind(k)]
        return remote(
            source,
            q_out.at[item, behind(k)],
            f_send,
            f_recv,
            k * (peers - 1) + t - 1,
            "item",
            other(t),
        )

    @pl.when(step == 0)
    def _():
        greet((("seq", me, shares), ("item", item, peers)))
        each(1, peers, lambda t: share_q(t).start())
        each(1, peers, lambda t: share_b(t).start())
        own_b().start()
        own_q().start()

    @pl.when(step == quarter)
    def _():
        own_q().wait()
        own_b().wait()

        def arrived(t):
            share_q(t).wait_recv()
            share_b(t).wait_recv()

        each(1, peers, arrived)

        def sum_q(p):
            def add(t, total):
                return total + q_box[t, p].astype(f32)

            q_stage[p] = lax.fori_loop(1, peers, add, q_box[0, p].astype(f32)).astype(bf16)

        each(0, shares, sum_q)
        rows = 16 if b_box.shape[1] % 16 == 0 else b_box.shape[1]

        def sum_b(r):
            place = pl.ds(pl.multiple_of(r * rows, rows), rows)

            def add(t, total):
                return total + b_box[t, place, :].astype(f32)

            total = lax.fori_loop(1, peers, add, b_box[0, place, :].astype(f32))
            b_box[0, place, :] = total.astype(bf16)

        each(0, b_box.shape[1] // rows, sum_b)
        each(1, shares, lambda k: place_q(k).start())
        each(1, peers, lambda t: forward_q(0, t).start())
        each(1, peers, lambda t: give_b(t).start())
        keep_b().start()
        keep_q().start()

    @pl.when(step == 2 * quarter)
    def _():
        def pass_on(k):
            block = q_out.at[item, behind(k)]
            remote(block, block, z_send, z_recv, k, "seq", behind(k)).wait_recv()
            each(1, peers, lambda t: forward_q(k, t).start())

        each(1, shares, pass_on)

    @pl.when(step == 3 * quarter)
    def _():
        keep_b().wait()
        keep_q().wait()

        def finish(t):
            block = b_out.at[origin(t)]
            remote(block, block, j_send, j_recv, t - 1, "item", other(t)).wait_recv()
            give_b(t).wait_send()
            share_b(t).wait_send()
            share_q(t).wait_send()

        each(1, peers, finish)

        def finish_q(k):
            def one(t):
                block = q_out.at[origin(t), behind(k)]
                remote(
                    block, block, f_send, f_recv, k * (peers - 1) + t - 1, "item", other(t)
                ).wait_recv()
                forward_q(k, t).wait_send()

            each(1, peers, one)

        each(0, shares, finish_q)
        each(1, shares, lambda k: place_q(k).wait_send())


def adjoint_kernel(
    count,
    bc_ref,
    x_ref,
    w_ref,
    r_ref,
    copies_ref,
    skip_ref,
    dt_ref,
    g_ref,
    h_ref,
    edge_ref,
    b_ref,
    q_ref,
    low_ref,
    input_ref,
    gsel_ref,
    decay_ref,
    sums_ref,
    b_out,
    q_out,
    pending,
    coefs,
    even,
    odd,
    *side,
):
    slots, width = dt_ref.shape[1], dt_ref.shape[3]
    groups = width // lanes
    states = r_ref.shape[1]
    last_block = pl.program_id(1) == pl.num_programs(1) - 1

    side_exchange(b_ref, q_ref, b_out, q_out, *side)

    @pl.when(pl.program_id(1) == 0)
    def _():
        pending[...] = jnp.zeros_like(pending)
        decay_ref[...] = jnp.zeros_like(decay_ref)
        sums_ref[...] = jnp.zeros_like(sums_ref)

    def one_direction(reverse):
        mix = spread_matrix()
        picks = (
            lax.broadcasted_iota(jnp.int32, (8, 2 * lanes), 0)
            == lax.broadcasted_iota(jnp.int32, (8, 2 * lanes), 1) // lanes
        ).astype(f32).astype(bf16)

        def place(i):
            return i if reverse else (count - 1 - i)

        def spread(i, into):
            start = pl.multiple_of(place(i) * chunk, chunk)
            for s in range(slots):
                both = bc_ref[0, s, pl.ds(start, chunk), :]
                span = both.shape[1] // 2
                into[s] = dot_rows(jnp.concatenate([both[:, :span], both[:, span:]], axis=0), mix)

        def body(i, held):
            here = place(i)
            start = pl.multiple_of(here * chunk, chunk)
            order = range(chunk) if reverse else range(chunk - 1, -1, -1)
            size = chunk * states
            base = pl.multiple_of(start * states, size)
            at_end = here == (count - 1 if reverse else 0)
            outer = jnp.where(last_block, 0.0, 1.0)
            near = pl.multiple_of(
                jnp.clip(start + (chunk if reverse else -1), 0, count * chunk - 1) * states, states
            )
            for s in range(slots):
                pend = pending[s]
                rate = r_ref[0]
                dt = dt_ref[0, s, pl.ds(start, chunk), :]
                x = x_ref[0, s, pl.ds(start, chunk), :].astype(f32)
                g = g_ref[s, pl.ds(start, chunk), :].astype(f32)
                u = dt * x
                before = jnp.where(
                    at_end,
                    edge_ref[0, s].astype(f32) * outer,
                    h_ref[0, s, pl.ds(near, states), :].astype(f32),
                )
                total = decay_ref[0, s]
                rate_sums, into_sums = [None] * chunk, [None] * chunk
                coef = [None] * chunk
                hidden = h_ref[0, s, pl.ds(base, size), :]
                now = hidden[order[0] * states : (order[0] + 1) * states].astype(f32)
                for k, t in enumerate(order):
                    rows = slice(t * states, (t + 1) * states)
                    b = wide(held[s, rows, :lanes], groups)
                    c = wide(held[s, rows, lanes:], groups)
                    if k + 1 < chunk:
                        q = order[k + 1]
                        prev = hidden[q * states : (q + 1) * states].astype(f32)
                    else:
                        prev = before
                    gt = g[t : t + 1]
                    adj = c * gt + pend
                    pend = jnp.exp2(dt[t : t + 1] * rate) * adj
                    through = pend * prev * rate
                    total = total + through * dt[t : t + 1]
                    rate_sums[t] = through[:8] + through[8:]
                    w = adj * b
                    into_sums[t] = w[:8] + w[8:]
                    cb, cc = adj * u[t : t + 1], now * gt
                    sb, sc = cb[:, :lanes], cc[:, :lanes]
                    for j in range(1, groups):
                        sb = sb + cb[:, j * lanes : (j + 1) * lanes]
                        sc = sc + cc[:, j * lanes : (j + 1) * lanes]
                    coef[t] = jnp.concatenate([sb, sc], axis=1).astype(bf16)
                    now = prev
                pending[s] = pend
                decay_ref[0, s] = total
                weighted = fold_sublanes(into_sums)
                few = dt * (1.0 - dt * (0.5 - dt * (1.0 / 6.0 - dt * (1.0 / 24.0))))
                slope = jnp.where(dt < 0.03, few, 1.0 - jnp.exp(-dt))
                grad_pre = (fold_sublanes(rate_sums) * ln2 + weighted * x) * slope
                low_ref[0, s, pl.ds(start, chunk), :] = grad_pre.astype(bf16)
                direct = weighted * dt + skip_ref[0] * g
                input_ref[0, s, pl.ds(start, chunk), :] = direct.astype(bf16)
                gx = g * x
                sums_ref[0] += jnp.concatenate(
                    [grad_pre[:8] + grad_pre[8:], gx[:8] + gx[8:]], axis=0
                )
                coefs[s, pl.ds(pl.multiple_of(here * 8, 8), 8), :] = dot_cols(
                    picks, jnp.concatenate(coef, axis=0)
                )

        chunk_sweep(count, body, spread, even, odd)

    for d in range(2):

        @pl.when(pl.program_id(0) == d)
        def _():
            one_direction(d == 1)


    own = lax.broadcasted_iota(jnp.int32, (chunk, chunk * states), 0) == (
        lax.broadcasted_iota(jnp.int32, (chunk, chunk * states), 1) // states
    )
    for s in range(slots):
        placed = []
        for c in range(count):
            placed.append(
                jnp.concatenate(
                    [
                        jnp.where(own, coefs[s, c * 8 + k : c * 8 + k + 1, :], 0.0)
                        for k in range(2)
                    ],
                    axis=1,
                )
            )
        placed = jnp.concatenate(placed, axis=0).astype(bf16)
        gsel_ref[0, s] = (
            dot_cols(low_ref[0, s], w_ref[0]) + dot_cols(placed, copies_ref[...])
        ).astype(bf16)


def block_of(length):
    return math.gcd(length, 256)


def scan_states(selection, x, weight, bias, rate, copies, skip):
    two, slots, length, width = x.shape
    select = selection.shape[3]
    states = rate.shape[1]
    hidden_size = two * slots * length * states * width
    block = block_of(length)
    blocks = length // block
    spread = copies.shape[1]

    def where(d, i):
        return (d, 0, jnp.where(d == 1, blocks - 1 - i, i), 0)

    def by_direction(d, i):
        return (d, 0, 0)

    return pl.pallas_call(
        functools.partial(states_kernel, block // chunk),
        grid=(two, blocks),
        in_specs=[
            pl.BlockSpec((1, slots, block, select), where),
            pl.BlockSpec((1, slots, block, width), where),
            pl.BlockSpec((1, select, width), by_direction),
            pl.BlockSpec((1, 1, width), by_direction),
            pl.BlockSpec((1, states, width), by_direction),
            pl.BlockSpec((select, spread), lambda d, i: (0, 0)),
            pl.BlockSpec((1, 1, width), by_direction),
        ],
        out_specs=[
            pl.BlockSpec((1, slots, block, width), where),
            pl.BlockSpec((1, slots, block * states, width), where),
            pl.BlockSpec((1, slots, block, width), where),
            pl.BlockSpec((1, slots, block, spread), where),
        ],
        out_shape=[
            jax.ShapeDtypeStruct((two, slots, length, width), bf16),
            jax.ShapeDtypeStruct((two, slots, length * states, width), bf16),
            jax.ShapeDtypeStruct((two, slots, length, width), f32),
            jax.ShapeDtypeStruct((two, slots, length, spread), bf16),
        ],
        scratch_shapes=[
            pltpu.VMEM((slots, states, width), f32),
            pltpu.VMEM((slots, chunk * states, 2 * lanes), f32),
            pltpu.VMEM((slots, chunk * states, 2 * lanes), f32),
        ],
        compiler_params=pltpu.CompilerParams(vmem_limit_bytes=48 * 2**20),
        cost_estimate=pl.CostEstimate(
            flops=64 * 10**9, bytes_accessed=80 * 2**20, transcendentals=hidden_size
        ),
        name="scan_states",
    )(selection, x, weight, bias, rate, copies, skip)


def scan_adjoint(bc, x, weight, rate, copies, skip, dt, g, h, b, q):
    two, slots, length, width = dt.shape
    select = weight.shape[1]
    states = rate.shape[1]
    hidden_size = two * slots * length * states * width
    block = block_of(length)
    blocks = length // block
    spread = copies.shape[1]
    shares, peers = q.shape[:2]
    anywhere, dma = pl.BlockSpec(memory_space=pl.ANY), pltpu.SemaphoreType.DMA

    def at(d, i):
        return jnp.where(d == 1, i, blocks - 1 - i)

    def where(d, i):
        return (d, 0, at(d, i), 0)

    def edge(d, i):
        mine = at(d, i) * block
        return (d, 0, jnp.clip(jnp.where(d == 1, mine + block, mine - 1), 0, length - 1), 0)

    def by_direction(d, i):
        return (d, 0, 0)

    return pl.pallas_call(
        functools.partial(adjoint_kernel, block // chunk),
        grid=(two, blocks),
        in_specs=[
            pl.BlockSpec((1, slots, block, spread), where),
            pl.BlockSpec((1, slots, block, width), where),
            pl.BlockSpec((1, select, width), by_direction),
            pl.BlockSpec((1, states, width), by_direction),
            pl.BlockSpec((select, spread), lambda d, i: (0, 0)),
            pl.BlockSpec((1, 1, width), by_direction),
            pl.BlockSpec((1, slots, block, width), where),
            pl.BlockSpec((slots, block, width), lambda d, i: (0, at(d, i), 0)),
            pl.BlockSpec((1, slots, block * states, width), where),
            pl.BlockSpec((1, slots, states, width), edge),
            anywhere,
            anywhere,
        ],
        out_specs=[
            pl.BlockSpec((1, slots, block, width), where),
            pl.BlockSpec((1, slots, block, width), where),
            pl.BlockSpec((1, slots, block, select), where),
            pl.BlockSpec((1, slots, states, width), lambda d, i: (d, 0, 0, 0)),
            pl.BlockSpec((1, 16, width), by_direction),
            anywhere,
            anywhere,
        ],
        out_shape=[
            jax.ShapeDtypeStruct((two, slots, length, width), bf16),
            jax.ShapeDtypeStruct((two, slots, length, width), bf16),
            jax.ShapeDtypeStruct((two, slots, length, select), bf16),
            jax.ShapeDtypeStruct((two, slots, states, width), f32),
            jax.ShapeDtypeStruct((two, 16, width), f32),
            jax.ShapeDtypeStruct(b.shape, bf16),
            jax.ShapeDtypeStruct((peers, shares) + q.shape[2:], bf16),
        ],
        scratch_shapes=[
            pltpu.VMEM((slots, states, width), f32),
            pltpu.VMEM((slots, block // chunk * 8, chunk * states), f32),
            pltpu.VMEM((slots, chunk * states, 2 * lanes), f32),
            pltpu.VMEM((slots, chunk * states, 2 * lanes), f32),
            pltpu.VMEM(b.shape, bf16),
            pltpu.VMEM((peers, shares) + q.shape[2:], bf16),
            pltpu.VMEM((shares,) + q.shape[2:], bf16),
        ]
        + [dma] * 4
        + [dma((peers - 1,))] * 6
        + [dma((shares,))] * 2
        + [dma((shares * (peers - 1),))] * 2,
        compiler_params=pltpu.CompilerParams(
            collective_id=6, has_side_effects=True, vmem_limit_bytes=48 * 2**20
        ),
        cost_estimate=pl.CostEstimate(
            flops=100 * 10**9, bytes_accessed=100 * 2**20, transcendentals=hidden_size
        ),
        name="scan_adjoint",
    )(bc, x, weight, rate, copies, skip, dt, g, h, h, b, q)


def coefficient_copies(width, rank, states):
    span = chunk * states
    col = jnp.arange(2 * span)
    origin = rank + (col // span) * states + col % states
    return (jnp.arange(width)[:, None] == origin[None, :]).astype(bf16)


def widen(v, width):
    short = width - v.shape[-1]
    return v if short == 0 else jnp.pad(v, ((0, 0),) * (v.ndim - 1) + ((0, short),))


def remote(src, dst, sends, recvs, slot, axis, to):
    return pltpu.make_async_remote_copy(
        src_ref=src,
        dst_ref=dst,
        send_sem=sends.at[slot],
        recv_sem=recvs.at[slot],
        device_id={axis: to},
        device_id_type=pl.DeviceIdType.MESH,
    )


def each(first, last, body):
    def run(k, carry):
        body(k)
        return carry

    lax.fori_loop(first, last, run, 0)


def greet(peers):
    barrier = pltpu.get_barrier_semaphore()
    total = 0
    for axis, me, count in peers:

        def hello(k):
            pl.semaphore_signal(
                barrier,
                inc=1,
                device_id={axis: lax.rem(me + k, count)},
                device_id_type=pl.DeviceIdType.MESH,
            )

        each(1, count, hello)
        total += count - 1
    pl.semaphore_wait(barrier, total)


def total_kernel(line, v_ref, o_ref, pairbox, stage, inbox, *sems):
    pair_send, pair_recv, sum_send, sum_recv, out_send, out_recv, fwd_send, fwd_recv = sems
    me = lax.axis_index("seq")
    pos, core = me // 2, lax.rem(me, 2)
    partner = me + 1 - 2 * core
    barrier = pltpu.get_barrier_semaphore()

    def hello(to):
        pl.semaphore_signal(
            barrier, inc=1, device_id={"seq": to}, device_id_type=pl.DeviceIdType.MESH
        )

    hello(partner)
    each(1, line, lambda k: hello(lax.rem(pos + k, line) * 2 + core))
    pl.semaphore_wait(barrier, line)

    pair = remote(v_ref.at[:, :, 1 - core], pairbox, pair_send, pair_recv, 0, "seq", partner)
    pair.start()
    pair.wait_recv()

    def own(q):
        return v_ref[:, q, core].astype(f32) + pairbox[:, q].astype(f32)

    def summand(k):
        q = lax.rem(pos + k, line)
        return remote(
            stage.at[q], inbox.at[pos], sum_send, sum_recv, k - 1, "seq", q * 2 + core
        )

    def send(k):
        q = lax.rem(pos + k, line)
        stage[q] = own(q).astype(bf16)
        summand(k).start()

    each(1, line, send)

    def source(k):
        return lax.rem(pos - k + line, line)

    def arrived(k, total):
        q = source(k)
        remote(stage.at[q], inbox.at[q], sum_send, sum_recv, k - 1, "seq", partner).wait_recv()
        return total + inbox[q].astype(f32)

    total = lax.fori_loop(1, line, arrived, own(pos))
    o_ref[:, pos, core] = total.astype(bf16)

    def result(k):
        mine = o_ref.at[:, pos, core]
        return remote(
            mine, mine, out_send, out_recv, k - 1, "seq", lax.rem(pos + k, line) * 2 + core
        )

    def forward(k):
        block = o_ref.at[:, source(k), core]
        return remote(block, block, fwd_send, fwd_recv, k, "seq", partner)

    each(1, line, lambda k: result(k).start())
    forward(0).start()

    def pass_on(k):
        block = o_ref.at[:, source(k), core]
        remote(block, block, out_send, out_recv, k - 1, "seq", partner).wait_recv()
        forward(k).start()

    each(1, line, pass_on)

    def finish(k):
        block = o_ref.at[:, source(k), 1 - core]
        remote(block, block, fwd_send, fwd_recv, k, "seq", partner).wait_recv()
        forward(k).wait_send()

    each(0, line, finish)
    pair.wait_send()

    def drain(k):
        summand(k).wait_send()
        result(k).wait_send()

    each(1, line, drain)


def summed_everywhere(v, call):
    batch, length, width = v.shape
    shares = lax.axis_size("seq")
    line, rows = shares // 2, length // shares
    vmem = pl.BlockSpec(memory_space=pltpu.VMEM)
    dma = pltpu.SemaphoreType.DMA
    blocks = v.reshape(batch, line, 2, rows, width)
    out = pl.pallas_call(
        functools.partial(total_kernel, line),
        in_specs=[vmem],
        out_specs=vmem,
        out_shape=jax.ShapeDtypeStruct(blocks.shape, bf16),
        scratch_shapes=[
            pltpu.VMEM((batch, line, rows, width), bf16),
            pltpu.VMEM((line, batch, rows, width), bf16),
            pltpu.VMEM((line, batch, rows, width), bf16),
            dma((1,)),
            dma((1,)),
            dma((line,)),
            dma((line,)),
            dma((line,)),
            dma((line,)),
            dma((line,)),
            dma((line,)),
        ],
        compiler_params=pltpu.CompilerParams(
            collective_id=call, has_side_effects=True, vmem_limit_bytes=40 * 2**20
        ),
        cost_estimate=pl.CostEstimate(flops=25 * 10**9, bytes_accessed=2**20, transcendentals=0),
        name="sum_" + str(call),
    )(blocks)
    return out.reshape(v.shape)


def head_kernel(line, t_ref, w_ref, mod_ref, all_ref, box_ref, out_ref, parts, *sems):
    keep, t_keep, u_send, u_recv, d_send, d_recv, p_send, p_recv = sems[:8]
    w_send, w_recv, f_send, f_recv, m_send, m_recv = sems[8:]
    shares, peers = box_ref.shape[0], box_ref.shape[1]
    slots, local = t_ref.shape[0], t_ref.shape[1]
    me, item = lax.axis_index("seq"), lax.axis_index("item")
    pos, core = me // 2, lax.rem(me, 2)
    partner = me + 1 - 2 * core
    greet((("seq", me, shares), ("item", item, peers)))

    def region(q, c, s):
        first = pl.multiple_of((q * 2 + c) * local, local)
        return all_ref.at[s, pl.ds(first, local), :]

    def hop(q, s, source, sends, recvs, k, to):
        return remote(source, region(q, core, s), sends, recvs, k * slots + s, "seq", to)

    def up(k, s):
        source = t_ref.at[s] if isinstance(k, int) else region(pos - k, core, s)
        return hop(pos - k, s, source, u_send, u_recv, k, me + 2)

    def down(k, s):
        source = t_ref.at[s] if isinstance(k, int) else region(pos + k, core, s)
        return hop(pos + k, s, source, d_send, d_recv, k, me - 2)

    def across(q, s):
        return remote(
            region(q, core, s), region(q, core, s), p_send, p_recv, q * slots + s, "seq", partner
        )

    def own_across(s):
        return remote(
            t_ref.at[s], region(pos, core, s), p_send, p_recv, pos * slots + s, "seq", partner
        )

    not_last, not_first = pos < line - 1, pos > 0
    for s in range(slots):

        @pl.when(not_last)
        def _():
            up(0, s).start()

        @pl.when(not_first)
        def _():
            down(0, s).start()

    def modulation(k):
        return remote(
            mod_ref, parts.at[k - 1], m_send, m_recv, k - 1, "seq", lax.rem(me + k, shares)
        )

    def weight(k):
        to = lax.rem(me + k, shares)
        return remote(w_ref.at[to], box_ref.at[me, item], w_send, w_recv, k, "seq", to)

    each(1, shares, lambda k: modulation(k).start())
    each(1, shares, lambda k: weight(k).start())
    own = pltpu.make_async_copy(w_ref.at[me], box_ref.at[me, item], keep)
    own.start()
    kept = []
    for s in range(slots):
        own_across(s).start()
        kept.append(pltpu.make_async_copy(t_ref.at[s], region(pos, core, s), t_keep.at[s]))
        kept[-1].start()

    def forward(k, t):
        block = box_ref.at[lax.rem(me - k + shares, shares), item]
        return remote(
            block, block, f_send, f_recv, k * (peers - 1) + t - 1, "item", lax.rem(item + t, peers)
        )

    def pass_on(k):
        source = lax.rem(me - k + shares, shares)
        block = box_ref.at[source, item]
        remote(block, block, w_send, w_recv, k, "seq", source).wait_recv()
        each(1, peers, lambda t: forward(k, t).start())

    def relay(k):
        for s in range(slots):

            @pl.when(k < pos)
            def _():
                q = pos - 1 - k
                hop(q, s, region(q, core, s), u_send, u_recv, k, partner).wait_recv()

                @pl.when(not_last)
                def _():
                    up(k + 1, s).start()

                across(q, s).start()

            @pl.when(k < line - 1 - pos)
            def _():
                q = pos + 1 + k
                hop(q, s, region(q, core, s), d_send, d_recv, k, partner).wait_recv()

                @pl.when(not_first)
                def _():
                    down(k + 1, s).start()

                across(q, s).start()

    own.wait()
    each(1, peers, lambda t: forward(0, t).start())
    half = shares // 2
    each(1, half, pass_on)
    each(0, 1, relay)
    each(half, shares, pass_on)

    def add(k, total):
        modulation(k).wait_recv()
        return total + parts[k - 1]

    out_ref[...] = lax.fori_loop(1, shares, add, mod_ref[...])
    each(1, line - 1, relay)

    def finish(k):
        def one(t):
            source = lax.rem(item - t + peers, peers)
            block = box_ref.at[lax.rem(me - k + shares, shares), source]
            remote(
                block, block, f_send, f_recv, k * (peers - 1) + t - 1, "item", source
            ).wait_recv()
            forward(k, t).wait_send()

        each(1, peers, one)

    each(0, shares, finish)

    def drain(k):
        weight(k).wait_send()
        modulation(k).wait_send()

    each(1, shares, drain)

    def drain_tokens(q):
        for s in range(slots):
            remote(
                region(q, core, s),
                region(q, 1 - core, s),
                p_send,
                p_recv,
                q * slots + s,
                "seq",
                partner,
            ).wait_recv()
            across(q, s).wait_send()

    each(0, line, drain_tokens)

    def drain_line(k):
        for s in range(slots):

            @pl.when(not_last & (k <= pos))
            def _():
                up(k, s).wait_send()

            @pl.when(not_first & (k <= line - 1 - pos))
            def _():
                down(k, s).wait_send()

    each(0, line, drain_line)
    for copy in kept:
        copy.wait()


def gather_inputs(tokens, blocks, modulation):
    shares, peers = lax.axis_size("seq"), lax.axis_size("item")
    slots, local, model = tokens.shape
    line = shares // 2
    vmem, anywhere = pl.BlockSpec(memory_space=pltpu.VMEM), pl.BlockSpec(memory_space=pl.ANY)
    dma = pltpu.SemaphoreType.DMA
    return pl.pallas_call(
        functools.partial(head_kernel, line),
        in_specs=[anywhere, anywhere, vmem],
        out_specs=[anywhere, anywhere, vmem],
        out_shape=[
            jax.ShapeDtypeStruct((slots, local * shares, model), bf16),
            jax.ShapeDtypeStruct((shares, peers) + blocks.shape[1:], bf16),
            jax.ShapeDtypeStruct(modulation.shape, f32),
        ],
        scratch_shapes=[pltpu.VMEM((shares - 1,) + modulation.shape, f32), dma, dma((slots,))]
        + [dma((line * slots,))] * 6
        + [dma((shares,))] * 2
        + [dma((shares * (peers - 1),))] * 2
        + [dma((shares,))] * 2,
        compiler_params=pltpu.CompilerParams(collective_id=1, has_side_effects=True),
        cost_estimate=pl.CostEstimate(flops=60 * 10**9, bytes_accessed=2**20, transcendentals=0),
        name="gather_inputs",
    )(tokens, blocks, modulation)


def tail_kernel(cuts, m_ref, g_ref, gate_ref, small_ref, select_ref, m_out, *refs):
    if cuts is None:
        g_out, small_out, select_out, *refs = refs
    else:
        in_final, select_final, *refs = refs
        finals, refs = refs[: len(cuts)], refs[len(cuts) :]
        g_out, small_out, select_out, *refs = refs
    m_parts, g_box, small_box, select_box, g_stage, *sems = refs
    (a_send, a_recv, s_send, s_recv, c_send, c_recv, z_send, z_recv, y_send, y_recv) = sems[:10]
    f_send, f_recv, h_send, h_recv, e_send, e_recv = sems[10:16]
    m_send, m_recv, n_send, n_recv = sems[16:]
    shares, peers = g_ref.shape[0], g_ref.shape[1]
    me, item = lax.axis_index("seq"), lax.axis_index("item")
    greet((("seq", me, shares), ("item", item, peers)))

    def other(t):
        return lax.rem(item + t, peers)

    def origin(t):
        return lax.rem(item - t + peers, peers)

    def ahead(k):
        return lax.rem(me + k, shares)

    def behind(k):
        return lax.rem(me - k + shares, shares)

    def flat(k, t):
        return k * (peers - 1) + t - 1

    def share_small(t):
        return remote(
            small_ref.at[other(t)], small_box.at[t - 1], s_send, s_recv, t - 1, "item", other(t)
        )

    def share_select(t):
        return remote(
            select_ref.at[other(t)], select_box.at[t - 1], c_send, c_recv, t - 1, "item", other(t)
        )

    def share_in(k, t):
        p = ahead(k)
        return remote(
            g_ref.at[p, other(t)], g_box.at[t - 1, p], a_send, a_recv, flat(k, t), "item", other(t)
        )

    def part(k):
        return remote(m_ref, m_parts.at[k - 1], m_send, m_recv, k - 1, "seq", ahead(k))

    def forward_modulation(t):
        block = m_out.at[item]
        return remote(block, block, n_send, n_recv, t - 1, "item", other(t))

    each(1, shares, lambda k: part(k).start())
    each(1, peers, lambda t: share_small(t).start())
    each(1, shares, lambda k: each(1, peers, lambda t: share_in(k, t).start()))
    each(1, peers, lambda t: share_in(0, t).start())
    each(1, peers, lambda t: share_select(t).start())

    def add_small(t, total):
        share_small(t).wait_recv()
        return total + small_box[t - 1].astype(f32)

    small_out[item, me] = lax.fori_loop(
        1, peers, add_small, small_ref[item].astype(f32)
    ).astype(bf16)

    def spread_small(k):
        block = small_out.at[item, me]
        return remote(block, block, y_send, y_recv, k, "seq", ahead(k))

    each(1, shares, lambda k: spread_small(k).start())

    def sum_in(k):
        p = ahead(k)

        def add(t, total):
            share_in(k, t).wait_recv()
            return total + g_box[t - 1, p].astype(f32)

        return lax.fori_loop(1, peers, add, g_ref[p, item].astype(f32)).astype(bf16)

    def place_in(k):
        return remote(
            g_stage.at[k], g_out.at[item, me], z_send, z_recv, k, "seq", ahead(k)
        )

    def turn(k):
        g_stage[k] = sum_in(k)
        place_in(k).start()

    each(1, shares, turn)
    g_out[item, me] = sum_in(0)

    def forward_in(k, t):
        block = g_out.at[item, behind(k)]
        return remote(block, block, f_send, f_recv, flat(k, t), "item", other(t))

    def forward_small(k, t):
        block = small_out.at[item, behind(k)]
        return remote(block, block, h_send, h_recv, flat(k, t), "item", other(t))

    each(1, peers, lambda t: forward_in(0, t).start())
    each(1, peers, lambda t: forward_small(0, t).start())

    def add_part(k, total):
        part(k).wait_recv()
        return total + m_parts[k - 1]

    m_out[item] = lax.fori_loop(1, shares, add_part, m_ref[...])
    each(1, peers, lambda t: forward_modulation(t).start())

    def add_select(t, total):
        share_select(t).wait_recv()
        return total + select_box[t - 1].astype(f32)

    select_out[item] = lax.fori_loop(
        1, peers, add_select, select_ref[item].astype(f32)
    ).astype(bf16)

    def forward_select(t):
        block = select_out.at[item]
        return remote(block, block, e_send, e_recv, t - 1, "item", other(t))

    each(1, peers, lambda t: forward_select(t).start())

    def pass_on(k):
        block = g_out.at[item, behind(k)]
        remote(block, block, z_send, z_recv, k, "seq", behind(k)).wait_recv()
        each(1, peers, lambda t: forward_in(k, t).start())
        little = small_out.at[item, behind(k)]
        remote(little, little, y_send, y_recv, k, "seq", behind(k)).wait_recv()
        each(1, peers, lambda t: forward_small(k, t).start())

    each(1, shares, pass_on)

    def widen_half(block, half, j, s):
        rows, mine = block.shape
        inner = in_final.shape[1] // 2
        place = pl.ds(pl.multiple_of(j * rows, rows), rows)
        first = pl.multiple_of(s * mine + half * inner, lanes)
        in_final[place, pl.ds(first, mine)] = block.astype(f32)

    def widen_in(j, s):
        if cuts is not None:
            widen_half(g_out[j, s], 0, j, s)

    if cuts is not None:
        each(
            0,
            peers,
            lambda j: each(0, shares, lambda s: widen_half(gate_ref[j, s], 1, j, s)),
        )
    each(0, shares, lambda k: widen_in(item, behind(k)))

    def finish(k):
        def one(t):
            block = g_out.at[origin(t), behind(k)]
            remote(block, block, f_send, f_recv, flat(k, t), "item", other(t)).wait_recv()
            little = small_out.at[origin(t), behind(k)]
            remote(little, little, h_send, h_recv, flat(k, t), "item", other(t)).wait_recv()
            widen_in(origin(t), behind(k))
            forward_in(k, t).wait_send()
            forward_small(k, t).wait_send()
            share_in(k, t).wait_send()

        each(1, peers, one)

    each(0, shares, finish)

    def finish_item(t):
        block = select_out.at[origin(t)]
        remote(block, block, e_send, e_recv, t - 1, "item", other(t)).wait_recv()
        forward_select(t).wait_send()
        block = m_out.at[origin(t)]
        remote(block, block, n_send, n_recv, t - 1, "item", other(t)).wait_recv()
        forward_modulation(t).wait_send()
        share_small(t).wait_send()
        share_select(t).wait_send()

    each(1, peers, finish_item)

    def finish_seq(k):
        spread_small(k).wait_send()
        place_in(k).wait_send()
        part(k).wait_send()

    each(1, shares, finish_seq)
    if cuts is None:
        return
    for j in range(peers):
        rows = select_ref.shape[1]
        select_final[j * rows : (j + 1) * rows] = select_out[j].astype(f32)
    inner = in_final.shape[1] // 2
    mine, share = small_ref.shape[2] // 2, small_ref.shape[1]
    for s in range(shares):
        whole = jnp.concatenate([small_out[j, s].astype(f32) for j in range(peers)], axis=0)
        for half in range(2):
            columns = slice(half * inner + s * mine, half * inner + (s + 1) * mine)
            first = 0
            for cut, final in zip(cuts, finals):
                final[:, columns] = whole[first : first + cut, half * mine : (half + 1) * mine]
                first += cut


def weight_sums(modulation, g, gate, small, select, cuts):
    shares, peers = g.shape[:2]
    vmem = pl.BlockSpec(memory_space=pltpu.VMEM)
    dma = pltpu.SemaphoreType.DMA
    some = peers - 1
    sizes = [shares * some] * 2 + [some] * 4 + [shares] * 4 + [shares * some] * 4 + [some] * 2
    sizes += [shares] * 2 + [some] * 2
    kept = [
        ((peers, shares) + g.shape[2:], bf16),
        ((peers, shares) + small.shape[1:], bf16),
        (select.shape, bf16),
    ]
    inner2 = 2 * shares * g.shape[3]
    direct = g.shape[3] % lanes == 0
    outs = kept
    if direct:
        outs = [((peers * g.shape[2], inner2), f32), ((peers * select.shape[1], select.shape[2]), f32)]
        outs += [((cut, inner2), f32) for cut in cuts]
    outs = [((peers,) + modulation.shape, f32)] + outs
    return pl.pallas_call(
        functools.partial(tail_kernel, cuts if direct else None),
        in_specs=[vmem] * 5,
        out_specs=[vmem] * len(outs),
        out_shape=[jax.ShapeDtypeStruct(shape, kind) for shape, kind in outs],
        scratch_shapes=[pltpu.VMEM(shape, kind) for shape, kind in kept if direct]
        + [
            pltpu.VMEM((shares - 1,) + modulation.shape, f32),
            pltpu.VMEM((some, shares) + g.shape[2:], bf16),
            pltpu.VMEM((some,) + small.shape[1:], bf16),
            pltpu.VMEM((some,) + select.shape[1:], bf16),
            pltpu.VMEM((shares,) + g.shape[2:], bf16),
        ]
        + [dma((size,)) for size in sizes],
        compiler_params=pltpu.CompilerParams(
            collective_id=2, has_side_effects=True, vmem_limit_bytes=40 * 2**20
        ),
        cost_estimate=pl.CostEstimate(flops=60 * 10**9, bytes_accessed=2**20, transcendentals=0),
        name="weight_sums",
    )(modulation, g, gate, small, select)


def filter_windows(x, taps, reverse):
    rim = taps - 1
    length = x.shape[1]
    padded = jnp.pad(x, ((0, 0), (rim, rim), (0, 0)))
    starts = [2 * rim - j if reverse else j for j in range(taps)]
    return [padded[:, s : s + length] for s in starts]


def per_device(
    tokens,
    timestep,
    slot_item,
    slot_valid,
    cotangent,
    in_weight,
    out_weight,
    select_weight,
    modulation_weight,
    delta_weight,
    filter_weight,
    filter_bias,
    delta_bias,
    decay_log,
    skip_gain,
    modulation_bias,
):
    slots, local, model = tokens.shape
    shares = lax.axis_size("seq")
    place = lax.axis_index("seq")
    rank, inner = delta_weight.shape[0], delta_weight.shape[1] // 2
    states = decay_log.shape[0]
    select = select_weight.shape[1] // 2
    taps = filter_weight.shape[0]
    rim = taps - 1
    length = local * shares
    rows = slots * length
    mine = inner // shares
    padded_width = -(-mine // lanes) * lanes
    shard_rows = modulation_weight.shape[0]
    items = timestep.shape[0]

    def own_columns(v):
        split = v.reshape(v.shape[:-1] + (2, shares, mine))
        return lax.dynamic_index_in_dim(split, place, split.ndim - 2, False)

    first_slot = lax.axis_index("item") * slots
    valid = lax.dynamic_slice_in_dim(slot_valid, first_slot, slots).astype(f32)[:, None, None]
    chooser = (slot_item[:, None] == jnp.arange(items, dtype=jnp.int32)[None, :]).astype(bf16)
    embedded = jnp.dot(chooser, timestep, preferred_element_type=f32)
    condition = jax.nn.silu(embedded).astype(bf16)
    own_features = lax.dynamic_slice_in_dim(condition, place * shard_rows, shard_rows, 1)
    own_condition = lax.dynamic_slice_in_dim(own_features, first_slot, slots, 0)
    modulation_part = jnp.dot(own_condition, modulation_weight, preferred_element_type=f32)
    peers = lax.axis_size("item")
    share_rows = in_weight.shape[0] // peers
    own_rows = lax.dynamic_slice_in_dim(
        in_weight, lax.axis_index("item") * share_rows, share_rows, 0
    )
    own_rows = jnp.moveaxis(own_rows.reshape(share_rows, 2, shares, mine), 2, 0)
    all_tokens, own_in, modulation = gather_inputs(
        tokens, own_rows.reshape(shares, share_rows, 2 * mine), modulation_part
    )
    own_in = own_in.reshape(model, 2 * mine)
    modulation = modulation + modulation_bias.astype(f32)[None, :]
    shift = modulation[:, None, :model]
    scale = modulation[:, None, model : 2 * model]
    gate = modulation[:, None, 2 * model :]

    source = all_tokens.astype(f32)
    centered = source - jnp.mean(source, axis=-1, keepdims=True)
    spread = lax.rsqrt(jnp.mean(centered * centered, axis=-1, keepdims=True) + epsilon)
    mixed_in = (centered * spread * (1.0 + scale) + shift).astype(bf16).reshape(rows, model)
    mixed_in = lax.optimization_barrier(mixed_in)
    projected = (
        jnp.dot(mixed_in, own_in, preferred_element_type=f32)
        .astype(bf16)
        .reshape(slots, length, 2 * mine)
    )
    x_half = projected[..., :mine]
    gate_half = projected[..., mine:].astype(f32)

    tap_weight = own_columns(filter_weight).astype(f32)
    tap_bias = own_columns(filter_bias).astype(f32)
    step_weight = own_columns(delta_weight)
    step_bias = own_columns(delta_bias)
    rate = -jnp.exp(own_columns(decay_log))
    skip = own_columns(skip_gain)

    filtered, activated, partial = [], [], []
    for d in range(2):
        f = tap_bias[d]
        for j, window in enumerate(filter_windows(x_half, taps, d == 1)):
            f = f + tap_weight[j, d] * window.astype(f32)
        a = jax.nn.silu(f).astype(bf16)
        filtered.append(f)
        activated.append(a)
        partial.append(
            jnp.dot(
                a.reshape(rows, mine),
                select_weight[:, d * select : (d + 1) * select],
                preferred_element_type=f32,
            )
        )
    selection = summed_everywhere(
        jnp.stack(partial).astype(bf16).reshape(2 * slots, length, select), 4
    ).reshape(2, rows, select)
    own_cotangent = cotangent.astype(f32)
    own_grad_branch = (valid * gate * own_cotangent).astype(bf16)
    selection, own_grad_branch = lax.optimization_barrier((selection, own_grad_branch))
    grad_branch = lax.all_gather(own_grad_branch, "seq", axis=1, tiled=True).reshape(rows, model)
    delta_rank = selection[:, :, :rank]
    selection = selection.reshape(2, slots, length, select)
    copies = coefficient_copies(select, rank, states)
    wide_active = widen(jnp.stack(activated), padded_width)
    wide_rate = widen(jnp.swapaxes(rate, 0, 1) * log2e, padded_width)
    wide_weight = widen(
        jnp.pad(jnp.swapaxes(step_weight, 0, 1), ((0, 0), (0, select - rank), (0, 0))),
        padded_width,
    )
    wide_bias = widen(step_bias[:, None, :], padded_width)
    wide_skip = widen(skip[:, None, :], padded_width)
    scanned, hidden, step, bc = scan_states(
        selection, wide_active, wide_weight, wide_bias, wide_rate, copies, wide_skip
    )
    scanned = scanned[..., :mine]
    scanned_sum = scanned[0].astype(f32) + scanned[1].astype(f32)
    silu_gate = jax.nn.silu(gate_half)
    mixed_out = (scanned_sum * silu_gate).astype(bf16).reshape(rows, mine)
    grad_mixed = dot_cols(grad_branch, out_weight).reshape(slots, length, mine)
    grad_scanned = grad_mixed * silu_gate
    grad_gate_half = grad_mixed * scanned_sum * silu_slope(gate_half)
    grad_out = dot_rows(mixed_out, grad_branch).astype(bf16)
    branch_part = (
        jnp.dot(mixed_out, out_weight, preferred_element_type=f32)
        .astype(bf16)
        .reshape(slots, length, model)
    )
    grad_gate_half = grad_gate_half.astype(bf16)
    grad_in_gate = dot_rows(mixed_in, grad_gate_half.reshape(rows, mine)).astype(bf16)
    branch_part, grad_out, grad_in_gate, scan_grad = lax.optimization_barrier(
        (branch_part, grad_out, grad_in_gate, grad_scanned)
    )
    branch_part = lax.psum_scatter(branch_part, "seq", scatter_dimension=1, tiled=True)
    grad_low, grad_input, grad_parts, grad_rate, grad_sums, grad_out, gate_in = scan_adjoint(
        bc,
        wide_active,
        wide_weight,
        wide_rate,
        copies,
        wide_skip,
        step,
        widen(scan_grad, padded_width),
        hidden,
        grad_out.reshape(peers, mine // peers, model),
        grad_in_gate.reshape(shares, peers, share_rows, mine),
    )
    grad_out = grad_out.reshape(mine, model).astype(f32)
    grad_decay = jnp.sum(grad_rate, axis=1)[..., :mine] * ln2
    grad_step_bias = jnp.sum(grad_sums[:, :8, :mine], axis=1)
    grad_skip = jnp.sum(grad_sums[:, 8:, :mine], axis=1)
    grad_parts, branch_part = lax.optimization_barrier((grad_parts, branch_part))
    grad_selection = summed_everywhere(
        grad_parts.reshape(2 * slots, length, select), 5
    ).reshape(2, rows, select)
    grad_delta = jnp.einsum(
        "drk,dre->kde",
        delta_rank,
        grad_low[..., :mine].reshape(2, rows, mine),
        preferred_element_type=f32,
    )
    grad_x = jnp.zeros((slots, length, mine), f32)
    grad_select, grad_taps, grad_tap_bias = [], [], []
    for d in range(2):
        block = select_weight[:, d * select : (d + 1) * select]
        grad_select.append(
            dot_rows(grad_selection[d], activated[d].reshape(rows, mine)).T
        )
        grad_active = (
            grad_input[d, ..., :mine]
            + dot_cols(grad_selection[d], block).reshape(slots, length, mine)
        )
        grad_filtered = grad_active * silu_slope(filtered[d])
        grad_tap_bias.append(jnp.sum(grad_filtered, axis=(0, 1)))
        windows = filter_windows(x_half, taps, d == 1)
        grad_taps.append(
            jnp.stack([jnp.sum(grad_filtered * w.astype(f32), axis=(0, 1)) for w in windows])
        )
        for j, window in enumerate(filter_windows(grad_filtered, taps, d == 0)):
            grad_x = grad_x + tap_weight[j, d] * window
    grad_x = grad_x.astype(bf16)
    grad_projected = (
        jnp.concatenate([grad_x, grad_gate_half], axis=2).reshape(rows, 2 * mine)
    )
    mixed_part = dot_cols(grad_projected, own_in).astype(bf16).reshape(slots, length, model)
    grad_mixed_in = lax.psum_scatter(mixed_part, "seq", scatter_dimension=1, tiled=True)
    wide_part = mixed_part.astype(f32)
    grad_modulation_part = jnp.concatenate(
        [
            jnp.sum(wide_part, axis=1),
            jnp.sum(wide_part * (centered * spread), axis=1),
            jnp.sum(valid * own_cotangent * branch_part.astype(f32), axis=1),
        ],
        axis=1,
    )
    grad_in = dot_rows(mixed_in, grad_x.reshape(rows, mine)).astype(bf16)
    branch = branch_part.astype(f32)
    output = (tokens.astype(f32) + valid * gate * branch).astype(bf16)
    small = jnp.concatenate(
        [
            grad_delta,
            jnp.swapaxes(grad_decay, 0, 1),
            jnp.stack(grad_taps, 1),
            jnp.stack(grad_tap_bias)[None],
            grad_step_bias[None],
            grad_skip[None],
        ],
        axis=0,
    )
    small_rows = small.shape[0]
    share = -(-small_rows // (16 * peers)) * 16
    small = jnp.pad(
        small.astype(bf16).reshape(small_rows, 2 * mine), ((0, peers * share - small_rows), (0, 0))
    )
    grad_select = jnp.concatenate(grad_select, axis=1).astype(bf16)
    cuts = [rank, states, taps, 1, 1, 1]
    grad_modulation, *results = weight_sums(
        grad_modulation_part,
        grad_in.reshape(shares, peers, share_rows, mine),
        gate_in,
        small.reshape(peers, share, 2 * mine),
        grad_select.reshape(peers, mine // peers, 2 * select),
        cuts,
    )
    grad_modulation, grad_mixed_in = lax.optimization_barrier((grad_modulation, grad_mixed_in))
    grad_mixed_in = grad_mixed_in.astype(f32)
    grad_modulation = grad_modulation.reshape(-1, 3 * model)
    own_source = tokens.astype(f32)
    own_centered = own_source - jnp.mean(own_source, axis=-1, keepdims=True)
    own_spread = lax.rsqrt(
        jnp.mean(own_centered * own_centered, axis=-1, keepdims=True) + epsilon
    )
    normed = own_centered * own_spread
    grad_normed = grad_mixed_in * (1.0 + scale)
    grad_source = own_spread * (
        grad_normed
        - jnp.mean(grad_normed, axis=-1, keepdims=True)
        - normed * jnp.mean(grad_normed * normed, axis=-1, keepdims=True)
    )
    grad_tokens = (own_cotangent + grad_source).astype(bf16)
    grad_modulation_weight = lax.dot_general(
        own_features.astype(f32),
        grad_modulation,
        (((0,), (0,)), ((), ())),
        precision=lax.Precision.HIGHEST,
        preferred_element_type=f32,
    )
    if mine % lanes == 0:
        grad_in, grad_select, *small = results
    else:
        grad_in, small, grad_select = results
        grad_in = jnp.stack([grad_in, gate_in]).reshape(2, peers, shares, share_rows, mine)
        grad_in = jnp.transpose(grad_in, (1, 3, 0, 2, 4)).reshape(peers * share_rows, 2 * inner)
        grad_in = grad_in.astype(f32)
        small = small.reshape(peers, shares, share, 2, mine)
        small = jnp.transpose(small, (0, 2, 3, 1, 4)).reshape(peers * share, 2 * inner).astype(f32)
        ends = [sum(cuts[: i + 1]) for i in range(len(cuts))]
        small = [small[end - cut : end] for cut, end in zip(cuts, ends)]
        grad_select = grad_select.reshape(mine, 2 * select).astype(f32)
    return (
        output,
        grad_tokens,
        grad_in,
        grad_out,
        grad_select,
        grad_modulation_weight,
        small[0],
        small[2],
        small[3].reshape(-1),
        small[4].reshape(-1),
        small[1],
        small[5].reshape(-1),
        jnp.sum(grad_modulation, axis=0),
    )


def solution(mesh):
    tokens, rows, same = P("item", "seq", None), P("seq", None), P()
    return jax.shard_map(
        per_device,
        mesh=mesh,
        in_specs=(tokens, same, same, same, tokens, rows, rows, rows, rows) + (same,) * 7,
        out_specs=(tokens, tokens, rows, rows, rows, rows) + (same,) * 7,
        check_vma=False,
    )
```

```python
import functools
import math

import jax
import jax.numpy as jnp
from jax import lax
from jax.experimental import pallas as pl
from jax.experimental.pallas import tpu as pltpu
from jax.sharding import PartitionSpec as P

epsilon = 1e-06
log2e = 1.4426950408889634
ln2 = 0.6931471805599453
chunk = 16
lanes = 128
f32 = jnp.float32
bf16 = jnp.bfloat16


def silu_slope(v):
    s = jax.nn.sigmoid(v)
    return s * (1.0 + v * (1.0 - s))


def dot_rows(a, b):
    return lax.dot_general(a, b, (((0,), (0,)), ((), ())), preferred_element_type=f32)


def dot_cols(a, b):
    return lax.dot_general(a, b, (((1,), (1,)), ((), ())), preferred_element_type=f32)


def fold_sublanes(parts):
    outs = []
    for first in range(0, len(parts), 8):
        cur = parts[first : first + 8]
        row = lax.broadcasted_iota(jnp.int32, cur[0].shape, 0)
        for hop in (4, 2, 1):
            keep = (row // hop) % 2 == 0
            half = len(cur) // 2
            merged = []
            for j in range(half):
                a, b = cur[j], cur[j + half]
                x, y = jnp.where(keep, a, b), jnp.where(keep, b, a)
                if hop == 4:
                    moved = pltpu.roll(y, 4, 0)
                else:
                    moved = jnp.where(keep, pltpu.roll(y, 8 - hop, 0), pltpu.roll(y, hop, 0))
                merged.append(x + moved)
            cur = merged
        outs.append(cur[0])
    return jnp.concatenate(outs, axis=0)


def wide(v, groups):
    return v if groups == 1 else jnp.concatenate([v] * groups, axis=1)


def spread_matrix():
    rows = lax.broadcasted_iota(jnp.int32, (2 * chunk, 2 * lanes), 0) // chunk
    cols = lax.broadcasted_iota(jnp.int32, (2 * chunk, 2 * lanes), 1) // lanes
    return (rows == cols).astype(f32).astype(bf16)


def chunk_sweep(count, body, spread, first, second):
    spread(0, first)
    if count == 1:
        body(0, first)
        return

    def pair(k, carry):
        spread(2 * k + 1, second)
        body(2 * k, first)
        spread(jnp.minimum(2 * k + 2, count - 1), first)
        body(2 * k + 1, second)
        return carry

    lax.fori_loop(0, count // 2, pair, 0)


def place_coefficients(selection, copies):
    placed = jnp.dot(selection, copies, preferred_element_type=f32)
    row = lax.rem(lax.broadcasted_iota(jnp.int32, placed.shape, 0), chunk)
    span = placed.shape[1] // 2
    col = lax.rem(lax.broadcasted_iota(jnp.int32, placed.shape, 1), span) // (span // chunk)
    return jnp.where(row == col, placed, 0.0).astype(bf16)


def softplus(v):
    return jnp.maximum(v, 0.0) + jnp.log1p(jnp.exp(-jnp.abs(v)))


def states_kernel(
    count,
    sel_ref,
    x_ref,
    w_ref,
    bias_ref,
    r_ref,
    copies_ref,
    skip_ref,
    y_ref,
    h_ref,
    dt_ref,
    bc_ref,
    state,
    even,
    odd,
):
    slots, width = dt_ref.shape[1], dt_ref.shape[3]
    groups = width // lanes
    states = r_ref.shape[1]

    @pl.when(pl.program_id(1) == 0)
    def _():
        state[...] = jnp.zeros_like(state)

    for s in range(slots):
        selection = sel_ref[0, s]
        dt_ref[0, s] = softplus(
            jnp.dot(selection, w_ref[0], preferred_element_type=f32) + bias_ref[0]
        )
        bc_ref[0, s] = place_coefficients(selection, copies_ref[...])

    def one_direction(reverse):
        mix = spread_matrix()

        def place(i):
            return (count - 1 - i) if reverse else i

        def spread(i, into):
            start = pl.multiple_of(place(i) * chunk, chunk)
            for s in range(slots):
                both = bc_ref[0, s, pl.ds(start, chunk), :]
                span = both.shape[1] // 2
                into[s] = dot_rows(jnp.concatenate([both[:, :span], both[:, span:]], axis=0), mix)

        def body(i, held):
            start = pl.multiple_of(place(i) * chunk, chunk)
            order = range(chunk - 1, -1, -1) if reverse else range(chunk)
            for s in range(slots):
                h = state[s]
                rate = r_ref[0]
                dt = dt_ref[0, s, pl.ds(start, chunk), :]
                x = x_ref[0, s, pl.ds(start, chunk), :].astype(f32)
                u = dt * x
                kept, sums = [None] * chunk, [None] * chunk
                for t in order:
                    rows = slice(t * states, (t + 1) * states)
                    b = wide(held[s, rows, :lanes], groups)
                    c = wide(held[s, rows, lanes:], groups)
                    h = jnp.exp2(dt[t : t + 1] * rate) * h + u[t : t + 1] * b
                    kept[t] = h.astype(bf16)
                    p = h * c
                    sums[t] = p[:8] + p[8:]
                size = chunk * states
                h_ref[0, s, pl.ds(pl.multiple_of(start * states, size), size), :] = jnp.concatenate(
                    kept, axis=0
                )
                y = fold_sublanes(sums) + skip_ref[0] * x
                y_ref[0, s, pl.ds(start, chunk), :] = y.astype(bf16)
                state[s] = h

        chunk_sweep(count, body, spread, even, odd)

    for d in range(2):

        @pl.when(pl.program_id(0) == d)
        def _():
            one_direction(d == 1)


def side_exchange(b_ref, q_ref, b_out, q_out, b_box, q_box, q_stage, *sems):
    b_keep, q_keep, o_keep, p_keep = sems[:4]
    (i_send, i_recv, j_send, j_recv, a_send, a_recv, z_send, z_recv, f_send, f_recv) = sems[4:]
    shares, peers = q_ref.shape[0], q_ref.shape[1]
    me, item = lax.axis_index("seq"), lax.axis_index("item")
    step = pl.program_id(0) * pl.num_programs(1) + pl.program_id(1)
    quarter = pl.num_programs(0) * pl.num_programs(1) // 4

    def other(t):
        return lax.rem(item + t, peers)

    def origin(t):
        return lax.rem(item - t + peers, peers)

    def ahead(k):
        return lax.rem(me + k, shares)

    def behind(k):
        return lax.rem(me - k + shares, shares)

    def own_b():
        return pltpu.make_async_copy(b_ref.at[item], b_box.at[0], b_keep)

    def own_q():
        return pltpu.make_async_copy(q_ref.at[:, item], q_box.at[0], q_keep)

    def share_b(t):
        return remote(b_ref.at[other(t)], b_box.at[t], i_send, i_recv, t - 1, "item", other(t))

    def share_q(t):
        return remote(q_ref.at[:, other(t)], q_box.at[t], a_send, a_recv, t - 1, "item", other(t))

    def keep_b():
        return pltpu.make_async_copy(b_box.at[0], b_out.at[item], o_keep)

    def keep_q():
        return pltpu.make_async_copy(q_stage.at[me], q_out.at[item, me], p_keep)

    def give_b(t):
        return remote(b_box.at[0], b_out.at[item], j_send, j_recv, t - 1, "item", other(t))

    def place_q(k):
        return remote(
            q_stage.at[ahead(k)], q_out.at[item, me], z_send, z_recv, k, "seq", ahead(k)
        )

    def forward_q(k, t):
        source = q_stage.at[me] if isinstance(k, int) else q_out.at[item, behind(k)]
        return remote(
            source,
            q_out.at[item, behind(k)],
            f_send,
            f_recv,
            k * (peers - 1) + t - 1,
            "item",
            other(t),
        )

    @pl.when(step == 0)
    def _():
        greet((("seq", me, shares), ("item", item, peers)))
        each(1, peers, lambda t: share_q(t).start())
        each(1, peers, lambda t: share_b(t).start())
        own_b().start()
        own_q().start()

    @pl.when(step == quarter)
    def _():
        own_q().wait()
        own_b().wait()

        def arrived(t):
            share_q(t).wait_recv()
            share_b(t).wait_recv()

        each(1, peers, arrived)

        def sum_q(p):
            def add(t, total):
                return total + q_box[t, p].astype(f32)

            q_stage[p] = lax.fori_loop(1, peers, add, q_box[0, p].astype(f32)).astype(bf16)

        each(0, shares, sum_q)
        rows = 16 if b_box.shape[1] % 16 == 0 else b_box.shape[1]

        def sum_b(r):
            place = pl.ds(pl.multiple_of(r * rows, rows), rows)

            def add(t, total):
                return total + b_box[t, place, :].astype(f32)

            total = lax.fori_loop(1, peers, add, b_box[0, place, :].astype(f32))
            b_box[0, place, :] = total.astype(bf16)

        each(0, b_box.shape[1] // rows, sum_b)
        each(1, shares, lambda k: place_q(k).start())
        each(1, peers, lambda t: forward_q(0, t).start())
        each(1, peers, lambda t: give_b(t).start())
        keep_b().start()
        keep_q().start()

    @pl.when(step == 2 * quarter)
    def _():
        def pass_on(k):
            block = q_out.at[item, behind(k)]
            remote(block, block, z_send, z_recv, k, "seq", behind(k)).wait_recv()
            each(1, peers, lambda t: forward_q(k, t).start())

        each(1, shares, pass_on)

    @pl.when(step == 3 * quarter)
    def _():
        keep_b().wait()
        keep_q().wait()

        def finish(t):
            block = b_out.at[origin(t)]
            remote(block, block, j_send, j_recv, t - 1, "item", other(t)).wait_recv()
            give_b(t).wait_send()
            share_b(t).wait_send()
            share_q(t).wait_send()

        each(1, peers, finish)

        def finish_q(k):
            def one(t):
                block = q_out.at[origin(t), behind(k)]
                remote(
                    block, block, f_send, f_recv, k * (peers - 1) + t - 1, "item", other(t)
                ).wait_recv()
                forward_q(k, t).wait_send()

            each(1, peers, one)

        each(0, shares, finish_q)
        each(1, shares, lambda k: place_q(k).wait_send())


def adjoint_kernel(
    count,
    bc_ref,
    x_ref,
    w_ref,
    r_ref,
    copies_ref,
    skip_ref,
    dt_ref,
    g_ref,
    h_ref,
    edge_ref,
    b_ref,
    q_ref,
    low_ref,
    input_ref,
    gsel_ref,
    decay_ref,
    sums_ref,
    b_out,
    q_out,
    pending,
    coefs,
    even,
    odd,
    *side,
):
    slots, width = dt_ref.shape[1], dt_ref.shape[3]
    groups = width // lanes
    states = r_ref.shape[1]
    last_block = pl.program_id(1) == pl.num_programs(1) - 1

    side_exchange(b_ref, q_ref, b_out, q_out, *side)

    @pl.when(pl.program_id(1) == 0)
    def _():
        pending[...] = jnp.zeros_like(pending)
        decay_ref[...] = jnp.zeros_like(decay_ref)
        sums_ref[...] = jnp.zeros_like(sums_ref)

    def one_direction(reverse):
        mix = spread_matrix()
        picks = (
            lax.broadcasted_iota(jnp.int32, (8, 2 * lanes), 0)
            == lax.broadcasted_iota(jnp.int32, (8, 2 * lanes), 1) // lanes
        ).astype(f32).astype(bf16)

        def place(i):
            return i if reverse else (count - 1 - i)

        def spread(i, into):
            start = pl.multiple_of(place(i) * chunk, chunk)
            for s in range(slots):
                both = bc_ref[0, s, pl.ds(start, chunk), :]
                span = both.shape[1] // 2
                into[s] = dot_rows(jnp.concatenate([both[:, :span], both[:, span:]], axis=0), mix)

        def body(i, held):
            here = place(i)
            start = pl.multiple_of(here * chunk, chunk)
            order = range(chunk) if reverse else range(chunk - 1, -1, -1)
            size = chunk * states
            base = pl.multiple_of(start * states, size)
            at_end = here == (count - 1 if reverse else 0)
            outer = jnp.where(last_block, 0.0, 1.0)
            near = pl.multiple_of(
                jnp.clip(start + (chunk if reverse else -1), 0, count * chunk - 1) * states, states
            )
            for s in range(slots):
                pend = pending[s]
                rate = r_ref[0]
                dt = dt_ref[0, s, pl.ds(start, chunk), :]
                x = x_ref[0, s, pl.ds(start, chunk), :].astype(f32)
                g = g_ref[s, pl.ds(start, chunk), :].astype(f32)
                u = dt * x
                before = jnp.where(
                    at_end,
                    edge_ref[0, s].astype(f32) * outer,
                    h_ref[0, s, pl.ds(near, states), :].astype(f32),
                )
                total = decay_ref[0, s]
                rate_sums, into_sums = [None] * chunk, [None] * chunk
                coef = [None] * chunk
                hidden = h_ref[0, s, pl.ds(base, size), :]
                now = hidden[order[0] * states : (order[0] + 1) * states].astype(f32)
                for k, t in enumerate(order):
                    rows = slice(t * states, (t + 1) * states)
                    b = wide(held[s, rows, :lanes], groups)
                    c = wide(held[s, rows, lanes:], groups)
                    if k + 1 < chunk:
                        q = order[k + 1]
                        prev = hidden[q * states : (q + 1) * states].astype(f32)
                    else:
                        prev = before
                    gt = g[t : t + 1]
                    adj = c * gt + pend
                    pend = jnp.exp2(dt[t : t + 1] * rate) * adj
                    through = pend * prev * rate
                    total = total + through * dt[t : t + 1]
                    rate_sums[t] = through[:8] + through[8:]
                    w = adj * b
                    into_sums[t] = w[:8] + w[8:]
                    cb, cc = adj * u[t : t + 1], now * gt
                    sb, sc = cb[:, :lanes], cc[:, :lanes]
                    for j in range(1, groups):
                        sb = sb + cb[:, j * lanes : (j + 1) * lanes]
                        sc = sc + cc[:, j * lanes : (j + 1) * lanes]
                    coef[t] = jnp.concatenate([sb, sc], axis=1).astype(bf16)
                    now = prev
                pending[s] = pend
                decay_ref[0, s] = total
                weighted = fold_sublanes(into_sums)
                few = dt * (1.0 - dt * (0.5 - dt * (1.0 / 6.0 - dt * (1.0 / 24.0))))
                slope = jnp.where(dt < 0.03, few, 1.0 - jnp.exp(-dt))
                grad_pre = (fold_sublanes(rate_sums) * ln2 + weighted * x) * slope
                low_ref[0, s, pl.ds(start, chunk), :] = grad_pre.astype(bf16)
                direct = weighted * dt + skip_ref[0] * g
                input_ref[0, s, pl.ds(start, chunk), :] = direct.astype(bf16)
                gx = g * x
                sums_ref[0] += jnp.concatenate(
                    [grad_pre[:8] + grad_pre[8:], gx[:8] + gx[8:]], axis=0
                )
                coefs[s, pl.ds(pl.multiple_of(here * 8, 8), 8), :] = dot_cols(
                    picks, jnp.concatenate(coef, axis=0)
                )

        chunk_sweep(count, body, spread, even, odd)

    for d in range(2):

        @pl.when(pl.program_id(0) == d)
        def _():
            one_direction(d == 1)


    own = lax.broadcasted_iota(jnp.int32, (chunk, chunk * states), 0) == (
        lax.broadcasted_iota(jnp.int32, (chunk, chunk * states), 1) // states
    )
    for s in range(slots):
        placed = []
        for c in range(count):
            placed.append(
                jnp.concatenate(
                    [
                        jnp.where(own, coefs[s, c * 8 + k : c * 8 + k + 1, :], 0.0)
                        for k in range(2)
                    ],
                    axis=1,
                )
            )
        placed = jnp.concatenate(placed, axis=0).astype(bf16)
        gsel_ref[0, s] = (
            dot_cols(low_ref[0, s], w_ref[0]) + dot_cols(placed, copies_ref[...])
        ).astype(bf16)


def block_of(length):
    return math.gcd(length, 256)


def scan_states(selection, x, weight, bias, rate, copies, skip):
    two, slots, length, width = x.shape
    select = selection.shape[3]
    states = rate.shape[1]
    hidden_size = two * slots * length * states * width
    block = block_of(length)
    blocks = length // block
    spread = copies.shape[1]

    def where(d, i):
        return (d, 0, jnp.where(d == 1, blocks - 1 - i, i), 0)

    def by_direction(d, i):
        return (d, 0, 0)

    return pl.pallas_call(
        functools.partial(states_kernel, block // chunk),
        grid=(two, blocks),
        in_specs=[
            pl.BlockSpec((1, slots, block, select), where),
            pl.BlockSpec((1, slots, block, width), where),
            pl.BlockSpec((1, select, width), by_direction),
            pl.BlockSpec((1, 1, width), by_direction),
            pl.BlockSpec((1, states, width), by_direction),
            pl.BlockSpec((select, spread), lambda d, i: (0, 0)),
            pl.BlockSpec((1, 1, width), by_direction),
        ],
        out_specs=[
            pl.BlockSpec((1, slots, block, width), where),
            pl.BlockSpec((1, slots, block * states, width), where),
            pl.BlockSpec((1, slots, block, width), where),
            pl.BlockSpec((1, slots, block, spread), where),
        ],
        out_shape=[
            jax.ShapeDtypeStruct((two, slots, length, width), bf16),
            jax.ShapeDtypeStruct((two, slots, length * states, width), bf16),
            jax.ShapeDtypeStruct((two, slots, length, width), f32),
            jax.ShapeDtypeStruct((two, slots, length, spread), bf16),
        ],
        scratch_shapes=[
            pltpu.VMEM((slots, states, width), f32),
            pltpu.VMEM((slots, chunk * states, 2 * lanes), f32),
            pltpu.VMEM((slots, chunk * states, 2 * lanes), f32),
        ],
        compiler_params=pltpu.CompilerParams(vmem_limit_bytes=48 * 2**20),
        cost_estimate=pl.CostEstimate(
            flops=64 * 10**9, bytes_accessed=80 * 2**20, transcendentals=hidden_size
        ),
        name="scan_states",
    )(selection, x, weight, bias, rate, copies, skip)


def scan_adjoint(bc, x, weight, rate, copies, skip, dt, g, h, b, q):
    two, slots, length, width = dt.shape
    select = weight.shape[1]
    states = rate.shape[1]
    hidden_size = two * slots * length * states * width
    block = block_of(length)
    blocks = length // block
    spread = copies.shape[1]
    shares, peers = q.shape[:2]
    anywhere, dma = pl.BlockSpec(memory_space=pl.ANY), pltpu.SemaphoreType.DMA

    def at(d, i):
        return jnp.where(d == 1, i, blocks - 1 - i)

    def where(d, i):
        return (d, 0, at(d, i), 0)

    def edge(d, i):
        mine = at(d, i) * block
        return (d, 0, jnp.clip(jnp.where(d == 1, mine + block, mine - 1), 0, length - 1), 0)

    def by_direction(d, i):
        return (d, 0, 0)

    return pl.pallas_call(
        functools.partial(adjoint_kernel, block // chunk),
        grid=(two, blocks),
        in_specs=[
            pl.BlockSpec((1, slots, block, spread), where),
            pl.BlockSpec((1, slots, block, width), where),
            pl.BlockSpec((1, select, width), by_direction),
            pl.BlockSpec((1, states, width), by_direction),
            pl.BlockSpec((select, spread), lambda d, i: (0, 0)),
            pl.BlockSpec((1, 1, width), by_direction),
            pl.BlockSpec((1, slots, block, width), where),
            pl.BlockSpec((slots, block, width), lambda d, i: (0, at(d, i), 0)),
            pl.BlockSpec((1, slots, block * states, width), where),
            pl.BlockSpec((1, slots, states, width), edge),
            anywhere,
            anywhere,
        ],
        out_specs=[
            pl.BlockSpec((1, slots, block, width), where),
            pl.BlockSpec((1, slots, block, width), where),
            pl.BlockSpec((1, slots, block, select), where),
            pl.BlockSpec((1, slots, states, width), lambda d, i: (d, 0, 0, 0)),
            pl.BlockSpec((1, 16, width), by_direction),
            anywhere,
            anywhere,
        ],
        out_shape=[
            jax.ShapeDtypeStruct((two, slots, length, width), bf16),
            jax.ShapeDtypeStruct((two, slots, length, width), bf16),
            jax.ShapeDtypeStruct((two, slots, length, select), bf16),
            jax.ShapeDtypeStruct((two, slots, states, width), f32),
            jax.ShapeDtypeStruct((two, 16, width), f32),
            jax.ShapeDtypeStruct(b.shape, bf16),
            jax.ShapeDtypeStruct((peers, shares) + q.shape[2:], bf16),
        ],
        scratch_shapes=[
            pltpu.VMEM((slots, states, width), f32),
            pltpu.VMEM((slots, block // chunk * 8, chunk * states), f32),
            pltpu.VMEM((slots, chunk * states, 2 * lanes), f32),
            pltpu.VMEM((slots, chunk * states, 2 * lanes), f32),
            pltpu.VMEM(b.shape, bf16),
            pltpu.VMEM((peers, shares) + q.shape[2:], bf16),
            pltpu.VMEM((shares,) + q.shape[2:], bf16),
        ]
        + [dma] * 4
        + [dma((peers - 1,))] * 6
        + [dma((shares,))] * 2
        + [dma((shares * (peers - 1),))] * 2,
        compiler_params=pltpu.CompilerParams(
            collective_id=6, has_side_effects=True, vmem_limit_bytes=48 * 2**20
        ),
        cost_estimate=pl.CostEstimate(
            flops=100 * 10**9, bytes_accessed=100 * 2**20, transcendentals=hidden_size
        ),
        name="scan_adjoint",
    )(bc, x, weight, rate, copies, skip, dt, g, h, h, b, q)


def coefficient_copies(width, rank, states):
    span = chunk * states
    col = jnp.arange(2 * span)
    origin = rank + (col // span) * states + col % states
    return (jnp.arange(width)[:, None] == origin[None, :]).astype(bf16)


def widen(v, width):
    short = width - v.shape[-1]
    return v if short == 0 else jnp.pad(v, ((0, 0),) * (v.ndim - 1) + ((0, short),))


def remote(src, dst, sends, recvs, slot, axis, to):
    return pltpu.make_async_remote_copy(
        src_ref=src,
        dst_ref=dst,
        send_sem=sends.at[slot],
        recv_sem=recvs.at[slot],
        device_id={axis: to},
        device_id_type=pl.DeviceIdType.MESH,
    )


def each(first, last, body):
    def run(k, carry):
        body(k)
        return carry

    lax.fori_loop(first, last, run, 0)


def greet(peers):
    barrier = pltpu.get_barrier_semaphore()
    total = 0
    for axis, me, count in peers:

        def hello(k):
            pl.semaphore_signal(
                barrier,
                inc=1,
                device_id={axis: lax.rem(me + k, count)},
                device_id_type=pl.DeviceIdType.MESH,
            )

        each(1, count, hello)
        total += count - 1
    pl.semaphore_wait(barrier, total)


def total_kernel(line, produce, v_ref, o_ref, pairbox, stage, inbox, *sems):
    pair_send, pair_recv, sum_send, sum_recv, out_send, out_recv, fwd_send, fwd_recv = sems
    me = lax.axis_index("seq")
    pos, core = me // 2, lax.rem(me, 2)
    partner = me + 1 - 2 * core
    barrier = pltpu.get_barrier_semaphore()

    def hello(to):
        pl.semaphore_signal(
            barrier, inc=1, device_id={"seq": to}, device_id_type=pl.DeviceIdType.MESH
        )

    hello(partner)
    each(1, line, lambda k: hello(lax.rem(pos + k, line) * 2 + core))
    pl.semaphore_wait(barrier, line)

    pair = remote(v_ref.at[:, :, 1 - core], pairbox, pair_send, pair_recv, 0, "seq", partner)
    if produce is not None:
        produce(1 - core)
    pair.start()
    if produce is not None:
        produce(core)
    pair.wait_recv()

    def own(q):
        return v_ref[:, q, core].astype(f32) + pairbox[:, q].astype(f32)

    def summand(k):
        q = lax.rem(pos + k, line)
        return remote(
            stage.at[q], inbox.at[pos], sum_send, sum_recv, k - 1, "seq", q * 2 + core
        )

    def send(k):
        q = lax.rem(pos + k, line)
        stage[q] = own(q).astype(bf16)
        summand(k).start()

    each(1, line, send)

    def source(k):
        return lax.rem(pos - k + line, line)

    def arrived(k, total):
        q = source(k)
        remote(stage.at[q], inbox.at[q], sum_send, sum_recv, k - 1, "seq", partner).wait_recv()
        return total + inbox[q].astype(f32)

    total = lax.fori_loop(1, line, arrived, own(pos))
    o_ref[:, pos, core] = total.astype(bf16)

    def result(k):
        mine = o_ref.at[:, pos, core]
        return remote(
            mine, mine, out_send, out_recv, k - 1, "seq", lax.rem(pos + k, line) * 2 + core
        )

    def forward(k):
        block = o_ref.at[:, source(k), core]
        return remote(block, block, fwd_send, fwd_recv, k, "seq", partner)

    each(1, line, lambda k: result(k).start())
    forward(0).start()

    def pass_on(k):
        block = o_ref.at[:, source(k), core]
        remote(block, block, out_send, out_recv, k - 1, "seq", partner).wait_recv()
        forward(k).start()

    each(1, line, pass_on)

    def finish(k):
        block = o_ref.at[:, source(k), 1 - core]
        remote(block, block, fwd_send, fwd_recv, k, "seq", partner).wait_recv()
        forward(k).wait_send()

    each(0, line, finish)
    pair.wait_send()

    def drain(k):
        summand(k).wait_send()
        result(k).wait_send()

    each(1, line, drain)


def summed_everywhere(v, call):
    batch, length, width = v.shape
    shares = lax.axis_size("seq")
    line, rows = shares // 2, length // shares
    vmem = pl.BlockSpec(memory_space=pltpu.VMEM)
    dma = pltpu.SemaphoreType.DMA
    blocks = v.reshape(batch, line, 2, rows, width)
    out = pl.pallas_call(
        functools.partial(total_kernel, line, None),
        in_specs=[vmem],
        out_specs=vmem,
        out_shape=jax.ShapeDtypeStruct(blocks.shape, bf16),
        scratch_shapes=[
            pltpu.VMEM((batch, line, rows, width), bf16),
            pltpu.VMEM((line, batch, rows, width), bf16),
            pltpu.VMEM((line, batch, rows, width), bf16),
            dma((1,)),
            dma((1,)),
            dma((line,)),
            dma((line,)),
            dma((line,)),
            dma((line,)),
            dma((line,)),
            dma((line,)),
        ],
        compiler_params=pltpu.CompilerParams(
            collective_id=call, has_side_effects=True, vmem_limit_bytes=40 * 2**20
        ),
        cost_estimate=pl.CostEstimate(flops=25 * 10**9, bytes_accessed=2**20, transcendentals=0),
        name="sum_" + str(call),
    )(blocks)
    return out.reshape(v.shape)


def filter_kernel(line, x_ref, tap_ref, bias_ref, select_ref, o_ref, a_ref, padded, v_ref, *rest):
    slots, length, width = x_ref.shape
    taps = tap_ref.shape[1]
    rows = v_ref.shape[3]
    rim = 8
    edge = jnp.zeros((slots, rim, width), f32)
    padded[:, :rim, :] = edge
    padded[:, rim + length :, :] = edge
    padded[:, rim : rim + length, :] = x_ref[...].astype(f32)

    def produce(core):
        def block(q):
            start = pl.multiple_of((q * 2 + core) * rows, rows)
            for s in range(slots):
                near = padded[s, pl.ds(start, rows + 2 * rim), :]
                for d in range(2):
                    total = bias_ref[d]
                    for j in range(taps):
                        first = rim + (taps - 1 - j if d == 1 else j - taps + 1)
                        total = total + tap_ref[d, j : j + 1, :] * near[first : first + rows]
                    active = (total / (1.0 + jnp.exp(-total))).astype(bf16)
                    a_ref[d, s, pl.ds(start, rows), :] = active
                    v_ref[d * slots + s, q, core] = jnp.dot(
                        active, select_ref[d], preferred_element_type=f32
                    ).astype(bf16)

        each(0, line, block)

    total_kernel(line, produce, v_ref, o_ref, *rest)


def filter_and_select(x, taps, bias, select):
    slots, length, width = x.shape
    batch, columns = 2 * slots, select.shape[2]
    shares = lax.axis_size("seq")
    line, rows = shares // 2, length // shares
    vmem = pl.BlockSpec(memory_space=pltpu.VMEM)
    dma = pltpu.SemaphoreType.DMA
    blocks = (batch, line, 2, rows, columns)
    out, active = pl.pallas_call(
        functools.partial(filter_kernel, line),
        in_specs=[vmem] * 4,
        out_specs=[vmem] * 2,
        out_shape=[
            jax.ShapeDtypeStruct(blocks, bf16),
            jax.ShapeDtypeStruct((2, slots, length, width), bf16),
        ],
        scratch_shapes=[
            pltpu.VMEM((slots, length + 16, width), f32),
            pltpu.VMEM(blocks, bf16),
            pltpu.VMEM((batch, line, rows, columns), bf16),
            pltpu.VMEM((line, batch, rows, columns), bf16),
            pltpu.VMEM((line, batch, rows, columns), bf16),
        ]
        + [dma((1,))] * 2
        + [dma((line,))] * 6,
        compiler_params=pltpu.CompilerParams(
            collective_id=4, has_side_effects=True, vmem_limit_bytes=40 * 2**20
        ),
        cost_estimate=pl.CostEstimate(flops=30 * 10**9, bytes_accessed=2**20, transcendentals=0),
        name="filter_and_select",
    )(x, taps, bias, select)
    return out.reshape(batch, length, columns), active


def head_kernel(line, t_ref, w_ref, mod_ref, all_ref, box_ref, out_ref, parts, *sems):
    keep, t_keep, u_send, u_recv, d_send, d_recv, p_send, p_recv = sems[:8]
    w_send, w_recv, f_send, f_recv, m_send, m_recv = sems[8:]
    shares, peers = box_ref.shape[0], box_ref.shape[1]
    slots, local = t_ref.shape[0], t_ref.shape[1]
    me, item = lax.axis_index("seq"), lax.axis_index("item")
    pos, core = me // 2, lax.rem(me, 2)
    partner = me + 1 - 2 * core
    greet((("seq", me, shares), ("item", item, peers)))

    def region(q, c, s):
        first = pl.multiple_of((q * 2 + c) * local, local)
        return all_ref.at[s, pl.ds(first, local), :]

    def hop(q, s, source, sends, recvs, k, to):
        return remote(source, region(q, core, s), sends, recvs, k * slots + s, "seq", to)

    def up(k, s):
        source = t_ref.at[s] if isinstance(k, int) else region(pos - k, core, s)
        return hop(pos - k, s, source, u_send, u_recv, k, me + 2)

    def down(k, s):
        source = t_ref.at[s] if isinstance(k, int) else region(pos + k, core, s)
        return hop(pos + k, s, source, d_send, d_recv, k, me - 2)

    def across(q, s):
        return remote(
            region(q, core, s), region(q, core, s), p_send, p_recv, q * slots + s, "seq", partner
        )

    def own_across(s):
        return remote(
            t_ref.at[s], region(pos, core, s), p_send, p_recv, pos * slots + s, "seq", partner
        )

    not_last, not_first = pos < line - 1, pos > 0
    for s in range(slots):

        @pl.when(not_last)
        def _():
            up(0, s).start()

        @pl.when(not_first)
        def _():
            down(0, s).start()

    def modulation(k):
        return remote(
            mod_ref, parts.at[k - 1], m_send, m_recv, k - 1, "seq", lax.rem(me + k, shares)
        )

    def weight(k):
        to = lax.rem(me + k, shares)
        return remote(w_ref.at[to], box_ref.at[me, item], w_send, w_recv, k, "seq", to)

    each(1, shares, lambda k: modulation(k).start())
    each(1, shares, lambda k: weight(k).start())
    own = pltpu.make_async_copy(w_ref.at[me], box_ref.at[me, item], keep)
    own.start()
    kept = []
    for s in range(slots):
        own_across(s).start()
        kept.append(pltpu.make_async_copy(t_ref.at[s], region(pos, core, s), t_keep.at[s]))
        kept[-1].start()

    def forward(k, t):
        block = box_ref.at[lax.rem(me - k + shares, shares), item]
        return remote(
            block, block, f_send, f_recv, k * (peers - 1) + t - 1, "item", lax.rem(item + t, peers)
        )

    def pass_on(k):
        source = lax.rem(me - k + shares, shares)
        block = box_ref.at[source, item]
        remote(block, block, w_send, w_recv, k, "seq", source).wait_recv()
        each(1, peers, lambda t: forward(k, t).start())

    def relay(k):
        for s in range(slots):

            @pl.when(k < pos)
            def _():
                q = pos - 1 - k
                hop(q, s, region(q, core, s), u_send, u_recv, k, partner).wait_recv()

                @pl.when(not_last)
                def _():
                    up(k + 1, s).start()

                across(q, s).start()

            @pl.when(k < line - 1 - pos)
            def _():
                q = pos + 1 + k
                hop(q, s, region(q, core, s), d_send, d_recv, k, partner).wait_recv()

                @pl.when(not_first)
                def _():
                    down(k + 1, s).start()

                across(q, s).start()

    own.wait()
    each(1, peers, lambda t: forward(0, t).start())
    half = shares // 2
    each(1, half, pass_on)
    each(0, 1, relay)
    each(half, shares, pass_on)

    def add(k, total):
        modulation(k).wait_recv()
        return total + parts[k - 1]

    out_ref[...] = lax.fori_loop(1, shares, add, mod_ref[...])
    each(1, line - 1, relay)

    def finish(k):
        def one(t):
            source = lax.rem(item - t + peers, peers)
            block = box_ref.at[lax.rem(me - k + shares, shares), source]
            remote(
                block, block, f_send, f_recv, k * (peers - 1) + t - 1, "item", source
            ).wait_recv()
            forward(k, t).wait_send()

        each(1, peers, one)

    each(0, shares, finish)

    def drain(k):
        weight(k).wait_send()
        modulation(k).wait_send()

    each(1, shares, drain)

    def drain_tokens(q):
        for s in range(slots):
            remote(
                region(q, core, s),
                region(q, 1 - core, s),
                p_send,
                p_recv,
                q * slots + s,
                "seq",
                partner,
            ).wait_recv()
            across(q, s).wait_send()

    each(0, line, drain_tokens)

    def drain_line(k):
        for s in range(slots):

            @pl.when(not_last & (k <= pos))
            def _():
                up(k, s).wait_send()

            @pl.when(not_first & (k <= line - 1 - pos))
            def _():
                down(k, s).wait_send()

    each(0, line, drain_line)
    for copy in kept:
        copy.wait()


def gather_inputs(tokens, blocks, modulation):
    shares, peers = lax.axis_size("seq"), lax.axis_size("item")
    slots, local, model = tokens.shape
    line = shares // 2
    vmem, anywhere = pl.BlockSpec(memory_space=pltpu.VMEM), pl.BlockSpec(memory_space=pl.ANY)
    dma = pltpu.SemaphoreType.DMA
    return pl.pallas_call(
        functools.partial(head_kernel, line),
        in_specs=[anywhere, anywhere, vmem],
        out_specs=[anywhere, anywhere, vmem],
        out_shape=[
            jax.ShapeDtypeStruct((slots, local * shares, model), bf16),
            jax.ShapeDtypeStruct((shares, peers) + blocks.shape[1:], bf16),
            jax.ShapeDtypeStruct(modulation.shape, f32),
        ],
        scratch_shapes=[pltpu.VMEM((shares - 1,) + modulation.shape, f32), dma, dma((slots,))]
        + [dma((line * slots,))] * 6
        + [dma((shares,))] * 2
        + [dma((shares * (peers - 1),))] * 2
        + [dma((shares,))] * 2,
        compiler_params=pltpu.CompilerParams(collective_id=1, has_side_effects=True),
        cost_estimate=pl.CostEstimate(flops=60 * 10**9, bytes_accessed=2**20, transcendentals=0),
        name="gather_inputs",
    )(tokens, blocks, modulation)


def tail_kernel(cuts, m_ref, g_ref, gate_ref, small_ref, select_ref, m_out, *refs):
    if cuts is None:
        g_out, small_out, select_out, *refs = refs
    else:
        in_final, select_final, *refs = refs
        finals, refs = refs[: len(cuts)], refs[len(cuts) :]
        g_out, small_out, select_out, *refs = refs
    m_parts, g_box, small_box, select_box, g_stage, *sems = refs
    (a_send, a_recv, s_send, s_recv, c_send, c_recv, z_send, z_recv, y_send, y_recv) = sems[:10]
    f_send, f_recv, h_send, h_recv, e_send, e_recv = sems[10:16]
    m_send, m_recv, n_send, n_recv = sems[16:]
    shares, peers = g_ref.shape[0], g_ref.shape[1]
    me, item = lax.axis_index("seq"), lax.axis_index("item")
    greet((("seq", me, shares), ("item", item, peers)))

    def other(t):
        return lax.rem(item + t, peers)

    def origin(t):
        return lax.rem(item - t + peers, peers)

    def ahead(k):
        return lax.rem(me + k, shares)

    def behind(k):
        return lax.rem(me - k + shares, shares)

    def flat(k, t):
        return k * (peers - 1) + t - 1

    def share_small(t):
        return remote(
            small_ref.at[other(t)], small_box.at[t - 1], s_send, s_recv, t - 1, "item", other(t)
        )

    def share_select(t):
        return remote(
            select_ref.at[other(t)], select_box.at[t - 1], c_send, c_recv, t - 1, "item", other(t)
        )

    def share_in(k, t):
        p = ahead(k)
        return remote(
            g_ref.at[p, other(t)], g_box.at[t - 1, p], a_send, a_recv, flat(k, t), "item", other(t)
        )

    def part(k):
        return remote(m_ref, m_parts.at[k - 1], m_send, m_recv, k - 1, "seq", ahead(k))

    def forward_modulation(t):
        block = m_out.at[item]
        return remote(block, block, n_send, n_recv, t - 1, "item", other(t))

    each(1, shares, lambda k: part(k).start())
    each(1, peers, lambda t: share_small(t).start())
    each(1, shares, lambda k: each(1, peers, lambda t: share_in(k, t).start()))
    each(1, peers, lambda t: share_in(0, t).start())
    each(1, peers, lambda t: share_select(t).start())

    def add_small(t, total):
        share_small(t).wait_recv()
        return total + small_box[t - 1].astype(f32)

    small_out[item, me] = lax.fori_loop(
        1, peers, add_small, small_ref[item].astype(f32)
    ).astype(bf16)

    def spread_small(k):
        block = small_out.at[item, me]
        return remote(block, block, y_send, y_recv, k, "seq", ahead(k))

    each(1, shares, lambda k: spread_small(k).start())

    def sum_in(k):
        p = ahead(k)

        def add(t, total):
            share_in(k, t).wait_recv()
            return total + g_box[t - 1, p].astype(f32)

        return lax.fori_loop(1, peers, add, g_ref[p, item].astype(f32)).astype(bf16)

    def place_in(k):
        return remote(
            g_stage.at[k], g_out.at[item, me], z_send, z_recv, k, "seq", ahead(k)
        )

    def turn(k):
        g_stage[k] = sum_in(k)
        place_in(k).start()

    each(1, shares, turn)
    g_out[item, me] = sum_in(0)

    def forward_in(k, t):
        block = g_out.at[item, behind(k)]
        return remote(block, block, f_send, f_recv, flat(k, t), "item", other(t))

    def forward_small(k, t):
        block = small_out.at[item, behind(k)]
        return remote(block, block, h_send, h_recv, flat(k, t), "item", other(t))

    each(1, peers, lambda t: forward_in(0, t).start())
    each(1, peers, lambda t: forward_small(0, t).start())

    def add_part(k, total):
        part(k).wait_recv()
        return total + m_parts[k - 1].astype(f32)

    m_out[item] = lax.fori_loop(1, shares, add_part, m_ref[...].astype(f32))
    each(1, peers, lambda t: forward_modulation(t).start())

    def add_select(t, total):
        share_select(t).wait_recv()
        return total + select_box[t - 1].astype(f32)

    select_out[item] = lax.fori_loop(
        1, peers, add_select, select_ref[item].astype(f32)
    ).astype(bf16)

    def forward_select(t):
        block = select_out.at[item]
        return remote(block, block, e_send, e_recv, t - 1, "item", other(t))

    each(1, peers, lambda t: forward_select(t).start())

    def pass_on(k):
        block = g_out.at[item, behind(k)]
        remote(block, block, z_send, z_recv, k, "seq", behind(k)).wait_recv()
        each(1, peers, lambda t: forward_in(k, t).start())
        little = small_out.at[item, behind(k)]
        remote(little, little, y_send, y_recv, k, "seq", behind(k)).wait_recv()
        each(1, peers, lambda t: forward_small(k, t).start())

    each(1, shares, pass_on)

    def widen_half(block, half, j, s):
        rows, mine = block.shape
        inner = in_final.shape[1] // 2
        place = pl.ds(pl.multiple_of(j * rows, rows), rows)
        first = pl.multiple_of(s * mine + half * inner, lanes)
        in_final[place, pl.ds(first, mine)] = block.astype(f32)

    def widen_in(j, s):
        if cuts is not None:
            widen_half(g_out[j, s], 0, j, s)

    if cuts is not None:
        each(
            0,
            peers,
            lambda j: each(0, shares, lambda s: widen_half(gate_ref[j, s], 1, j, s)),
        )
    each(0, shares, lambda k: widen_in(item, behind(k)))

    def finish(k):
        def one(t):
            block = g_out.at[origin(t), behind(k)]
            remote(block, block, f_send, f_recv, flat(k, t), "item", other(t)).wait_recv()
            little = small_out.at[origin(t), behind(k)]
            remote(little, little, h_send, h_recv, flat(k, t), "item", other(t)).wait_recv()
            widen_in(origin(t), behind(k))
            forward_in(k, t).wait_send()
            forward_small(k, t).wait_send()
            share_in(k, t).wait_send()

        each(1, peers, one)

    each(0, shares, finish)

    def finish_item(t):
        block = select_out.at[origin(t)]
        remote(block, block, e_send, e_recv, t - 1, "item", other(t)).wait_recv()
        forward_select(t).wait_send()
        block = m_out.at[origin(t)]
        remote(block, block, n_send, n_recv, t - 1, "item", other(t)).wait_recv()
        forward_modulation(t).wait_send()
        share_small(t).wait_send()
        share_select(t).wait_send()

    each(1, peers, finish_item)

    def finish_seq(k):
        spread_small(k).wait_send()
        place_in(k).wait_send()
        part(k).wait_send()

    each(1, shares, finish_seq)
    if cuts is None:
        return
    for j in range(peers):
        rows = select_ref.shape[1]
        select_final[j * rows : (j + 1) * rows] = select_out[j].astype(f32)
    inner = in_final.shape[1] // 2
    mine, share = small_ref.shape[2] // 2, small_ref.shape[1]
    for s in range(shares):
        whole = jnp.concatenate([small_out[j, s].astype(f32) for j in range(peers)], axis=0)
        for half in range(2):
            columns = slice(half * inner + s * mine, half * inner + (s + 1) * mine)
            first = 0
            for cut, final in zip(cuts, finals):
                final[:, columns] = whole[first : first + cut, half * mine : (half + 1) * mine]
                first += cut


def weight_sums(modulation, g, gate, small, select, cuts):
    shares, peers = g.shape[:2]
    vmem = pl.BlockSpec(memory_space=pltpu.VMEM)
    dma = pltpu.SemaphoreType.DMA
    some = peers - 1
    sizes = [shares * some] * 2 + [some] * 4 + [shares] * 4 + [shares * some] * 4 + [some] * 2
    sizes += [shares] * 2 + [some] * 2
    kept = [
        ((peers, shares) + g.shape[2:], bf16),
        ((peers, shares) + small.shape[1:], bf16),
        (select.shape, bf16),
    ]
    inner2 = 2 * shares * g.shape[3]
    direct = g.shape[3] % lanes == 0
    outs = kept
    if direct:
        outs = [((peers * g.shape[2], inner2), f32), ((peers * select.shape[1], select.shape[2]), f32)]
        outs += [((cut, inner2), f32) for cut in cuts]
    outs = [((peers,) + modulation.shape, f32)] + outs
    return pl.pallas_call(
        functools.partial(tail_kernel, cuts if direct else None),
        in_specs=[vmem] * 5,
        out_specs=[vmem] * len(outs),
        out_shape=[jax.ShapeDtypeStruct(shape, kind) for shape, kind in outs],
        scratch_shapes=[pltpu.VMEM(shape, kind) for shape, kind in kept if direct]
        + [
            pltpu.VMEM((shares - 1,) + modulation.shape, bf16),
            pltpu.VMEM((some, shares) + g.shape[2:], bf16),
            pltpu.VMEM((some,) + small.shape[1:], bf16),
            pltpu.VMEM((some,) + select.shape[1:], bf16),
            pltpu.VMEM((shares,) + g.shape[2:], bf16),
        ]
        + [dma((size,)) for size in sizes],
        compiler_params=pltpu.CompilerParams(
            collective_id=2, has_side_effects=True, vmem_limit_bytes=40 * 2**20
        ),
        cost_estimate=pl.CostEstimate(flops=60 * 10**9, bytes_accessed=2**20, transcendentals=0),
        name="weight_sums",
    )(modulation, g, gate, small, select)


def filter_windows(x, taps, reverse):
    rim = taps - 1
    length = x.shape[1]
    padded = jnp.pad(x, ((0, 0), (rim, rim), (0, 0)))
    starts = [2 * rim - j if reverse else j for j in range(taps)]
    return [padded[:, s : s + length] for s in starts]


def per_device(
    tokens,
    timestep,
    slot_item,
    slot_valid,
    cotangent,
    in_weight,
    out_weight,
    select_weight,
    modulation_weight,
    delta_weight,
    filter_weight,
    filter_bias,
    delta_bias,
    decay_log,
    skip_gain,
    modulation_bias,
):
    slots, local, model = tokens.shape
    shares = lax.axis_size("seq")
    place = lax.axis_index("seq")
    rank, inner = delta_weight.shape[0], delta_weight.shape[1] // 2
    states = decay_log.shape[0]
    select = select_weight.shape[1] // 2
    taps = filter_weight.shape[0]
    rim = taps - 1
    length = local * shares
    rows = slots * length
    mine = inner // shares
    padded_width = -(-mine // lanes) * lanes
    shard_rows = modulation_weight.shape[0]
    items = timestep.shape[0]

    def own_columns(v):
        split = v.reshape(v.shape[:-1] + (2, shares, mine))
        return lax.dynamic_index_in_dim(split, place, split.ndim - 2, False)

    first_slot = lax.axis_index("item") * slots
    valid = lax.dynamic_slice_in_dim(slot_valid, first_slot, slots).astype(f32)[:, None, None]
    chooser = (slot_item[:, None] == jnp.arange(items, dtype=jnp.int32)[None, :]).astype(bf16)
    embedded = jnp.dot(chooser, timestep, preferred_element_type=f32)
    condition = jax.nn.silu(embedded).astype(bf16)
    own_features = lax.dynamic_slice_in_dim(condition, place * shard_rows, shard_rows, 1)
    own_condition = lax.dynamic_slice_in_dim(own_features, first_slot, slots, 0)
    modulation_part = jnp.dot(own_condition, modulation_weight, preferred_element_type=f32)
    peers = lax.axis_size("item")
    share_rows = in_weight.shape[0] // peers
    own_rows = lax.dynamic_slice_in_dim(
        in_weight, lax.axis_index("item") * share_rows, share_rows, 0
    )
    own_rows = jnp.moveaxis(own_rows.reshape(share_rows, 2, shares, mine), 2, 0)
    all_tokens, own_in, modulation = gather_inputs(
        tokens, own_rows.reshape(shares, share_rows, 2 * mine), modulation_part
    )
    own_in = own_in.reshape(model, 2 * mine)
    modulation = modulation + modulation_bias.astype(f32)[None, :]
    shift = modulation[:, None, :model]
    scale = modulation[:, None, model : 2 * model]
    gate = modulation[:, None, 2 * model :]

    source = all_tokens.astype(f32)
    centered = source - jnp.mean(source, axis=-1, keepdims=True)
    spread = lax.rsqrt(jnp.mean(centered * centered, axis=-1, keepdims=True) + epsilon)
    mixed_in = (centered * spread * (1.0 + scale) + shift).astype(bf16).reshape(rows, model)
    mixed_in = lax.optimization_barrier(mixed_in)
    projected = (
        jnp.dot(mixed_in, own_in, preferred_element_type=f32)
        .astype(bf16)
        .reshape(slots, length, 2 * mine)
    )
    x_half = projected[..., :mine]
    gate_half = projected[..., mine:].astype(f32)

    tap_weight = own_columns(filter_weight).astype(f32)
    tap_bias = own_columns(filter_bias).astype(f32)
    step_weight = own_columns(delta_weight)
    step_bias = own_columns(delta_bias)
    rate = -jnp.exp(own_columns(decay_log))
    skip = own_columns(skip_gain)

    wide_taps = widen(jnp.swapaxes(tap_weight, 0, 1), padded_width)
    wide_select = jnp.swapaxes(select_weight.reshape(mine, 2, select), 0, 1)
    wide_select = jnp.pad(wide_select, ((0, 0), (0, padded_width - mine), (0, 0)))
    selection, wide_active = filter_and_select(
        widen(x_half, padded_width),
        wide_taps,
        widen(tap_bias[:, None, :], padded_width),
        wide_select,
    )
    selection = selection.reshape(2, rows, select)
    activated = [wide_active[d, ..., :mine] for d in range(2)]
    own_cotangent = cotangent.astype(f32)
    own_grad_branch = (valid * gate * own_cotangent).astype(bf16)
    selection, own_grad_branch = lax.optimization_barrier((selection, own_grad_branch))
    grad_branch = lax.all_gather(own_grad_branch, "seq", axis=1, tiled=True).reshape(rows, model)
    delta_rank = selection[:, :, :rank]
    selection = selection.reshape(2, slots, length, select)
    copies = coefficient_copies(select, rank, states)
    wide_rate = widen(jnp.swapaxes(rate, 0, 1) * log2e, padded_width)
    wide_weight = widen(
        jnp.pad(jnp.swapaxes(step_weight, 0, 1), ((0, 0), (0, select - rank), (0, 0))),
        padded_width,
    )
    wide_bias = widen(step_bias[:, None, :], padded_width)
    wide_skip = widen(skip[:, None, :], padded_width)
    scanned, hidden, step, bc = scan_states(
        selection, wide_active, wide_weight, wide_bias, wide_rate, copies, wide_skip
    )
    scanned = scanned[..., :mine]
    scanned_sum = scanned[0].astype(f32) + scanned[1].astype(f32)
    silu_gate = jax.nn.silu(gate_half)
    mixed_out = (scanned_sum * silu_gate).astype(bf16).reshape(rows, mine)
    branch_part = (
        jnp.dot(mixed_out, out_weight, preferred_element_type=f32)
        .astype(bf16)
        .reshape(slots, length, model)
    )
    branch_part, grad_branch = lax.optimization_barrier((branch_part, grad_branch))
    grad_mixed = dot_cols(grad_branch, out_weight).reshape(slots, length, mine)
    grad_scanned = grad_mixed * silu_gate
    grad_gate_half = grad_mixed * scanned_sum * silu_slope(gate_half)
    grad_out = dot_rows(mixed_out, grad_branch).astype(bf16)
    grad_gate_half = grad_gate_half.astype(bf16)
    grad_in_gate = dot_rows(mixed_in, grad_gate_half.reshape(rows, mine)).astype(bf16)
    branch_part, grad_out, grad_in_gate, scan_grad = lax.optimization_barrier(
        (branch_part, grad_out, grad_in_gate, grad_scanned)
    )
    branch_part = lax.psum_scatter(branch_part, "seq", scatter_dimension=1, tiled=True)
    grad_low, grad_input, grad_parts, grad_rate, grad_sums, grad_out, gate_in = scan_adjoint(
        bc,
        wide_active,
        wide_weight,
        wide_rate,
        copies,
        wide_skip,
        step,
        widen(scan_grad, padded_width),
        hidden,
        grad_out.reshape(peers, mine // peers, model),
        grad_in_gate.reshape(shares, peers, share_rows, mine),
    )
    grad_out, grad_low = lax.optimization_barrier(
        (grad_out.reshape(mine, model).astype(f32), grad_low)
    )
    grad_decay = jnp.sum(grad_rate, axis=1)[..., :mine] * ln2
    grad_step_bias = jnp.sum(grad_sums[:, :8, :mine], axis=1)
    grad_skip = jnp.sum(grad_sums[:, 8:, :mine], axis=1)
    grad_parts, branch_part = lax.optimization_barrier((grad_parts, branch_part))
    grad_selection = summed_everywhere(
        grad_parts.reshape(2 * slots, length, select), 5
    ).reshape(2, rows, select)
    grad_delta = jnp.einsum(
        "drk,dre->kde",
        delta_rank,
        grad_low[..., :mine].reshape(2, rows, mine),
        preferred_element_type=f32,
    )
    grad_x = jnp.zeros((slots, length, mine), f32)
    filtered = []
    for d in range(2):
        f = tap_bias[d]
        for j, window in enumerate(filter_windows(x_half, taps, d == 1)):
            f = f + tap_weight[j, d] * window.astype(f32)
        filtered.append(f)
    grad_select, grad_taps, grad_tap_bias = [], [], []
    for d in range(2):
        block = select_weight[:, d * select : (d + 1) * select]
        grad_select.append(
            dot_rows(grad_selection[d], activated[d].reshape(rows, mine)).T
        )
        grad_active = (
            grad_input[d, ..., :mine]
            + dot_cols(grad_selection[d], block).reshape(slots, length, mine)
        )
        grad_filtered = grad_active * silu_slope(filtered[d])
        grad_tap_bias.append(jnp.sum(grad_filtered, axis=(0, 1)))
        windows = filter_windows(x_half, taps, d == 1)
        grad_taps.append(
            jnp.stack([jnp.sum(grad_filtered * w.astype(f32), axis=(0, 1)) for w in windows])
        )
        for j, window in enumerate(filter_windows(grad_filtered, taps, d == 0)):
            grad_x = grad_x + tap_weight[j, d] * window
    grad_x = grad_x.astype(bf16)
    grad_projected = (
        jnp.concatenate([grad_x, grad_gate_half], axis=2).reshape(rows, 2 * mine)
    )
    mixed_part = dot_cols(grad_projected, own_in).astype(bf16).reshape(slots, length, model)
    grad_mixed_in = lax.psum_scatter(mixed_part, "seq", scatter_dimension=1, tiled=True)
    wide_part = mixed_part.astype(f32)
    grad_modulation_part = jnp.concatenate(
        [
            jnp.sum(wide_part, axis=1),
            jnp.sum(wide_part * (centered * spread), axis=1),
            jnp.sum(valid * own_cotangent * branch_part.astype(f32), axis=1),
        ],
        axis=1,
    )
    grad_in = dot_rows(mixed_in, grad_x.reshape(rows, mine)).astype(bf16)
    branch = branch_part.astype(f32)
    output = (tokens.astype(f32) + valid * gate * branch).astype(bf16)
    small = jnp.concatenate(
        [
            grad_delta,
            jnp.swapaxes(grad_decay, 0, 1),
            jnp.stack(grad_taps, 1),
            jnp.stack(grad_tap_bias)[None],
            grad_step_bias[None],
            grad_skip[None],
        ],
        axis=0,
    )
    small_rows = small.shape[0]
    share = -(-small_rows // (16 * peers)) * 16
    small = jnp.pad(
        small.astype(bf16).reshape(small_rows, 2 * mine), ((0, peers * share - small_rows), (0, 0))
    )
    grad_select = jnp.concatenate(grad_select, axis=1).astype(bf16)
    cuts = [rank, states, taps, 1, 1, 1]
    grad_modulation, *results = weight_sums(
        grad_modulation_part.astype(bf16),
        grad_in.reshape(shares, peers, share_rows, mine),
        gate_in,
        small.reshape(peers, share, 2 * mine),
        grad_select.reshape(peers, mine // peers, 2 * select),
        cuts,
    )
    grad_modulation, grad_mixed_in = lax.optimization_barrier((grad_modulation, grad_mixed_in))
    grad_mixed_in = grad_mixed_in.astype(f32)
    grad_modulation = grad_modulation.reshape(-1, 3 * model)
    own_source = tokens.astype(f32)
    own_centered = own_source - jnp.mean(own_source, axis=-1, keepdims=True)
    own_spread = lax.rsqrt(
        jnp.mean(own_centered * own_centered, axis=-1, keepdims=True) + epsilon
    )
    normed = own_centered * own_spread
    grad_normed = grad_mixed_in * (1.0 + scale)
    grad_source = own_spread * (
        grad_normed
        - jnp.mean(grad_normed, axis=-1, keepdims=True)
        - normed * jnp.mean(grad_normed * normed, axis=-1, keepdims=True)
    )
    grad_tokens = (own_cotangent + grad_source).astype(bf16)
    grad_modulation_weight = lax.dot_general(
        own_features.astype(f32),
        grad_modulation,
        (((0,), (0,)), ((), ())),
        precision=lax.Precision.HIGHEST,
        preferred_element_type=f32,
    )
    if mine % lanes == 0:
        grad_in, grad_select, *small = results
    else:
        grad_in, small, grad_select = results
        grad_in = jnp.stack([grad_in, gate_in]).reshape(2, peers, shares, share_rows, mine)
        grad_in = jnp.transpose(grad_in, (1, 3, 0, 2, 4)).reshape(peers * share_rows, 2 * inner)
        grad_in = grad_in.astype(f32)
        small = small.reshape(peers, shares, share, 2, mine)
        small = jnp.transpose(small, (0, 2, 3, 1, 4)).reshape(peers * share, 2 * inner).astype(f32)
        ends = [sum(cuts[: i + 1]) for i in range(len(cuts))]
        small = [small[end - cut : end] for cut, end in zip(cuts, ends)]
        grad_select = grad_select.reshape(mine, 2 * select).astype(f32)
    return (
        output,
        grad_tokens,
        grad_in,
        grad_out,
        grad_select,
        grad_modulation_weight,
        small[0],
        small[2],
        small[3].reshape(-1),
        small[4].reshape(-1),
        small[1],
        small[5].reshape(-1),
        jnp.sum(grad_modulation, axis=0),
    )


def solution(mesh):
    tokens, rows, same = P("item", "seq", None), P("seq", None), P()
    return jax.shard_map(
        per_device,
        mesh=mesh,
        in_specs=(tokens, same, same, same, tokens, rows, rows, rows, rows) + (same,) * 7,
        out_specs=(tokens, tokens, rows, rows, rows, rows) + (same,) * 7,
        check_vma=False,
    )
```

```python
import functools
import math

import jax
import jax.numpy as jnp
from jax import lax
from jax.experimental import pallas as pl
from jax.experimental.pallas import tpu as pltpu
from jax.sharding import PartitionSpec as P

epsilon = 1e-06
log2e = 1.4426950408889634
ln2 = 0.6931471805599453
chunk = 16
lanes = 128
f32 = jnp.float32
bf16 = jnp.bfloat16


def silu_slope(v):
    s = jax.nn.sigmoid(v)
    return s * (1.0 + v * (1.0 - s))


def dot_rows(a, b):
    return lax.dot_general(a, b, (((0,), (0,)), ((), ())), preferred_element_type=f32)


def dot_cols(a, b):
    return lax.dot_general(a, b, (((1,), (1,)), ((), ())), preferred_element_type=f32)


def fold_sublanes(parts):
    outs = []
    for first in range(0, len(parts), 8):
        cur = parts[first : first + 8]
        row = lax.broadcasted_iota(jnp.int32, cur[0].shape, 0)
        for hop in (4, 2, 1):
            keep = (row // hop) % 2 == 0
            half = len(cur) // 2
            merged = []
            for j in range(half):
                a, b = cur[j], cur[j + half]
                x, y = jnp.where(keep, a, b), jnp.where(keep, b, a)
                if hop == 4:
                    moved = pltpu.roll(y, 4, 0)
                else:
                    moved = jnp.where(keep, pltpu.roll(y, 8 - hop, 0), pltpu.roll(y, hop, 0))
                merged.append(x + moved)
            cur = merged
        outs.append(cur[0])
    return jnp.concatenate(outs, axis=0)


def wide(v, groups):
    return v if groups == 1 else jnp.concatenate([v] * groups, axis=1)


def spread_matrix():
    rows = lax.broadcasted_iota(jnp.int32, (2 * chunk, 2 * lanes), 0) // chunk
    cols = lax.broadcasted_iota(jnp.int32, (2 * chunk, 2 * lanes), 1) // lanes
    return (rows == cols).astype(f32).astype(bf16)


def chunk_sweep(count, body, spread, first, second):
    spread(0, first)
    if count == 1:
        body(0, first)
        return

    def pair(k, carry):
        spread(2 * k + 1, second)
        body(2 * k, first)
        spread(jnp.minimum(2 * k + 2, count - 1), first)
        body(2 * k + 1, second)
        return carry

    lax.fori_loop(0, count // 2, pair, 0)


def place_coefficients(selection, copies):
    placed = jnp.dot(selection, copies, preferred_element_type=f32)
    row = lax.rem(lax.broadcasted_iota(jnp.int32, placed.shape, 0), chunk)
    span = placed.shape[1] // 2
    col = lax.rem(lax.broadcasted_iota(jnp.int32, placed.shape, 1), span) // (span // chunk)
    return jnp.where(row == col, placed, 0.0).astype(bf16)


def softplus(v):
    return jnp.maximum(v, 0.0) + jnp.log1p(jnp.exp(-jnp.abs(v)))


def states_kernel(
    count,
    sel_ref,
    x_ref,
    w_ref,
    bias_ref,
    r_ref,
    copies_ref,
    skip_ref,
    y_ref,
    h_ref,
    dt_ref,
    bc_ref,
    state,
    even,
    odd,
):
    slots, width = dt_ref.shape[1], dt_ref.shape[3]
    groups = width // lanes
    states = r_ref.shape[1]

    @pl.when(pl.program_id(1) == 0)
    def _():
        state[...] = jnp.zeros_like(state)

    for s in range(slots):
        selection = sel_ref[0, s]
        dt_ref[0, s] = softplus(
            jnp.dot(selection, w_ref[0], preferred_element_type=f32) + bias_ref[0]
        )
        bc_ref[0, s] = place_coefficients(selection, copies_ref[...])

    def one_direction(reverse):
        mix = spread_matrix()

        def place(i):
            return (count - 1 - i) if reverse else i

        def spread(i, into):
            start = pl.multiple_of(place(i) * chunk, chunk)
            for s in range(slots):
                both = bc_ref[0, s, pl.ds(start, chunk), :]
                span = both.shape[1] // 2
                into[s] = dot_rows(jnp.concatenate([both[:, :span], both[:, span:]], axis=0), mix)

        def body(i, held):
            start = pl.multiple_of(place(i) * chunk, chunk)
            order = range(chunk - 1, -1, -1) if reverse else range(chunk)
            for s in range(slots):
                h = state[s]
                rate = r_ref[0]
                dt = dt_ref[0, s, pl.ds(start, chunk), :]
                x = x_ref[0, s, pl.ds(start, chunk), :].astype(f32)
                u = dt * x
                kept, sums = [None] * chunk, [None] * chunk
                for t in order:
                    rows = slice(t * states, (t + 1) * states)
                    b = wide(held[s, rows, :lanes], groups)
                    c = wide(held[s, rows, lanes:], groups)
                    h = jnp.exp2(dt[t : t + 1] * rate) * h + u[t : t + 1] * b
                    kept[t] = h.astype(bf16)
                    p = h * c
                    sums[t] = p[:8] + p[8:]
                size = chunk * states
                h_ref[0, s, pl.ds(pl.multiple_of(start * states, size), size), :] = jnp.concatenate(
                    kept, axis=0
                )
                y = fold_sublanes(sums) + skip_ref[0] * x
                y_ref[0, s, pl.ds(start, chunk), :] = y.astype(bf16)
                state[s] = h

        chunk_sweep(count, body, spread, even, odd)

    for d in range(2):

        @pl.when(pl.program_id(0) == d)
        def _():
            one_direction(d == 1)


def side_exchange(b_ref, q_ref, b_out, q_out, b_box, q_box, q_stage, *sems):
    b_keep, q_keep, o_keep, p_keep = sems[:4]
    (i_send, i_recv, j_send, j_recv, a_send, a_recv, z_send, z_recv, f_send, f_recv) = sems[4:]
    shares, peers = q_ref.shape[0], q_ref.shape[1]
    me, item = lax.axis_index("seq"), lax.axis_index("item")
    step = pl.program_id(0) * pl.num_programs(1) + pl.program_id(1)
    quarter = pl.num_programs(0) * pl.num_programs(1) // 4

    def other(t):
        return lax.rem(item + t, peers)

    def origin(t):
        return lax.rem(item - t + peers, peers)

    def ahead(k):
        return lax.rem(me + k, shares)

    def behind(k):
        return lax.rem(me - k + shares, shares)

    def own_b():
        return pltpu.make_async_copy(b_ref.at[item], b_box.at[0], b_keep)

    def own_q():
        return pltpu.make_async_copy(q_ref.at[:, item], q_box.at[0], q_keep)

    def share_b(t):
        return remote(b_ref.at[other(t)], b_box.at[t], i_send, i_recv, t - 1, "item", other(t))

    def share_q(t):
        return remote(q_ref.at[:, other(t)], q_box.at[t], a_send, a_recv, t - 1, "item", other(t))

    def keep_b():
        return pltpu.make_async_copy(b_box.at[0], b_out.at[item], o_keep)

    def keep_q():
        return pltpu.make_async_copy(q_stage.at[me], q_out.at[item, me], p_keep)

    def give_b(t):
        return remote(b_box.at[0], b_out.at[item], j_send, j_recv, t - 1, "item", other(t))

    def place_q(k):
        return remote(
            q_stage.at[ahead(k)], q_out.at[item, me], z_send, z_recv, k, "seq", ahead(k)
        )

    def forward_q(k, t):
        source = q_stage.at[me] if isinstance(k, int) else q_out.at[item, behind(k)]
        return remote(
            source,
            q_out.at[item, behind(k)],
            f_send,
            f_recv,
            k * (peers - 1) + t - 1,
            "item",
            other(t),
        )

    @pl.when(step == 0)
    def _():
        greet((("seq", me, shares), ("item", item, peers)))
        each(1, peers, lambda t: share_q(t).start())
        each(1, peers, lambda t: share_b(t).start())
        own_b().start()
        own_q().start()

    @pl.when(step == quarter)
    def _():
        own_q().wait()
        own_b().wait()

        def arrived(t):
            share_q(t).wait_recv()
            share_b(t).wait_recv()

        each(1, peers, arrived)

        def sum_q(p):
            def add(t, total):
                return total + q_box[t, p].astype(f32)

            q_stage[p] = lax.fori_loop(1, peers, add, q_box[0, p].astype(f32)).astype(bf16)

        each(0, shares, sum_q)
        rows = 16 if b_box.shape[1] % 16 == 0 else b_box.shape[1]

        def sum_b(r):
            place = pl.ds(pl.multiple_of(r * rows, rows), rows)

            def add(t, total):
                return total + b_box[t, place, :].astype(f32)

            total = lax.fori_loop(1, peers, add, b_box[0, place, :].astype(f32))
            b_box[0, place, :] = total.astype(bf16)

        each(0, b_box.shape[1] // rows, sum_b)
        each(1, shares, lambda k: place_q(k).start())
        each(1, peers, lambda t: forward_q(0, t).start())
        each(1, peers, lambda t: give_b(t).start())
        keep_b().start()
        keep_q().start()

    @pl.when(step == 2 * quarter)
    def _():
        def pass_on(k):
            block = q_out.at[item, behind(k)]
            remote(block, block, z_send, z_recv, k, "seq", behind(k)).wait_recv()
            each(1, peers, lambda t: forward_q(k, t).start())

        each(1, shares, pass_on)

    @pl.when(step == 3 * quarter)
    def _():
        keep_b().wait()
        keep_q().wait()

        def finish(t):
            block = b_out.at[origin(t)]
            remote(block, block, j_send, j_recv, t - 1, "item", other(t)).wait_recv()
            give_b(t).wait_send()
            share_b(t).wait_send()
            share_q(t).wait_send()

        each(1, peers, finish)

        def finish_q(k):
            def one(t):
                block = q_out.at[origin(t), behind(k)]
                remote(
                    block, block, f_send, f_recv, k * (peers - 1) + t - 1, "item", other(t)
                ).wait_recv()
                forward_q(k, t).wait_send()

            each(1, peers, one)

        each(0, shares, finish_q)
        each(1, shares, lambda k: place_q(k).wait_send())


def adjoint_kernel(
    count,
    bc_ref,
    x_ref,
    w_ref,
    r_ref,
    copies_ref,
    skip_ref,
    dt_ref,
    g_ref,
    h_ref,
    edge_ref,
    b_ref,
    q_ref,
    low_ref,
    input_ref,
    gsel_ref,
    decay_ref,
    sums_ref,
    b_out,
    q_out,
    pending,
    coefs,
    even,
    odd,
    *side,
):
    slots, width = dt_ref.shape[1], dt_ref.shape[3]
    groups = width // lanes
    states = r_ref.shape[1]
    last_block = pl.program_id(1) == pl.num_programs(1) - 1

    side_exchange(b_ref, q_ref, b_out, q_out, *side)

    @pl.when(pl.program_id(1) == 0)
    def _():
        pending[...] = jnp.zeros_like(pending)
        decay_ref[...] = jnp.zeros_like(decay_ref)
        sums_ref[...] = jnp.zeros_like(sums_ref)

    def one_direction(reverse):
        mix = spread_matrix()
        picks = (
            lax.broadcasted_iota(jnp.int32, (8, 2 * lanes), 0)
            == lax.broadcasted_iota(jnp.int32, (8, 2 * lanes), 1) // lanes
        ).astype(f32).astype(bf16)

        def place(i):
            return i if reverse else (count - 1 - i)

        def spread(i, into):
            start = pl.multiple_of(place(i) * chunk, chunk)
            for s in range(slots):
                both = bc_ref[0, s, pl.ds(start, chunk), :]
                span = both.shape[1] // 2
                into[s] = dot_rows(jnp.concatenate([both[:, :span], both[:, span:]], axis=0), mix)

        def body(i, held):
            here = place(i)
            start = pl.multiple_of(here * chunk, chunk)
            order = range(chunk) if reverse else range(chunk - 1, -1, -1)
            size = chunk * states
            base = pl.multiple_of(start * states, size)
            at_end = here == (count - 1 if reverse else 0)
            outer = jnp.where(last_block, 0.0, 1.0)
            near = pl.multiple_of(
                jnp.clip(start + (chunk if reverse else -1), 0, count * chunk - 1) * states, states
            )
            for s in range(slots):
                pend = pending[s]
                rate = r_ref[0]
                dt = dt_ref[0, s, pl.ds(start, chunk), :]
                x = x_ref[0, s, pl.ds(start, chunk), :].astype(f32)
                g = g_ref[s, pl.ds(start, chunk), :].astype(f32)
                u = dt * x
                before = jnp.where(
                    at_end,
                    edge_ref[0, s].astype(f32) * outer,
                    h_ref[0, s, pl.ds(near, states), :].astype(f32),
                )
                total = decay_ref[0, s]
                rate_sums, into_sums = [None] * chunk, [None] * chunk
                coef = [None] * chunk
                hidden = h_ref[0, s, pl.ds(base, size), :]
                now = hidden[order[0] * states : (order[0] + 1) * states].astype(f32)
                for k, t in enumerate(order):
                    rows = slice(t * states, (t + 1) * states)
                    b = wide(held[s, rows, :lanes], groups)
                    c = wide(held[s, rows, lanes:], groups)
                    if k + 1 < chunk:
                        q = order[k + 1]
                        prev = hidden[q * states : (q + 1) * states].astype(f32)
                    else:
                        prev = before
                    gt = g[t : t + 1]
                    adj = c * gt + pend
                    pend = jnp.exp2(dt[t : t + 1] * rate) * adj
                    through = pend * prev * rate
                    total = total + through * dt[t : t + 1]
                    rate_sums[t] = through[:8] + through[8:]
                    w = adj * b
                    into_sums[t] = w[:8] + w[8:]
                    cb, cc = adj * u[t : t + 1], now * gt
                    sb, sc = cb[:, :lanes], cc[:, :lanes]
                    for j in range(1, groups):
                        sb = sb + cb[:, j * lanes : (j + 1) * lanes]
                        sc = sc + cc[:, j * lanes : (j + 1) * lanes]
                    coef[t] = jnp.concatenate([sb, sc], axis=1).astype(bf16)
                    now = prev
                pending[s] = pend
                decay_ref[0, s] = total
                weighted = fold_sublanes(into_sums)
                few = dt * (1.0 - dt * (0.5 - dt * (1.0 / 6.0 - dt * (1.0 / 24.0))))
                slope = jnp.where(dt < 0.03, few, 1.0 - jnp.exp(-dt))
                grad_pre = (fold_sublanes(rate_sums) * ln2 + weighted * x) * slope
                low_ref[0, s, pl.ds(start, chunk), :] = grad_pre.astype(bf16)
                direct = weighted * dt + skip_ref[0] * g
                input_ref[0, s, pl.ds(start, chunk), :] = direct.astype(bf16)
                gx = g * x
                sums_ref[0] += jnp.concatenate(
                    [grad_pre[:8] + grad_pre[8:], gx[:8] + gx[8:]], axis=0
                )
                coefs[s, pl.ds(pl.multiple_of(here * 8, 8), 8), :] = dot_cols(
                    picks, jnp.concatenate(coef, axis=0)
                )

        chunk_sweep(count, body, spread, even, odd)

    for d in range(2):

        @pl.when(pl.program_id(0) == d)
        def _():
            one_direction(d == 1)


    own = lax.broadcasted_iota(jnp.int32, (chunk, chunk * states), 0) == (
        lax.broadcasted_iota(jnp.int32, (chunk, chunk * states), 1) // states
    )
    for s in range(slots):
        placed = []
        for c in range(count):
            placed.append(
                jnp.concatenate(
                    [
                        jnp.where(own, coefs[s, c * 8 + k : c * 8 + k + 1, :], 0.0)
                        for k in range(2)
                    ],
                    axis=1,
                )
            )
        placed = jnp.concatenate(placed, axis=0).astype(bf16)
        gsel_ref[0, s] = (
            dot_cols(low_ref[0, s], w_ref[0]) + dot_cols(placed, copies_ref[...])
        ).astype(bf16)


def block_of(length):
    return math.gcd(length, 256)


def scan_states(selection, x, weight, bias, rate, copies, skip):
    two, slots, length, width = x.shape
    select = selection.shape[3]
    states = rate.shape[1]
    hidden_size = two * slots * length * states * width
    block = block_of(length)
    blocks = length // block
    spread = copies.shape[1]

    def where(d, i):
        return (d, 0, jnp.where(d == 1, blocks - 1 - i, i), 0)

    def by_direction(d, i):
        return (d, 0, 0)

    return pl.pallas_call(
        functools.partial(states_kernel, block // chunk),
        grid=(two, blocks),
        in_specs=[
            pl.BlockSpec((1, slots, block, select), where),
            pl.BlockSpec((1, slots, block, width), where),
            pl.BlockSpec((1, select, width), by_direction),
            pl.BlockSpec((1, 1, width), by_direction),
            pl.BlockSpec((1, states, width), by_direction),
            pl.BlockSpec((select, spread), lambda d, i: (0, 0)),
            pl.BlockSpec((1, 1, width), by_direction),
        ],
        out_specs=[
            pl.BlockSpec((1, slots, block, width), where),
            pl.BlockSpec((1, slots, block * states, width), where),
            pl.BlockSpec((1, slots, block, width), where),
            pl.BlockSpec((1, slots, block, spread), where),
        ],
        out_shape=[
            jax.ShapeDtypeStruct((two, slots, length, width), bf16),
            jax.ShapeDtypeStruct((two, slots, length * states, width), bf16),
            jax.ShapeDtypeStruct((two, slots, length, width), f32),
            jax.ShapeDtypeStruct((two, slots, length, spread), bf16),
        ],
        scratch_shapes=[
            pltpu.VMEM((slots, states, width), f32),
            pltpu.VMEM((slots, chunk * states, 2 * lanes), f32),
            pltpu.VMEM((slots, chunk * states, 2 * lanes), f32),
        ],
        compiler_params=pltpu.CompilerParams(vmem_limit_bytes=48 * 2**20),
        cost_estimate=pl.CostEstimate(
            flops=64 * 10**9, bytes_accessed=80 * 2**20, transcendentals=hidden_size
        ),
        name="scan_states",
    )(selection, x, weight, bias, rate, copies, skip)


def scan_adjoint(bc, x, weight, rate, copies, skip, dt, g, h, b, q):
    two, slots, length, width = dt.shape
    select = weight.shape[1]
    states = rate.shape[1]
    hidden_size = two * slots * length * states * width
    block = block_of(length)
    blocks = length // block
    spread = copies.shape[1]
    shares, peers = q.shape[:2]
    anywhere, dma = pl.BlockSpec(memory_space=pl.ANY), pltpu.SemaphoreType.DMA

    def at(d, i):
        return jnp.where(d == 1, i, blocks - 1 - i)

    def where(d, i):
        return (d, 0, at(d, i), 0)

    def edge(d, i):
        mine = at(d, i) * block
        return (d, 0, jnp.clip(jnp.where(d == 1, mine + block, mine - 1), 0, length - 1), 0)

    def by_direction(d, i):
        return (d, 0, 0)

    return pl.pallas_call(
        functools.partial(adjoint_kernel, block // chunk),
        grid=(two, blocks),
        in_specs=[
            pl.BlockSpec((1, slots, block, spread), where),
            pl.BlockSpec((1, slots, block, width), where),
            pl.BlockSpec((1, select, width), by_direction),
            pl.BlockSpec((1, states, width), by_direction),
            pl.BlockSpec((select, spread), lambda d, i: (0, 0)),
            pl.BlockSpec((1, 1, width), by_direction),
            pl.BlockSpec((1, slots, block, width), where),
            pl.BlockSpec((slots, block, width), lambda d, i: (0, at(d, i), 0)),
            pl.BlockSpec((1, slots, block * states, width), where),
            pl.BlockSpec((1, slots, states, width), edge),
            anywhere,
            anywhere,
        ],
        out_specs=[
            pl.BlockSpec((1, slots, block, width), where),
            pl.BlockSpec((1, slots, block, width), where),
            pl.BlockSpec((1, slots, block, select), where),
            pl.BlockSpec((1, slots, states, width), lambda d, i: (d, 0, 0, 0)),
            pl.BlockSpec((1, 16, width), by_direction),
            anywhere,
            anywhere,
        ],
        out_shape=[
            jax.ShapeDtypeStruct((two, slots, length, width), bf16),
            jax.ShapeDtypeStruct((two, slots, length, width), bf16),
            jax.ShapeDtypeStruct((two, slots, length, select), bf16),
            jax.ShapeDtypeStruct((two, slots, states, width), f32),
            jax.ShapeDtypeStruct((two, 16, width), f32),
            jax.ShapeDtypeStruct(b.shape, bf16),
            jax.ShapeDtypeStruct((peers, shares) + q.shape[2:], bf16),
        ],
        scratch_shapes=[
            pltpu.VMEM((slots, states, width), f32),
            pltpu.VMEM((slots, block // chunk * 8, chunk * states), f32),
            pltpu.VMEM((slots, chunk * states, 2 * lanes), f32),
            pltpu.VMEM((slots, chunk * states, 2 * lanes), f32),
            pltpu.VMEM(b.shape, bf16),
            pltpu.VMEM((peers, shares) + q.shape[2:], bf16),
            pltpu.VMEM((shares,) + q.shape[2:], bf16),
        ]
        + [dma] * 4
        + [dma((peers - 1,))] * 6
        + [dma((shares,))] * 2
        + [dma((shares * (peers - 1),))] * 2,
        compiler_params=pltpu.CompilerParams(
            collective_id=6, has_side_effects=True, vmem_limit_bytes=48 * 2**20
        ),
        cost_estimate=pl.CostEstimate(
            flops=100 * 10**9, bytes_accessed=100 * 2**20, transcendentals=hidden_size
        ),
        name="scan_adjoint",
    )(bc, x, weight, rate, copies, skip, dt, g, h, h, b, q)


def coefficient_copies(width, rank, states):
    span = chunk * states
    col = jnp.arange(2 * span)
    origin = rank + (col // span) * states + col % states
    return (jnp.arange(width)[:, None] == origin[None, :]).astype(bf16)


def widen(v, width):
    short = width - v.shape[-1]
    return v if short == 0 else jnp.pad(v, ((0, 0),) * (v.ndim - 1) + ((0, short),))


def remote(src, dst, sends, recvs, slot, axis, to):
    return pltpu.make_async_remote_copy(
        src_ref=src,
        dst_ref=dst,
        send_sem=sends.at[slot],
        recv_sem=recvs.at[slot],
        device_id={axis: to},
        device_id_type=pl.DeviceIdType.MESH,
    )


def each(first, last, body):
    def run(k, carry):
        body(k)
        return carry

    lax.fori_loop(first, last, run, 0)


def greet(peers):
    barrier = pltpu.get_barrier_semaphore()
    total = 0
    for axis, me, count in peers:

        def hello(k):
            pl.semaphore_signal(
                barrier,
                inc=1,
                device_id={axis: lax.rem(me + k, count)},
                device_id_type=pl.DeviceIdType.MESH,
            )

        each(1, count, hello)
        total += count - 1
    pl.semaphore_wait(barrier, total)


def total_kernel(line, produce, v_ref, o_ref, pairbox, stage, inbox, *sems):
    pair_send, pair_recv, sum_send, sum_recv, out_send, out_recv, fwd_send, fwd_recv = sems
    me = lax.axis_index("seq")
    pos, core = me // 2, lax.rem(me, 2)
    partner = me + 1 - 2 * core
    barrier = pltpu.get_barrier_semaphore()

    def hello(to):
        pl.semaphore_signal(
            barrier, inc=1, device_id={"seq": to}, device_id_type=pl.DeviceIdType.MESH
        )

    hello(partner)
    each(1, line, lambda k: hello(lax.rem(pos + k, line) * 2 + core))
    pl.semaphore_wait(barrier, line)

    pair = remote(v_ref.at[:, :, 1 - core], pairbox, pair_send, pair_recv, 0, "seq", partner)
    if produce is not None:
        produce(1 - core)
    pair.start()
    if produce is not None:
        produce(core)
    pair.wait_recv()

    def own(q):
        return v_ref[:, q, core].astype(f32) + pairbox[:, q].astype(f32)

    def summand(k):
        q = lax.rem(pos + k, line)
        return remote(
            stage.at[q], inbox.at[pos], sum_send, sum_recv, k - 1, "seq", q * 2 + core
        )

    def send(k):
        q = lax.rem(pos + k, line)
        stage[q] = own(q).astype(bf16)
        summand(k).start()

    each(1, line, send)

    def source(k):
        return lax.rem(pos - k + line, line)

    def arrived(k, total):
        q = source(k)
        remote(stage.at[q], inbox.at[q], sum_send, sum_recv, k - 1, "seq", partner).wait_recv()
        return total + inbox[q].astype(f32)

    total = lax.fori_loop(1, line, arrived, own(pos))
    o_ref[:, pos, core] = total.astype(bf16)

    def result(k):
        mine = o_ref.at[:, pos, core]
        return remote(
            mine, mine, out_send, out_recv, k - 1, "seq", lax.rem(pos + k, line) * 2 + core
        )

    def forward(k):
        block = o_ref.at[:, source(k), core]
        return remote(block, block, fwd_send, fwd_recv, k, "seq", partner)

    each(1, line, lambda k: result(k).start())
    forward(0).start()

    def pass_on(k):
        block = o_ref.at[:, source(k), core]
        remote(block, block, out_send, out_recv, k - 1, "seq", partner).wait_recv()
        forward(k).start()

    each(1, line, pass_on)

    def finish(k):
        block = o_ref.at[:, source(k), 1 - core]
        remote(block, block, fwd_send, fwd_recv, k, "seq", partner).wait_recv()
        forward(k).wait_send()

    each(0, line, finish)
    pair.wait_send()

    def drain(k):
        summand(k).wait_send()
        result(k).wait_send()

    each(1, line, drain)


def summed_everywhere(v, call):
    batch, length, width = v.shape
    shares = lax.axis_size("seq")
    line, rows = shares // 2, length // shares
    vmem = pl.BlockSpec(memory_space=pltpu.VMEM)
    dma = pltpu.SemaphoreType.DMA
    blocks = v.reshape(batch, line, 2, rows, width)
    out = pl.pallas_call(
        functools.partial(total_kernel, line, None),
        in_specs=[vmem],
        out_specs=vmem,
        out_shape=jax.ShapeDtypeStruct(blocks.shape, bf16),
        scratch_shapes=[
            pltpu.VMEM((batch, line, rows, width), bf16),
            pltpu.VMEM((line, batch, rows, width), bf16),
            pltpu.VMEM((line, batch, rows, width), bf16),
            dma((1,)),
            dma((1,)),
            dma((line,)),
            dma((line,)),
            dma((line,)),
            dma((line,)),
            dma((line,)),
            dma((line,)),
        ],
        compiler_params=pltpu.CompilerParams(
            collective_id=call, has_side_effects=True, vmem_limit_bytes=40 * 2**20
        ),
        cost_estimate=pl.CostEstimate(flops=25 * 10**9, bytes_accessed=2**20, transcendentals=0),
        name="sum_" + str(call),
    )(blocks)
    return out.reshape(v.shape)


def filter_kernel(line, x_ref, tap_ref, bias_ref, select_ref, o_ref, a_ref, padded, v_ref, *rest):
    slots, length, width = x_ref.shape
    taps = tap_ref.shape[1]
    rows = v_ref.shape[3]
    rim = 8
    edge = jnp.zeros((slots, rim, width), f32)
    padded[:, :rim, :] = edge
    padded[:, rim + length :, :] = edge
    padded[:, rim : rim + length, :] = x_ref[...].astype(f32)

    def produce(core):
        def block(q):
            start = pl.multiple_of((q * 2 + core) * rows, rows)
            for s in range(slots):
                near = padded[s, pl.ds(start, rows + 2 * rim), :]
                for d in range(2):
                    total = bias_ref[d]
                    for j in range(taps):
                        first = rim + (taps - 1 - j if d == 1 else j - taps + 1)
                        total = total + tap_ref[d, j : j + 1, :] * near[first : first + rows]
                    active = (total / (1.0 + jnp.exp(-total))).astype(bf16)
                    a_ref[d, s, pl.ds(start, rows), :] = active
                    v_ref[d * slots + s, q, core] = jnp.dot(
                        active, select_ref[d], preferred_element_type=f32
                    ).astype(bf16)

        each(0, line, block)

    total_kernel(line, produce, v_ref, o_ref, *rest)


def filter_and_select(x, taps, bias, select):
    slots, length, width = x.shape
    batch, columns = 2 * slots, select.shape[2]
    shares = lax.axis_size("seq")
    line, rows = shares // 2, length // shares
    vmem = pl.BlockSpec(memory_space=pltpu.VMEM)
    dma = pltpu.SemaphoreType.DMA
    blocks = (batch, line, 2, rows, columns)
    out, active = pl.pallas_call(
        functools.partial(filter_kernel, line),
        in_specs=[vmem] * 4,
        out_specs=[vmem] * 2,
        out_shape=[
            jax.ShapeDtypeStruct(blocks, bf16),
            jax.ShapeDtypeStruct((2, slots, length, width), bf16),
        ],
        scratch_shapes=[
            pltpu.VMEM((slots, length + 16, width), f32),
            pltpu.VMEM(blocks, bf16),
            pltpu.VMEM((batch, line, rows, columns), bf16),
            pltpu.VMEM((line, batch, rows, columns), bf16),
            pltpu.VMEM((line, batch, rows, columns), bf16),
        ]
        + [dma((1,))] * 2
        + [dma((line,))] * 6,
        compiler_params=pltpu.CompilerParams(
            collective_id=4, has_side_effects=True, vmem_limit_bytes=40 * 2**20
        ),
        cost_estimate=pl.CostEstimate(flops=30 * 10**9, bytes_accessed=2**20, transcendentals=0),
        name="filter_and_select",
    )(x, taps, bias, select)
    return out.reshape(batch, length, columns), active


def head_kernel(line, t_ref, w_ref, mod_ref, all_ref, box_ref, out_ref, parts, *sems):
    keep, t_keep, u_send, u_recv, d_send, d_recv, p_send, p_recv = sems[:8]
    w_send, w_recv, f_send, f_recv, m_send, m_recv = sems[8:]
    shares, peers = box_ref.shape[0], box_ref.shape[1]
    slots, local = t_ref.shape[0], t_ref.shape[1]
    me, item = lax.axis_index("seq"), lax.axis_index("item")
    pos, core = me // 2, lax.rem(me, 2)
    partner = me + 1 - 2 * core
    greet((("seq", me, shares), ("item", item, peers)))

    def region(q, c, s):
        first = pl.multiple_of((q * 2 + c) * local, local)
        return all_ref.at[s, pl.ds(first, local), :]

    def hop(q, s, source, sends, recvs, k, to):
        return remote(source, region(q, core, s), sends, recvs, k * slots + s, "seq", to)

    def up(k, s):
        source = t_ref.at[s] if isinstance(k, int) else region(pos - k, core, s)
        return hop(pos - k, s, source, u_send, u_recv, k, me + 2)

    def down(k, s):
        source = t_ref.at[s] if isinstance(k, int) else region(pos + k, core, s)
        return hop(pos + k, s, source, d_send, d_recv, k, me - 2)

    def across(q, s):
        return remote(
            region(q, core, s), region(q, core, s), p_send, p_recv, q * slots + s, "seq", partner
        )

    def own_across(s):
        return remote(
            t_ref.at[s], region(pos, core, s), p_send, p_recv, pos * slots + s, "seq", partner
        )

    not_last, not_first = pos < line - 1, pos > 0
    for s in range(slots):

        @pl.when(not_last)
        def _():
            up(0, s).start()

        @pl.when(not_first)
        def _():
            down(0, s).start()

    def modulation(k):
        return remote(
            mod_ref, parts.at[k - 1], m_send, m_recv, k - 1, "seq", lax.rem(me + k, shares)
        )

    def weight(k):
        to = lax.rem(me + k, shares)
        return remote(w_ref.at[to], box_ref.at[me, item], w_send, w_recv, k, "seq", to)

    each(1, shares, lambda k: modulation(k).start())
    each(1, shares, lambda k: weight(k).start())
    own = pltpu.make_async_copy(w_ref.at[me], box_ref.at[me, item], keep)
    own.start()
    kept = []
    for s in range(slots):
        own_across(s).start()
        kept.append(pltpu.make_async_copy(t_ref.at[s], region(pos, core, s), t_keep.at[s]))
        kept[-1].start()

    def forward(k, t):
        block = box_ref.at[lax.rem(me - k + shares, shares), item]
        return remote(
            block, block, f_send, f_recv, k * (peers - 1) + t - 1, "item", lax.rem(item + t, peers)
        )

    def pass_on(k):
        source = lax.rem(me - k + shares, shares)
        block = box_ref.at[source, item]
        remote(block, block, w_send, w_recv, k, "seq", source).wait_recv()
        each(1, peers, lambda t: forward(k, t).start())

    def relay(k):
        for s in range(slots):

            @pl.when(k < pos)
            def _():
                q = pos - 1 - k
                hop(q, s, region(q, core, s), u_send, u_recv, k, partner).wait_recv()

                @pl.when(not_last)
                def _():
                    up(k + 1, s).start()

                across(q, s).start()

            @pl.when(k < line - 1 - pos)
            def _():
                q = pos + 1 + k
                hop(q, s, region(q, core, s), d_send, d_recv, k, partner).wait_recv()

                @pl.when(not_first)
                def _():
                    down(k + 1, s).start()

                across(q, s).start()

    own.wait()
    each(1, peers, lambda t: forward(0, t).start())
    half = shares // 2
    each(1, half, pass_on)
    each(0, 1, relay)
    each(half, shares, pass_on)

    def add(k, total):
        modulation(k).wait_recv()
        return total + parts[k - 1].astype(f32)

    out_ref[...] = lax.fori_loop(1, shares, add, mod_ref[...].astype(f32))
    each(1, line - 1, relay)

    def finish(k):
        def one(t):
            source = lax.rem(item - t + peers, peers)
            block = box_ref.at[lax.rem(me - k + shares, shares), source]
            remote(
                block, block, f_send, f_recv, k * (peers - 1) + t - 1, "item", source
            ).wait_recv()
            forward(k, t).wait_send()

        each(1, peers, one)

    each(0, shares, finish)

    def drain(k):
        weight(k).wait_send()
        modulation(k).wait_send()

    each(1, shares, drain)

    def drain_tokens(q):
        for s in range(slots):
            remote(
                region(q, core, s),
                region(q, 1 - core, s),
                p_send,
                p_recv,
                q * slots + s,
                "seq",
                partner,
            ).wait_recv()
            across(q, s).wait_send()

    each(0, line, drain_tokens)

    def drain_line(k):
        for s in range(slots):

            @pl.when(not_last & (k <= pos))
            def _():
                up(k, s).wait_send()

            @pl.when(not_first & (k <= line - 1 - pos))
            def _():
                down(k, s).wait_send()

    each(0, line, drain_line)
    for copy in kept:
        copy.wait()


def gather_inputs(tokens, blocks, modulation):
    shares, peers = lax.axis_size("seq"), lax.axis_size("item")
    slots, local, model = tokens.shape
    line = shares // 2
    vmem, anywhere = pl.BlockSpec(memory_space=pltpu.VMEM), pl.BlockSpec(memory_space=pl.ANY)
    dma = pltpu.SemaphoreType.DMA
    return pl.pallas_call(
        functools.partial(head_kernel, line),
        in_specs=[anywhere, anywhere, vmem],
        out_specs=[anywhere, anywhere, vmem],
        out_shape=[
            jax.ShapeDtypeStruct((slots, local * shares, model), bf16),
            jax.ShapeDtypeStruct((shares, peers) + blocks.shape[1:], bf16),
            jax.ShapeDtypeStruct(modulation.shape, f32),
        ],
        scratch_shapes=[pltpu.VMEM((shares - 1,) + modulation.shape, bf16), dma, dma((slots,))]
        + [dma((line * slots,))] * 6
        + [dma((shares,))] * 2
        + [dma((shares * (peers - 1),))] * 2
        + [dma((shares,))] * 2,
        compiler_params=pltpu.CompilerParams(collective_id=1, has_side_effects=True),
        cost_estimate=pl.CostEstimate(flops=60 * 10**9, bytes_accessed=2**20, transcendentals=0),
        name="gather_inputs",
    )(tokens, blocks, modulation)


def tail_kernel(cuts, m_ref, g_ref, gate_ref, small_ref, select_ref, m_out, *refs):
    if cuts is None:
        g_out, small_out, select_out, *refs = refs
    else:
        in_final, select_final, *refs = refs
        finals, refs = refs[: len(cuts)], refs[len(cuts) :]
        g_out, small_out, select_out, *refs = refs
    m_parts, g_box, small_box, select_box, g_stage, *sems = refs
    (a_send, a_recv, s_send, s_recv, c_send, c_recv, z_send, z_recv, y_send, y_recv) = sems[:10]
    f_send, f_recv, h_send, h_recv, e_send, e_recv = sems[10:16]
    m_send, m_recv, n_send, n_recv = sems[16:]
    shares, peers = g_ref.shape[0], g_ref.shape[1]
    me, item = lax.axis_index("seq"), lax.axis_index("item")
    greet((("seq", me, shares), ("item", item, peers)))

    def other(t):
        return lax.rem(item + t, peers)

    def origin(t):
        return lax.rem(item - t + peers, peers)

    def ahead(k):
        return lax.rem(me + k, shares)

    def behind(k):
        return lax.rem(me - k + shares, shares)

    def flat(k, t):
        return k * (peers - 1) + t - 1

    def share_small(t):
        return remote(
            small_ref.at[other(t)], small_box.at[t - 1], s_send, s_recv, t - 1, "item", other(t)
        )

    def share_select(t):
        return remote(
            select_ref.at[other(t)], select_box.at[t - 1], c_send, c_recv, t - 1, "item", other(t)
        )

    def share_in(k, t):
        p = ahead(k)
        return remote(
            g_ref.at[p, other(t)], g_box.at[t - 1, p], a_send, a_recv, flat(k, t), "item", other(t)
        )

    def part(k):
        return remote(m_ref, m_parts.at[k - 1], m_send, m_recv, k - 1, "seq", ahead(k))

    def forward_modulation(t):
        block = m_out.at[item]
        return remote(block, block, n_send, n_recv, t - 1, "item", other(t))

    each(1, shares, lambda k: part(k).start())
    each(1, peers, lambda t: share_small(t).start())
    each(1, shares, lambda k: each(1, peers, lambda t: share_in(k, t).start()))
    each(1, peers, lambda t: share_in(0, t).start())
    each(1, peers, lambda t: share_select(t).start())

    def add_small(t, total):
        share_small(t).wait_recv()
        return total + small_box[t - 1].astype(f32)

    small_out[item, me] = lax.fori_loop(
        1, peers, add_small, small_ref[item].astype(f32)
    ).astype(bf16)

    def spread_small(k):
        block = small_out.at[item, me]
        return remote(block, block, y_send, y_recv, k, "seq", ahead(k))

    each(1, shares, lambda k: spread_small(k).start())

    def sum_in(k):
        p = ahead(k)

        def add(t, total):
            share_in(k, t).wait_recv()
            return total + g_box[t - 1, p].astype(f32)

        return lax.fori_loop(1, peers, add, g_ref[p, item].astype(f32)).astype(bf16)

    def place_in(k):
        return remote(
            g_stage.at[k], g_out.at[item, me], z_send, z_recv, k, "seq", ahead(k)
        )

    def turn(k):
        g_stage[k] = sum_in(k)
        place_in(k).start()

    each(1, shares, turn)
    g_out[item, me] = sum_in(0)

    def forward_in(k, t):
        block = g_out.at[item, behind(k)]
        return remote(block, block, f_send, f_recv, flat(k, t), "item", other(t))

    def forward_small(k, t):
        block = small_out.at[item, behind(k)]
        return remote(block, block, h_send, h_recv, flat(k, t), "item", other(t))

    each(1, peers, lambda t: forward_in(0, t).start())
    each(1, peers, lambda t: forward_small(0, t).start())

    def add_part(k, total):
        part(k).wait_recv()
        return total + m_parts[k - 1].astype(f32)

    m_out[item] = lax.fori_loop(1, shares, add_part, m_ref[...].astype(f32))
    each(1, peers, lambda t: forward_modulation(t).start())

    def add_select(t, total):
        share_select(t).wait_recv()
        return total + select_box[t - 1].astype(f32)

    select_out[item] = lax.fori_loop(
        1, peers, add_select, select_ref[item].astype(f32)
    ).astype(bf16)

    def forward_select(t):
        block = select_out.at[item]
        return remote(block, block, e_send, e_recv, t - 1, "item", other(t))

    each(1, peers, lambda t: forward_select(t).start())

    def pass_on(k):
        block = g_out.at[item, behind(k)]
        remote(block, block, z_send, z_recv, k, "seq", behind(k)).wait_recv()
        each(1, peers, lambda t: forward_in(k, t).start())
        little = small_out.at[item, behind(k)]
        remote(little, little, y_send, y_recv, k, "seq", behind(k)).wait_recv()
        each(1, peers, lambda t: forward_small(k, t).start())

    each(1, shares, pass_on)

    def widen_half(block, half, j, s):
        rows, mine = block.shape
        inner = in_final.shape[1] // 2
        place = pl.ds(pl.multiple_of(j * rows, rows), rows)
        first = pl.multiple_of(s * mine + half * inner, lanes)
        in_final[place, pl.ds(first, mine)] = block.astype(f32)

    def widen_in(j, s):
        if cuts is not None:
            widen_half(g_out[j, s], 0, j, s)

    if cuts is not None:
        each(
            0,
            peers,
            lambda j: each(0, shares, lambda s: widen_half(gate_ref[j, s], 1, j, s)),
        )
    each(0, shares, lambda k: widen_in(item, behind(k)))

    def finish(k):
        def one(t):
            block = g_out.at[origin(t), behind(k)]
            remote(block, block, f_send, f_recv, flat(k, t), "item", other(t)).wait_recv()
            little = small_out.at[origin(t), behind(k)]
            remote(little, little, h_send, h_recv, flat(k, t), "item", other(t)).wait_recv()
            widen_in(origin(t), behind(k))
            forward_in(k, t).wait_send()
            forward_small(k, t).wait_send()
            share_in(k, t).wait_send()

        each(1, peers, one)

    each(0, shares, finish)

    def finish_item(t):
        block = select_out.at[origin(t)]
        remote(block, block, e_send, e_recv, t - 1, "item", other(t)).wait_recv()
        forward_select(t).wait_send()
        block = m_out.at[origin(t)]
        remote(block, block, n_send, n_recv, t - 1, "item", other(t)).wait_recv()
        forward_modulation(t).wait_send()
        share_small(t).wait_send()
        share_select(t).wait_send()

    each(1, peers, finish_item)

    def finish_seq(k):
        spread_small(k).wait_send()
        place_in(k).wait_send()
        part(k).wait_send()

    each(1, shares, finish_seq)
    if cuts is None:
        return
    for j in range(peers):
        rows = select_ref.shape[1]
        select_final[j * rows : (j + 1) * rows] = select_out[j].astype(f32)
    inner = in_final.shape[1] // 2
    mine, share = small_ref.shape[2] // 2, small_ref.shape[1]
    for s in range(shares):
        whole = jnp.concatenate([small_out[j, s].astype(f32) for j in range(peers)], axis=0)
        for half in range(2):
            columns = slice(half * inner + s * mine, half * inner + (s + 1) * mine)
            first = 0
            for cut, final in zip(cuts, finals):
                final[:, columns] = whole[first : first + cut, half * mine : (half + 1) * mine]
                first += cut


def weight_sums(modulation, g, gate, small, select, cuts):
    shares, peers = g.shape[:2]
    vmem = pl.BlockSpec(memory_space=pltpu.VMEM)
    dma = pltpu.SemaphoreType.DMA
    some = peers - 1
    sizes = [shares * some] * 2 + [some] * 4 + [shares] * 4 + [shares * some] * 4 + [some] * 2
    sizes += [shares] * 2 + [some] * 2
    kept = [
        ((peers, shares) + g.shape[2:], bf16),
        ((peers, shares) + small.shape[1:], bf16),
        (select.shape, bf16),
    ]
    inner2 = 2 * shares * g.shape[3]
    direct = g.shape[3] % lanes == 0
    outs = kept
    if direct:
        outs = [((peers * g.shape[2], inner2), f32), ((peers * select.shape[1], select.shape[2]), f32)]
        outs += [((cut, inner2), f32) for cut in cuts]
    outs = [((peers,) + modulation.shape, f32)] + outs
    return pl.pallas_call(
        functools.partial(tail_kernel, cuts if direct else None),
        in_specs=[vmem] * 5,
        out_specs=[vmem] * len(outs),
        out_shape=[jax.ShapeDtypeStruct(shape, kind) for shape, kind in outs],
        scratch_shapes=[pltpu.VMEM(shape, kind) for shape, kind in kept if direct]
        + [
            pltpu.VMEM((shares - 1,) + modulation.shape, bf16),
            pltpu.VMEM((some, shares) + g.shape[2:], bf16),
            pltpu.VMEM((some,) + small.shape[1:], bf16),
            pltpu.VMEM((some,) + select.shape[1:], bf16),
            pltpu.VMEM((shares,) + g.shape[2:], bf16),
        ]
        + [dma((size,)) for size in sizes],
        compiler_params=pltpu.CompilerParams(
            collective_id=2, has_side_effects=True, vmem_limit_bytes=40 * 2**20
        ),
        cost_estimate=pl.CostEstimate(flops=60 * 10**9, bytes_accessed=2**20, transcendentals=0),
        name="weight_sums",
    )(modulation, g, gate, small, select)


def filter_windows(x, taps, reverse):
    rim = taps - 1
    length = x.shape[1]
    padded = jnp.pad(x, ((0, 0), (rim, rim), (0, 0)))
    starts = [2 * rim - j if reverse else j for j in range(taps)]
    return [padded[:, s : s + length] for s in starts]


def per_device(
    tokens,
    timestep,
    slot_item,
    slot_valid,
    cotangent,
    in_weight,
    out_weight,
    select_weight,
    modulation_weight,
    delta_weight,
    filter_weight,
    filter_bias,
    delta_bias,
    decay_log,
    skip_gain,
    modulation_bias,
):
    slots, local, model = tokens.shape
    shares = lax.axis_size("seq")
    place = lax.axis_index("seq")
    rank, inner = delta_weight.shape[0], delta_weight.shape[1] // 2
    states = decay_log.shape[0]
    select = select_weight.shape[1] // 2
    taps = filter_weight.shape[0]
    rim = taps - 1
    length = local * shares
    rows = slots * length
    mine = inner // shares
    padded_width = -(-mine // lanes) * lanes
    shard_rows = modulation_weight.shape[0]
    items = timestep.shape[0]

    def own_columns(v):
        split = v.reshape(v.shape[:-1] + (2, shares, mine))
        return lax.dynamic_index_in_dim(split, place, split.ndim - 2, False)

    first_slot = lax.axis_index("item") * slots
    valid = lax.dynamic_slice_in_dim(slot_valid, first_slot, slots).astype(f32)[:, None, None]
    chooser = (slot_item[:, None] == jnp.arange(items, dtype=jnp.int32)[None, :]).astype(bf16)
    embedded = jnp.dot(chooser, timestep, preferred_element_type=f32)
    condition = jax.nn.silu(embedded).astype(bf16)
    own_features = lax.dynamic_slice_in_dim(condition, place * shard_rows, shard_rows, 1)
    own_condition = lax.dynamic_slice_in_dim(own_features, first_slot, slots, 0)
    modulation_part = jnp.dot(own_condition, modulation_weight, preferred_element_type=f32)
    peers = lax.axis_size("item")
    share_rows = in_weight.shape[0] // peers
    own_rows = lax.dynamic_slice_in_dim(
        in_weight, lax.axis_index("item") * share_rows, share_rows, 0
    )
    own_rows = jnp.moveaxis(own_rows.reshape(share_rows, 2, shares, mine), 2, 0)
    all_tokens, own_in, modulation = gather_inputs(
        tokens, own_rows.reshape(shares, share_rows, 2 * mine), modulation_part.astype(bf16)
    )
    own_in = own_in.reshape(model, 2 * mine)
    modulation = modulation + modulation_bias.astype(f32)[None, :]
    shift = modulation[:, None, :model]
    scale = modulation[:, None, model : 2 * model]
    gate = modulation[:, None, 2 * model :]

    source = all_tokens.astype(f32)
    centered = source - jnp.mean(source, axis=-1, keepdims=True)
    spread = lax.rsqrt(jnp.mean(centered * centered, axis=-1, keepdims=True) + epsilon)
    mixed_in = (centered * spread * (1.0 + scale) + shift).astype(bf16).reshape(rows, model)
    mixed_in = lax.optimization_barrier(mixed_in)
    projected = (
        jnp.dot(mixed_in, own_in, preferred_element_type=f32)
        .astype(bf16)
        .reshape(slots, length, 2 * mine)
    )
    x_half = projected[..., :mine]
    gate_half = projected[..., mine:].astype(f32)

    tap_weight = own_columns(filter_weight).astype(f32)
    tap_bias = own_columns(filter_bias).astype(f32)
    step_weight = own_columns(delta_weight)
    step_bias = own_columns(delta_bias)
    rate = -jnp.exp(own_columns(decay_log))
    skip = own_columns(skip_gain)

    wide_taps = widen(jnp.swapaxes(tap_weight, 0, 1), padded_width)
    wide_select = jnp.swapaxes(select_weight.reshape(mine, 2, select), 0, 1)
    wide_select = jnp.pad(wide_select, ((0, 0), (0, padded_width - mine), (0, 0)))
    selection, wide_active = filter_and_select(
        widen(x_half, padded_width),
        wide_taps,
        widen(tap_bias[:, None, :], padded_width),
        wide_select,
    )
    selection = selection.reshape(2, rows, select)
    activated = [wide_active[d, ..., :mine] for d in range(2)]
    own_cotangent = cotangent.astype(f32)
    own_grad_branch = (valid * gate * own_cotangent).astype(bf16)
    selection, own_grad_branch = lax.optimization_barrier((selection, own_grad_branch))
    grad_branch = lax.all_gather(own_grad_branch, "seq", axis=1, tiled=True).reshape(rows, model)
    delta_rank = selection[:, :, :rank]
    selection = selection.reshape(2, slots, length, select)
    copies = coefficient_copies(select, rank, states)
    wide_rate = widen(jnp.swapaxes(rate, 0, 1) * log2e, padded_width)
    wide_weight = widen(
        jnp.pad(jnp.swapaxes(step_weight, 0, 1), ((0, 0), (0, select - rank), (0, 0))),
        padded_width,
    )
    wide_bias = widen(step_bias[:, None, :], padded_width)
    wide_skip = widen(skip[:, None, :], padded_width)
    scanned, hidden, step, bc = scan_states(
        selection, wide_active, wide_weight, wide_bias, wide_rate, copies, wide_skip
    )
    scanned = scanned[..., :mine]
    scanned_sum = scanned[0].astype(f32) + scanned[1].astype(f32)
    silu_gate = jax.nn.silu(gate_half)
    mixed_out = (scanned_sum * silu_gate).astype(bf16).reshape(rows, mine)
    branch_part = (
        jnp.dot(mixed_out, out_weight, preferred_element_type=f32)
        .astype(bf16)
        .reshape(slots, length, model)
    )
    branch_part, grad_branch = lax.optimization_barrier((branch_part, grad_branch))
    grad_mixed = dot_cols(grad_branch, out_weight).reshape(slots, length, mine)
    grad_scanned = grad_mixed * silu_gate
    grad_gate_half = grad_mixed * scanned_sum * silu_slope(gate_half)
    grad_out = dot_rows(mixed_out, grad_branch).astype(bf16)
    grad_gate_half = grad_gate_half.astype(bf16)
    grad_in_gate = dot_rows(mixed_in, grad_gate_half.reshape(rows, mine)).astype(bf16)
    branch_part, grad_out, grad_in_gate, scan_grad = lax.optimization_barrier(
        (branch_part, grad_out, grad_in_gate, grad_scanned)
    )
    branch_part = lax.psum_scatter(branch_part, "seq", scatter_dimension=1, tiled=True)
    grad_low, grad_input, grad_parts, grad_rate, grad_sums, grad_out, gate_in = scan_adjoint(
        bc,
        wide_active,
        wide_weight,
        wide_rate,
        copies,
        wide_skip,
        step,
        widen(scan_grad, padded_width),
        hidden,
        grad_out.reshape(peers, mine // peers, model),
        grad_in_gate.reshape(shares, peers, share_rows, mine),
    )
    grad_out, grad_low = lax.optimization_barrier(
        (grad_out.reshape(mine, model).astype(f32), grad_low)
    )
    grad_decay = jnp.sum(grad_rate, axis=1)[..., :mine] * ln2
    grad_step_bias = jnp.sum(grad_sums[:, :8, :mine], axis=1)
    grad_skip = jnp.sum(grad_sums[:, 8:, :mine], axis=1)
    grad_parts, branch_part = lax.optimization_barrier((grad_parts, branch_part))
    grad_selection = summed_everywhere(
        grad_parts.reshape(2 * slots, length, select), 5
    ).reshape(2, rows, select)
    grad_delta = jnp.einsum(
        "drk,dre->kde",
        delta_rank,
        grad_low[..., :mine].reshape(2, rows, mine),
        preferred_element_type=f32,
    )
    grad_x = jnp.zeros((slots, length, mine), f32)
    filtered = []
    for d in range(2):
        f = tap_bias[d]
        for j, window in enumerate(filter_windows(x_half, taps, d == 1)):
            f = f + tap_weight[j, d] * window.astype(f32)
        filtered.append(f)
    grad_select, grad_taps, grad_tap_bias = [], [], []
    for d in range(2):
        block = select_weight[:, d * select : (d + 1) * select]
        grad_select.append(
            dot_rows(grad_selection[d], activated[d].reshape(rows, mine)).T
        )
        grad_active = (
            grad_input[d, ..., :mine]
            + dot_cols(grad_selection[d], block).reshape(slots, length, mine)
        )
        grad_filtered = grad_active * silu_slope(filtered[d])
        grad_tap_bias.append(jnp.sum(grad_filtered, axis=(0, 1)))
        windows = filter_windows(x_half, taps, d == 1)
        grad_taps.append(
            jnp.stack([jnp.sum(grad_filtered * w.astype(f32), axis=(0, 1)) for w in windows])
        )
        for j, window in enumerate(filter_windows(grad_filtered, taps, d == 0)):
            grad_x = grad_x + tap_weight[j, d] * window
    grad_x = grad_x.astype(bf16)
    grad_projected = (
        jnp.concatenate([grad_x, grad_gate_half], axis=2).reshape(rows, 2 * mine)
    )
    mixed_part = dot_cols(grad_projected, own_in).astype(bf16).reshape(slots, length, model)
    grad_mixed_in = lax.psum_scatter(mixed_part, "seq", scatter_dimension=1, tiled=True)
    wide_part = mixed_part.astype(f32)
    grad_modulation_part = jnp.concatenate(
        [
            jnp.sum(wide_part, axis=1),
            jnp.sum(wide_part * (centered * spread), axis=1),
            jnp.sum(valid * own_cotangent * branch_part.astype(f32), axis=1),
        ],
        axis=1,
    )
    grad_in = dot_rows(mixed_in, grad_x.reshape(rows, mine)).astype(bf16)
    branch = branch_part.astype(f32)
    output = (tokens.astype(f32) + valid * gate * branch).astype(bf16)
    small = jnp.concatenate(
        [
            grad_delta,
            jnp.swapaxes(grad_decay, 0, 1),
            jnp.stack(grad_taps, 1),
            jnp.stack(grad_tap_bias)[None],
            grad_step_bias[None],
            grad_skip[None],
        ],
        axis=0,
    )
    small_rows = small.shape[0]
    share = -(-small_rows // (16 * peers)) * 16
    small = jnp.pad(
        small.astype(bf16).reshape(small_rows, 2 * mine), ((0, peers * share - small_rows), (0, 0))
    )
    grad_select = jnp.concatenate(grad_select, axis=1).astype(bf16)
    cuts = [rank, states, taps, 1, 1, 1]
    grad_modulation, *results = weight_sums(
        grad_modulation_part.astype(bf16),
        grad_in.reshape(shares, peers, share_rows, mine),
        gate_in,
        small.reshape(peers, share, 2 * mine),
        grad_select.reshape(peers, mine // peers, 2 * select),
        cuts,
    )
    grad_modulation, grad_mixed_in = lax.optimization_barrier((grad_modulation, grad_mixed_in))
    grad_mixed_in = grad_mixed_in.astype(f32)
    grad_modulation = grad_modulation.reshape(-1, 3 * model)
    own_source = tokens.astype(f32)
    own_centered = own_source - jnp.mean(own_source, axis=-1, keepdims=True)
    own_spread = lax.rsqrt(
        jnp.mean(own_centered * own_centered, axis=-1, keepdims=True) + epsilon
    )
    normed = own_centered * own_spread
    grad_normed = grad_mixed_in * (1.0 + scale)
    grad_source = own_spread * (
        grad_normed
        - jnp.mean(grad_normed, axis=-1, keepdims=True)
        - normed * jnp.mean(grad_normed * normed, axis=-1, keepdims=True)
    )
    grad_tokens = (own_cotangent + grad_source).astype(bf16)
    grad_modulation_weight = lax.dot_general(
        own_features.astype(f32),
        grad_modulation,
        (((0,), (0,)), ((), ())),
        precision=lax.Precision.HIGHEST,
        preferred_element_type=f32,
    )
    if mine % lanes == 0:
        grad_in, grad_select, *small = results
    else:
        grad_in, small, grad_select = results
        grad_in = jnp.stack([grad_in, gate_in]).reshape(2, peers, shares, share_rows, mine)
        grad_in = jnp.transpose(grad_in, (1, 3, 0, 2, 4)).reshape(peers * share_rows, 2 * inner)
        grad_in = grad_in.astype(f32)
        small = small.reshape(peers, shares, share, 2, mine)
        small = jnp.transpose(small, (0, 2, 3, 1, 4)).reshape(peers * share, 2 * inner).astype(f32)
        ends = [sum(cuts[: i + 1]) for i in range(len(cuts))]
        small = [small[end - cut : end] for cut, end in zip(cuts, ends)]
        grad_select = grad_select.reshape(mine, 2 * select).astype(f32)
    return (
        output,
        grad_tokens,
        grad_in,
        grad_out,
        grad_select,
        grad_modulation_weight,
        small[0],
        small[2],
        small[3].reshape(-1),
        small[4].reshape(-1),
        small[1],
        small[5].reshape(-1),
        jnp.sum(grad_modulation, axis=0),
    )


def solution(mesh):
    tokens, rows, same = P("item", "seq", None), P("seq", None), P()
    return jax.shard_map(
        per_device,
        mesh=mesh,
        in_specs=(tokens, same, same, same, tokens, rows, rows, rows, rows) + (same,) * 7,
        out_specs=(tokens, tokens, rows, rows, rows, rows) + (same,) * 7,
        check_vma=False,
    )
```
